32 devices in a mesh: seq: 16 (over z, y, x), head: 2 (over core).
Axes of the slice: x: 2, y: 2, z: 4, core: 2. Of those that a mesh axis runs over, the one named last changes fastest.
Arguments:
- latents: float32 [3072, 128], P('seq'), may hold values from -6 to 6
- in_proj: bfloat16 [2, 128, 1536], replicated, may hold values from -0.5 to 0.5
- query_proj: bfloat16 [2, 1536, 256], P(None, None, 'head'), may hold values from -0.15625 to 0.15625
- key_proj: bfloat16 [2, 1536, 256], P(None, None, 'head'), may hold values from -0.15625 to 0.15625
- value_proj: bfloat16 [2, 1536, 256], P(None, None, 'head'), may hold values from -0.15625 to 0.15625
- mix_proj: bfloat16 [2, 256, 1536], P(None, 'head'), may hold values from -0.375 to 0.375
- param_proj: bfloat16 [2, 1536, 256], P(None, 'head'), may hold values from -0.15625 to 0.15625
- attn_gain: float32 [2, 1536], replicated, may hold values from 0.1 to 1.9
- param_gain: float32 [2, 1536], replicated, may hold values from 0.1 to 1.9
Outputs:
- final_latent: float32 [3072, 128], P('seq')
- token_loglik: float32 [3072], P('seq')
The draws below stay inside these ranges and needn't reach their ends.
All inputs are finite; a program needn't handle non-finite values.
Results may differ from the reference program's by a relative error of at most 0.007.
Values may be sent and summed in bfloat16 or wider, within the bound.
No kernel may reach another device: no remote copies, remote signals or barrier semaphores. Data moves between devices by JAX's collectives and lax.ppermute only.
A program may use at most 128 MiB of HBM per device.

```python
import math
import jax
import jax.numpy as jnp
from jax import lax

D = 1536
HS = 64
C = 128
HEADS = 4
TOKENS = 3072


def shard_levels(rng, extent, shards, least, top_value):
    level, own = 1.0, jax.random.fold_in(rng, 6)
    for position, blocks in shards:
        heights = jnp.exp(jax.random.uniform(jax.random.fold_in(own, position), (blocks,), jnp.float32, least / len(shards), top_value / len(shards)))
        level = level * jnp.repeat(heights, extent[position] // blocks).reshape([-1 if axis == position else 1 for axis in range(len(extent))])
    return level


def gaussian(stream_key, extent, spread, limit, split=(), kind=jnp.bfloat16):
    array = jax.random.normal(stream_key, extent, jnp.float32) * spread
    if len(split) > 0:
        array = shard_levels(stream_key, extent, split, -0.22, 0.18) * array
    return jnp.clip(array, min=-limit, max=limit).astype(kind)


def setup_inputs(seed: int = 0) -> dict:
    key_of = jax.random.split(jax.random.key(seed), 10)
    latents = gaussian(key_of[0], (TOKENS, C), 1.0, 6.0, ((0, 16),), jnp.float32)
    in_proj = gaussian(key_of[1], (2, C, D), C ** -0.5, 0.5)
    query_proj = gaussian(key_of[2], (2, D, HEADS * HS), D ** -0.5, 0.15625, ((2, 2),))
    key_proj = gaussian(key_of[3], (2, D, HEADS * HS), D ** -0.5, 0.15625, ((2, 2),))
    value_proj = gaussian(key_of[4], (2, D, HEADS * HS), D ** -0.5, 0.15625, ((2, 2),))
    mix_proj = gaussian(key_of[5], (2, HEADS * HS, D), (HEADS * HS) ** -0.5, 0.375, ((1, 2),))
    param_proj = gaussian(key_of[6], (2, D, 2 * C), D ** -0.5, 0.15625, ((1, 2),))
    attn_gain = jnp.clip(1.0 + 0.18 * jax.random.normal(key_of[7], (2, D), jnp.float32), 0.1, 1.9)
    param_gain = jnp.clip(1.0 + 0.18 * jax.random.normal(key_of[8], (2, D), jnp.float32), 0.1, 1.9)
    return {"latents": latents, "in_proj": in_proj, "query_proj": query_proj, "key_proj": key_proj, "value_proj": value_proj, "mix_proj": mix_proj, "param_proj": param_proj, "attn_gain": attn_gain, "param_gain": param_gain}


score_scale = 8.0
epsilon = 1e-06

def norm_rows(value, gain):
    return value * lax.rsqrt(lax.optimization_barrier(jnp.mean(value * value, axis=-1, keepdims=True)) + epsilon) * gain

def norm_heads(value):
    return (value * lax.rsqrt(lax.optimization_barrier(jnp.mean(value * value, axis=-1, keepdims=True)) + epsilon)).astype(jnp.bfloat16)

def attend_all(queries, key_rows, value_rows):
    length_all, head_count, head_size = queries.shape
    block_rows = min(512, length_all)
    key_pos = jnp.arange(length_all, dtype=jnp.int32)
    keys_wide = key_rows.astype(jnp.float32)
    values_wide = value_rows.astype(jnp.float32)

    def one_block(block_index):
        start_row = (block_index * block_rows).astype(jnp.int32)
        query_block = lax.dynamic_slice_in_dim(queries, start_row, block_rows, 0).astype(jnp.float32)
        scores = jnp.einsum('qhd,khd->hqk', query_block, keys_wide) * (score_scale / head_size)
        query_pos = start_row + jnp.arange(block_rows, dtype=jnp.int32)
        allowed = key_pos[None, None, :] <= query_pos[None, :, None]
        weights = jnp.where(allowed, jnp.exp(scores), jnp.zeros_like(scores))
        denominator = lax.optimization_barrier(jnp.sum(weights, axis=-1))
        rounded = lax.optimization_barrier(weights.astype(jnp.bfloat16)).astype(jnp.float32)
        numerator = jnp.einsum('hqk,khd->qhd', rounded, values_wide)
        return (numerator / jnp.transpose(denominator)[:, :, None]).astype(jnp.bfloat16)
    blocks = lax.map(one_block, jnp.arange(length_all // block_rows, dtype=jnp.int32))
    return blocks.reshape(length_all, head_count * head_size)

def flow_block(rows_in, layer_index, in_proj, query_proj, key_proj, value_proj, mix_proj, param_proj, attn_gain, param_gain):
    length_all = rows_in.shape[0]
    start_token = jnp.zeros((1, rows_in.shape[1]), rows_in.dtype)
    shifted = jnp.concatenate([start_token, rows_in[:-1]], axis=0).astype(jnp.bfloat16)
    hidden = jnp.dot(shifted, in_proj[layer_index], preferred_element_type=jnp.float32)
    normed = norm_rows(hidden, attn_gain[layer_index]).astype(jnp.bfloat16)
    queries = norm_heads(jnp.dot(normed, query_proj[layer_index], preferred_element_type=jnp.float32).reshape(length_all, -1, HS))
    key_rows = norm_heads(jnp.dot(normed, key_proj[layer_index], preferred_element_type=jnp.float32).reshape(length_all, -1, HS))
    value_rows = jnp.dot(normed, value_proj[layer_index], preferred_element_type=jnp.float32).astype(jnp.bfloat16).reshape(length_all, -1, HS)
    attended = attend_all(queries, key_rows, value_rows)
    mixture = hidden + jnp.dot(attended, mix_proj[layer_index], preferred_element_type=jnp.float32)
    scaled = norm_rows(mixture, param_gain[layer_index]).astype(jnp.bfloat16)
    predicted = jnp.dot(scaled, param_proj[layer_index], preferred_element_type=jnp.float32)
    shift_mu = predicted[:, :C]
    log_scale = 2.0 * jnp.tanh(0.5 * predicted[:, C:])
    block_out = (rows_in - shift_mu) * jnp.exp(-log_scale)
    return (block_out, -lax.optimization_barrier(jnp.sum(log_scale, axis=-1)))

def reference(latents, in_proj, query_proj, key_proj, value_proj, mix_proj, param_proj, attn_gain, param_gain):
    weights_all = (in_proj, query_proj, key_proj, value_proj, mix_proj, param_proj, attn_gain, param_gain)
    first_out, first_logdet = flow_block(latents, 0, *weights_all)
    second_out, second_logdet = flow_block(jnp.flip(first_out, 0), 1, *weights_all)
    final_latent = jnp.flip(second_out, 0)
    total_logdet = first_logdet + jnp.flip(second_logdet, 0)
    token_loglik = (total_logdet - 0.5 * lax.optimization_barrier(jnp.sum(final_latent * final_latent, axis=-1))) / C - 0.5 * math.log(2.0 * math.pi)
    return (final_latent, token_loglik)
```

```python
import functools
import math

import jax
import jax.numpy as jnp
import numpy as np
from jax import lax
from jax.experimental import pallas as pl
from jax.experimental.pallas import tpu as pltpu
from jax.sharding import PartitionSpec as P

HS = 64
GROUP = 256

score_scale = 8.0
epsilon = 1e-06

VMEM_LIMIT = 56 * 1024 * 1024


def dot(a, b):
    return jnp.dot(a, b, preferred_element_type=jnp.float32)


def dot_nt(a, b):
    return lax.dot_general(a, b, (((1,), (1,)), ((), ())), preferred_element_type=jnp.float32)


def cat(parts, axis):
    return parts[0] if len(parts) == 1 else jnp.concatenate(parts, axis=axis)


def combine_kernel(pieces, in_ref, gain_ref, *refs):
    key_refs, value_refs, out_ref = refs[:pieces], refs[pieces : 2 * pieces], refs[2 * pieces]
    block = pl.program_id(0)
    base = in_ref[0]
    channels = base.shape[0]
    scaled = base.astype(jnp.float32) * gain_ref[pl.ds(block, 1), :]
    high = scaled.astype(jnp.bfloat16)
    low = (scaled - high.astype(jnp.float32)).astype(jnp.bfloat16)
    both = jnp.concatenate([high, low], axis=0)
    row = 0
    for group in (key_refs, value_refs):
        for first in range(0, pieces, 2):
            columns = cat([ref[0] for ref in group[first : first + 2]], 1)
            product = dot(both, columns)
            product = product[:channels] + product[channels:]
            width = product.shape[1]
            out_ref[0, row : row + width, :] = product.T.astype(jnp.bfloat16)
            row += width
    gram = dot_nt(base, base)
    gram_high = gram.astype(jnp.bfloat16)
    out_ref[0, row : row + channels, :] = gram_high
    row += channels
    out_ref[0, row : row + channels, :] = (gram - gram_high.astype(jnp.float32)).astype(
        jnp.bfloat16
    )
    row += channels
    eye = lax.broadcasted_iota(jnp.int32, (channels, channels), 0) == lax.broadcasted_iota(
        jnp.int32, (channels, channels), 1
    )
    out_ref[0, row : row + channels, :] = jnp.where(eye, 1.0, 0.0).astype(jnp.bfloat16)


def combine(in_proj, attn_gain, key_pieces, value_pieces):
    pieces = len(key_pieces)
    layers, channels, features = in_proj.shape
    head_cols = key_pieces[0].shape[2]
    rows = 2 * pieces * head_cols + 3 * channels
    piece = pl.BlockSpec((1, features, head_cols), lambda b: (b, 0, 0))
    return pl.pallas_call(
        functools.partial(combine_kernel, pieces),
        grid=(layers,),
        in_specs=[
            pl.BlockSpec((1, channels, features), lambda b: (b, 0, 0)),
            pl.BlockSpec((layers, features), lambda b: (0, 0)),
        ]
        + [piece] * (2 * pieces),
        out_specs=pl.BlockSpec((1, rows, channels), lambda b: (b, 0, 0)),
        out_shape=jax.ShapeDtypeStruct((layers, rows, channels), jnp.bfloat16),
        compiler_params=pltpu.CompilerParams(vmem_limit_bytes=VMEM_LIMIT),
        name="combine",
    )(in_proj, attn_gain, *key_pieces, *value_pieces)


def block_kernel(cfg, place_ref, pos_ref, rows_ref, own_ref, other_ref, maps_ref, in_ref, again_ref, pgain_ref, *refs):
    layer, pieces, last = cfg["layer"], cfg["pieces"], cfg["last"]
    refs = list(refs)
    query_refs = [refs.pop(0) for _ in range(pieces)]
    mix_refs = [refs.pop(0) for _ in range(pieces)]
    param_refs = [refs.pop(0) for _ in range(pieces)]
    if last:
        first_log_ref, out_ref, param_ref = refs
    else:
        out_ref, log_ref, spread_ref, param_ref = refs
    side, member = place_ref[0], place_ref[1]
    first_token, border_row, border_on = place_ref[2], place_ref[3], place_ref[4]
    channels = own_ref.shape[1]
    features = in_ref.shape[2]
    count = cfg["count"]
    forward = layer == 0

    if last:
        values = rows_ref[...]
    else:
        values = rows_ref[pl.ds(pl.multiple_of(side * count, 8), count), :]
    window = other_ref[pl.ds(pl.multiple_of(border_row, 16), 16), :].astype(jnp.float32)
    border = window[15:16] if forward else window[0:1]
    border = jnp.where(border_on > 0, border, jnp.zeros_like(border))
    token = lax.broadcasted_iota(jnp.int32, (count, 1), 0)
    edge = 0 if forward else count - 1
    moved = pltpu.roll(values, 1 if forward else count - 1, 0)
    shifted = jnp.where(token == edge, border, moved).astype(jnp.bfloat16)

    hidden = dot(shifted, in_ref[0])
    spread = lax.rsqrt(jnp.mean(hidden * hidden, axis=1, keepdims=True) + epsilon)
    normed = (hidden * spread * again_ref[layer : layer + 1, :]).astype(jnp.bfloat16)

    head_cols = query_refs[0].shape[2]
    groups = []
    for first in range(0, pieces, 2):
        query = dot(normed, cat([ref[0] for ref in query_refs[first : first + 2]], 1))
        width = query.shape[1]
        head = lax.broadcasted_iota(jnp.int32, (count, width), 1) // HS
        bands = []
        for h in range(width // HS):
            band = jnp.where(head == h, query, 0.0)
            mean = jnp.sum(band * band, axis=1, keepdims=True) * (1.0 / HS)
            bands.append((band * lax.rsqrt(mean + epsilon)).astype(jnp.bfloat16))
        groups.append((cat(bands, 0), width))
    total_cols = pieces * head_cols
    group_cols = groups[0][1]
    heads = group_cols // HS
    query_token = first_token + jnp.concatenate([token] * heads, axis=0)

    def one_chunk(source_ref, start, offset, carry):
        source = source_ref[pl.ds(start, cfg["chunk"]), :]
        key_token = pos_ref[:, pl.ds(start, cfg["chunk"])] + offset
        allowed = key_token < query_token if forward else key_token > query_token
        tail = dot_nt(maps_ref[0, 2 * total_cols :, :], source)
        gram = tail[:channels] + tail[channels : 2 * channels]
        square = jnp.sum(gram * tail[2 * channels :], axis=0, keepdims=True)
        scale = lax.rsqrt(jnp.maximum(square, 0.0) * (1.0 / features) + epsilon)
        scale_sq = scale * scale
        result = []
        for g, (queries, width) in enumerate(groups):
            low = g * group_cols
            key = dot_nt(maps_ref[0, low : low + width, :], source)
            value = dot_nt(maps_ref[0, total_cols + low : total_cols + low + width, :], source)
            scaled_keys = []
            for h in range(width // HS):
                one = key[h * HS : (h + 1) * HS]
                mean = jnp.sum(one * one, axis=0, keepdims=True) * (1.0 / HS)
                factor = scale * lax.rsqrt(mean * scale_sq + epsilon)
                scaled_keys.append((one * factor).astype(jnp.bfloat16))
            keys = jnp.concatenate(scaled_keys, axis=0)
            value = (value * scale).astype(jnp.bfloat16)
            scores = dot(queries, keys) * (score_scale / HS)
            weights = jnp.where(allowed, jnp.exp(scores), 0.0)
            numerator, denominator = carry[g]
            denominator = denominator + jnp.sum(weights, axis=1, keepdims=True)
            numerator = numerator + dot_nt(weights.astype(jnp.bfloat16), value)
            result.append((numerator, denominator))
        return tuple(result)

    carry = tuple(
        (
            jnp.zeros((heads * count, width), jnp.float32),
            jnp.ones((heads * count, 1), jnp.float32),
        )
        for _, width in groups
    )
    chunks = own_ref.shape[0] // cfg["chunk"]
    for source_ref, offset in ((own_ref, side * count), (other_ref, (1 - side) * count)):
        if chunks <= 4:
            for c in range(chunks):
                carry = one_chunk(source_ref, c * cfg["chunk"], offset, carry)
        else:
            carry = lax.fori_loop(
                0,
                chunks,
                lambda c, now: one_chunk(
                    source_ref, pl.multiple_of(c * cfg["chunk"], cfg["chunk"]), offset, now
                ),
                carry,
            )

    mixture = hidden
    for g, (numerator, denominator) in enumerate(carry):
        head = lax.broadcasted_iota(jnp.int32, (count, group_cols), 1) // HS
        attended = jnp.zeros((count, group_cols), jnp.float32)
        for h in range(heads):
            band = slice(h * count, (h + 1) * count)
            attended = jnp.where(head == h, numerator[band] / denominator[band], attended)
        mixture = mixture + dot(
            attended.astype(jnp.bfloat16), cat([ref[0] for ref in mix_refs[2 * g : 2 * g + 2]], 0)
        )
    spread = lax.rsqrt(jnp.mean(mixture * mixture, axis=1, keepdims=True) + epsilon)
    scaled = (mixture * spread * pgain_ref[layer : layer + 1, :]).astype(jnp.bfloat16)
    share = features // pieces
    for j, ref in enumerate(param_refs):
        param_ref[pl.ds(pl.multiple_of(place_ref[5 + j] * share, 16), share), :] = ref[0]
    predicted = dot(scaled, param_ref[...])
    log_scale = 2.0 * jnp.tanh(0.5 * predicted[:, channels:])
    result = (values - predicted[:, :channels]) * jnp.exp(-log_scale)
    if last:
        term = -(first_log_ref[...] + log_scale) - 0.5 * (result * result)
        loglik = jnp.sum(term.T, axis=0, keepdims=True) * (1.0 / channels) - 0.5 * math.log(
            2.0 * math.pi
        )
        out_ref[:count, :] = result
        out_ref[count:, :count] = jnp.broadcast_to(loglik, (8, count))
    else:
        out_ref[...] = result
        log_ref[...] = log_scale
        narrow = result.astype(jnp.bfloat16)
        for i in range(spread_ref.shape[0]):
            spread_ref[i] = narrow


def run_block(layer, members, count, place, positions, rows, own, other, maps, in_proj, attn_gain, param_gain, query_pieces, mix_pieces, param_pieces, first_log=None):
    pieces = len(query_pieces)
    layers, channels, features = in_proj.shape
    last = first_log is not None
    chunk = next(size for size in (512, 384, 256, 192, 128, own.shape[0]) if own.shape[0] % size == 0)

    def full(array):
        return pl.BlockSpec(array.shape, lambda i: (0,) * array.ndim)

    def one_layer(array):
        return pl.BlockSpec((1,) + array.shape[1:], lambda i: (layer, 0, 0))

    stacked = list(query_pieces) + list(mix_pieces) + list(param_pieces)
    in_specs = (
        [pl.BlockSpec(memory_space=pltpu.SMEM)]
        + [full(array) for array in (positions, rows, own, other)]
        + [one_layer(maps), one_layer(in_proj), full(attn_gain), full(param_gain)]
        + [one_layer(array) for array in stacked]
    )
    operands = [place, positions, rows, own, other, maps, in_proj, attn_gain, param_gain] + stacked
    if last:
        in_specs.append(full(first_log))
        operands.append(first_log)
        out_shape = jax.ShapeDtypeStruct((count + 8, channels), jnp.float32)
        out_specs = pl.BlockSpec((count + 8, channels), lambda i: (0, 0))
    else:
        out_shape = (
            jax.ShapeDtypeStruct((count, channels), jnp.float32),
            jax.ShapeDtypeStruct((count, channels), jnp.float32),
            jax.ShapeDtypeStruct((members, count, channels), jnp.bfloat16),
        )
        out_specs = tuple(
            pl.BlockSpec(s.shape, lambda i, n=len(s.shape): (0,) * n) for s in out_shape
        )
    cfg = {"layer": layer, "pieces": pieces, "last": last, "count": count, "chunk": chunk}
    return pl.pallas_call(
        functools.partial(block_kernel, cfg),
        grid=(1,),
        in_specs=in_specs,
        out_specs=out_specs,
        out_shape=out_shape,
        scratch_shapes=[pltpu.VMEM((features, param_pieces[0].shape[2]), jnp.bfloat16)],
        compiler_params=pltpu.CompilerParams(vmem_limit_bytes=VMEM_LIMIT),
        name="flow_block",
    )(*operands)


def body(
    latents, in_proj, query_proj, key_proj, value_proj, mix_proj, param_proj, attn_gain, param_gain
):
    members, ways = lax.axis_size("seq"), lax.axis_size("head")
    rows, channels = latents.shape
    count = rows // 2
    member, way = lax.axis_index("seq"), lax.axis_index("head")
    side = way % 2

    def swap(array):
        return lax.ppermute(array, "head", [(i, i ^ 1) for i in range(ways)])

    def pieces_of(array):
        shares = [array]
        for j in range(1, ways):
            shares.append(
                lax.ppermute(array, "head", [((i + j) % ways, i) for i in range(ways)])
            )
        return shares

    key_pieces, value_pieces = pieces_of(key_proj), pieces_of(value_proj)
    query_pieces, mix_pieces = pieces_of(query_proj), pieces_of(mix_proj)
    param_pieces = pieces_of(param_proj)

    def gather(spread):
        return lax.all_to_all(spread, "seq", 0, 0).reshape(members * count, channels)

    positions = jnp.asarray(
        (np.arange(members * count) // count * rows + np.arange(members * count) % count)[None],
        jnp.int32,
    )
    first_token = member * rows + side * count
    owners = [(way + j) % ways for j in range(ways)]

    def place(layer):
        if layer == 0:
            group = member - 1 + side
            on = group >= 0
            border_row = jnp.maximum(group, 0) * count + count - 16
        else:
            group = member + side
            on = group < members
            border_row = jnp.minimum(group, members - 1) * count
        entries = [side, member, first_token, border_row, on] + owners
        return jnp.stack([jnp.asarray(e, jnp.int32) for e in entries])

    own_rows = lax.dynamic_slice_in_dim(latents, side * count, count, 0).astype(jnp.bfloat16)
    own = gather(jnp.broadcast_to(own_rows[None], (members, count, channels)))
    other = swap(own)
    maps = combine(in_proj, attn_gain, key_pieces, value_pieces)
    shared = (maps, in_proj, attn_gain, param_gain, query_pieces, mix_pieces, param_pieces)
    first_out, first_log, spread = run_block(
        0, members, count, place(0), positions, latents, own, other, *shared
    )
    own = gather(spread)
    other = swap(own)
    packed = run_block(
        1, members, count, place(1), positions, first_out, own, other, *shared, first_log=first_log
    )
    packed_other = swap(packed)
    low = jnp.where(side == 0, packed, packed_other)
    high = jnp.where(side == 0, packed_other, packed)
    final_latent = jnp.concatenate([low[:count], high[:count]], axis=0)
    token_loglik = jnp.concatenate([low[count, :count], high[count, :count]], axis=0)
    return (final_latent, token_loglik)


def solution(mesh):
    placed = (
        P("seq", None),
        P(),
        P(None, None, "head"),
        P(None, None, "head"),
        P(None, None, "head"),
        P(None, "head", None),
        P(None, "head", None),
        P(),
        P(),
    )
    return jax.shard_map(
        body, mesh=mesh, in_specs=placed, out_specs=(P("seq", None), P("seq")), check_vma=False
    )
```

```python
import functools
import math

import jax
import jax.numpy as jnp
import numpy as np
from jax import lax
from jax.experimental import pallas as pl
from jax.experimental.pallas import tpu as pltpu
from jax.sharding import PartitionSpec as P

HS = 64

score_scale = 8.0
epsilon = 1e-06

VMEM_LIMIT = 56 * 1024 * 1024


def dot(a, b):
    return jnp.dot(a, b, preferred_element_type=jnp.float32)


def dot_nt(a, b):
    return lax.dot_general(a, b, (((1,), (1,)), ((), ())), preferred_element_type=jnp.float32)


def cat(parts, axis):
    return parts[0] if len(parts) == 1 else jnp.concatenate(parts, axis=axis)


def side_of():
    return lax.rem(lax.axis_index("head"), 2)


def cost(flops, moved):
    return pl.CostEstimate(flops=int(flops), bytes_accessed=int(moved), transcendentals=0)


def size_of(arrays):
    return sum(math.prod(a.shape) * a.dtype.itemsize for a in arrays)


def vmem():
    return pl.BlockSpec(memory_space=pltpu.VMEM)


def spread_kernel(rows_ref, spread_ref, edge_ref):
    members, count, _ = spread_ref.shape
    own = rows_ref[pl.ds(pl.multiple_of(side_of() * count, 8), count), :].astype(jnp.bfloat16)
    for i in range(members):
        spread_ref[i] = own
    edge_ref[...] = rows_ref[rows_ref.shape[0] - 8 :, :]


def spread_rows(rows, members):
    count, channels = rows.shape[0] // 2, rows.shape[1]
    return pl.pallas_call(
        spread_kernel,
        in_specs=[vmem()],
        out_specs=(vmem(), vmem()),
        out_shape=(
            jax.ShapeDtypeStruct((members, count, channels), jnp.bfloat16),
            jax.ShapeDtypeStruct((8, channels), jnp.float32),
        ),
        name="spread_rows",
    )(rows)


def combine_kernel(pieces, in_ref, gain_ref, *refs):
    key_refs, value_refs, out_ref = refs[:pieces], refs[pieces : 2 * pieces], refs[2 * pieces]
    block = pl.program_id(0)
    base = in_ref[0]
    channels = base.shape[0]

    def store(row, value):
        high = value.astype(jnp.bfloat16)
        rows = value.shape[0]
        out_ref[0, row : row + rows, :channels] = high
        out_ref[0, row : row + rows, channels:] = (value - high.astype(jnp.float32)).astype(
            jnp.bfloat16
        )
        return row + rows

    scaled = base.astype(jnp.float32) * gain_ref[pl.ds(block, 1), :]
    high = scaled.astype(jnp.bfloat16)
    low = (scaled - high.astype(jnp.float32)).astype(jnp.bfloat16)
    both = jnp.concatenate([high, low], axis=0)
    row = 0
    for group in (key_refs, value_refs):
        for first in range(0, pieces, 2):
            columns = cat([ref[0] for ref in group[first : first + 2]], 1)
            product = dot(both, columns)
            row = store(row, (product[:channels] + product[channels:]).T)
    row = store(row, dot_nt(base, base))
    eye = lax.broadcasted_iota(jnp.int32, (channels, channels), 0) == lax.broadcasted_iota(
        jnp.int32, (channels, channels), 1
    )
    store(row, jnp.where(eye, 1.0, 0.0))


def combine(in_proj, attn_gain, key_pieces, value_pieces):
    pieces = len(key_pieces)
    layers, channels, features = in_proj.shape
    head_cols = key_pieces[0].shape[2]
    rows = 2 * pieces * head_cols + 2 * channels
    piece = pl.BlockSpec((1, features, head_cols), lambda b: (b, 0, 0))
    operands = [in_proj, attn_gain, *key_pieces, *value_pieces]
    return pl.pallas_call(
        functools.partial(combine_kernel, pieces),
        grid=(layers,),
        in_specs=[
            pl.BlockSpec((1, channels, features), lambda b: (b, 0, 0)),
            pl.BlockSpec((layers, features), lambda b: (0, 0)),
        ]
        + [piece] * (2 * pieces),
        out_specs=pl.BlockSpec((1, rows, 2 * channels), lambda b: (b, 0, 0)),
        out_shape=jax.ShapeDtypeStruct((layers, rows, 2 * channels), jnp.bfloat16),
        compiler_params=pltpu.CompilerParams(vmem_limit_bytes=VMEM_LIMIT),
        cost_estimate=cost(4 * layers * channels * features * rows, size_of(operands)),
        name="combine",
    )(*operands)


def queries_kernel(layer, pieces, rows_ref, edge_ref, in_ref, gain_ref, *refs):
    query_refs, shifted_ref, out_ref = refs[:pieces], refs[pieces], refs[pieces + 1]
    count = shifted_ref.shape[0]
    token = lax.broadcasted_iota(jnp.int32, (count, 1), 0)
    if layer == 0:
        start = pl.multiple_of(side_of() * count, 8)
        values = rows_ref[pl.ds(start, count), :]
        border = jnp.where(side_of() == 0, edge_ref[7:8, :], rows_ref[count - 1 : count, :])
        moved, at = pltpu.roll(values, 1, 0), 0
    else:
        values = rows_ref[...]
        border = edge_ref[0:1, :]
        moved, at = pltpu.roll(values, count - 1, 0), count - 1
    shifted = jnp.where(token == at, border, moved).astype(jnp.bfloat16)
    shifted_ref[...] = shifted
    hidden = dot(shifted, in_ref[0])
    spread = lax.rsqrt(jnp.mean(hidden * hidden, axis=1, keepdims=True) + epsilon)
    normed = (hidden * spread * gain_ref[layer : layer + 1, :]).astype(jnp.bfloat16)
    for first in range(0, pieces, 2):
        query = dot(normed, cat([ref[0] for ref in query_refs[first : first + 2]], 1))
        width = query.shape[1]
        head = lax.broadcasted_iota(jnp.int32, (count, width), 1) // HS
        for h in range(width // HS):
            band = jnp.where(head == h, query, 0.0)
            mean = jnp.sum(band * band, axis=1, keepdims=True) * (1.0 / HS)
            out_ref[first // 2, h * count : (h + 1) * count, :] = (
                band * lax.rsqrt(mean + epsilon)
            ).astype(jnp.bfloat16)


def make_queries(layer, count, rows, edge, in_proj, attn_gain, query_pieces):
    pieces = len(query_pieces)
    channels, features = in_proj.shape[1:]
    width = min(2, pieces) * query_pieces[0].shape[2]
    groups = pieces * query_pieces[0].shape[2] // width

    def one_layer(array):
        return pl.BlockSpec((1,) + array.shape[1:], lambda i: (layer, 0, 0))

    def full(shape):
        return pl.BlockSpec(shape, lambda i: (0,) * len(shape))

    shapes = ((count, channels), (groups, width // HS * count, width))
    operands = [rows, edge, in_proj, attn_gain, *query_pieces]
    return pl.pallas_call(
        functools.partial(queries_kernel, layer, pieces),
        grid=(1,),
        in_specs=[full(rows.shape), full(edge.shape), one_layer(in_proj), full(attn_gain.shape)]
        + [one_layer(array) for array in query_pieces],
        out_specs=tuple(full(shape) for shape in shapes),
        out_shape=tuple(jax.ShapeDtypeStruct(shape, jnp.bfloat16) for shape in shapes),
        compiler_params=pltpu.CompilerParams(vmem_limit_bytes=VMEM_LIMIT),
        cost_estimate=cost(2 * count * features * (channels + groups * width), size_of(operands) // 2),
        name="queries",
    )(*operands)


def attend_kernel(cfg, pos_ref, pgain_ref, rows_ref, *refs):
    layer, pieces, last, count = cfg["layer"], cfg["pieces"], cfg["last"], cfg["count"]
    refs = list(refs)
    first_log_ref = refs.pop(0) if last else None
    maps_src, own_src, query_src, other_src, shifted_src, in_src = [refs.pop(0) for _ in range(6)]
    mix_src = [refs.pop(0) for _ in range(pieces)]
    param_src = [refs.pop(0) for _ in range(pieces)]
    outs = [refs.pop(0) for _ in range(1 if last else 4)]
    maps_ref, own_ref, query_ref, other_ref, shifted_ref, in_ref, mix_ref, param_ref, sems = refs
    side, way = side_of(), lax.axis_index("head")
    channels, features = in_ref.shape
    forward = layer == 0

    copies = []

    def fetch(source, target):
        copy = pltpu.make_async_copy(source, target, sems.at[len(copies)])
        copy.start()
        copies.append(copy)
        return copy

    maps_copy = fetch(maps_src.at[layer], maps_ref)
    own_copy = fetch(own_src, own_ref)
    query_copy = fetch(query_src, query_ref)
    other_copy = fetch(other_src, other_ref)
    late = [fetch(shifted_src, shifted_ref), fetch(in_src.at[layer], in_ref)]
    head_cols = mix_src[0].shape[1]
    for j in range(pieces):
        late.append(fetch(mix_src[j].at[layer], mix_ref.at[pl.ds(j * head_cols, head_cols)]))
    share = features // pieces
    for j in range(pieces):
        at = pl.multiple_of(lax.rem(way + j, pieces) * share, 16)
        late.append(fetch(param_src[j].at[layer], param_ref.at[pl.ds(at, share)]))
    groups, _, group_cols = query_ref.shape
    heads = group_cols // HS
    total_cols = groups * group_cols
    token = lax.broadcasted_iota(jnp.int32, (count, 1), 0)
    first_token = lax.axis_index("seq") * (2 * count) + side * count
    query_token = first_token + jnp.concatenate([token] * heads, axis=0)

    def one_chunk(source_ref, start, offset, carry):
        size = cfg["chunk"]
        source = source_ref[pl.ds(start, size), :]
        twice = jnp.concatenate([source, source], axis=1)
        key_token = pos_ref[:, pl.ds(start, size)] + offset
        allowed = key_token < query_token if forward else key_token > query_token
        tail = dot_nt(maps_ref[2 * total_cols :, :], twice)
        square = jnp.sum(tail[:channels] * tail[channels:], axis=0, keepdims=True)
        scale = lax.rsqrt(jnp.maximum(square, 0.0) * (1.0 / features) + epsilon)
        scale_sq = scale * scale
        result = []
        for g in range(groups):
            low = g * group_cols
            key = dot_nt(maps_ref[low : low + group_cols, :], twice)
            value = dot_nt(maps_ref[total_cols + low : total_cols + low + group_cols, :], twice)
            keys = []
            for h in range(heads):
                one = key[h * HS : (h + 1) * HS]
                mean = jnp.sum(one * one, axis=0, keepdims=True) * (1.0 / HS)
                factor = scale * lax.rsqrt(mean * scale_sq + epsilon)
                keys.append((one * factor).astype(jnp.bfloat16))
            value = (value * scale).astype(jnp.bfloat16)
            scores = dot(query_ref[g], jnp.concatenate(keys, axis=0)) * (score_scale / HS)
            weights = jnp.where(allowed, jnp.exp(scores), 0.0)
            numerator, denominator = carry[g]
            for lane in range(0, size, 128):
                denominator = denominator + weights[:, lane : lane + 128]
            numerator = numerator + dot_nt(weights.astype(jnp.bfloat16), value)
            result.append((numerator, denominator))
        return tuple(result)

    carry = tuple(
        (
            jnp.zeros((heads * count, group_cols), jnp.float32),
            jnp.zeros((heads * count, 128), jnp.float32),
        )
        for _ in range(groups)
    )
    chunks = own_ref.shape[0] // cfg["chunk"]
    maps_copy.wait()
    own_copy.wait()
    query_copy.wait()
    for source_ref, offset in ((own_ref, side * count), (other_ref, (1 - side) * count)):
        if source_ref is other_ref:
            other_copy.wait()
        if chunks <= 4:
            for c in range(chunks):
                carry = one_chunk(source_ref, c * cfg["chunk"], offset, carry)
        else:
            carry = lax.fori_loop(
                0,
                chunks,
                lambda c, now, source_ref=source_ref, offset=offset: one_chunk(
                    source_ref, pl.multiple_of(c * cfg["chunk"], cfg["chunk"]), offset, now
                ),
                carry,
            )

    for copy in late:
        copy.wait()
    mixture = dot(shifted_ref[...], in_ref[...])
    head = lax.broadcasted_iota(jnp.int32, (count, group_cols), 1) // HS
    for g, (numerator, denominator) in enumerate(carry):
        share_of = 1.0 / (jnp.sum(denominator, axis=1, keepdims=True) + 1.0)
        attended = jnp.zeros((count, group_cols), jnp.float32)
        for h in range(heads):
            band = slice(h * count, (h + 1) * count)
            attended = jnp.where(head == h, numerator[band] * share_of[band], attended)
        rows = mix_ref[g * group_cols : (g + 1) * group_cols, :]
        mixture = mixture + dot(attended.astype(jnp.bfloat16), rows)
    spread = lax.rsqrt(jnp.mean(mixture * mixture, axis=1, keepdims=True) + epsilon)
    scaled = (mixture * spread * pgain_ref[layer : layer + 1, :]).astype(jnp.bfloat16)
    predicted = dot(scaled, param_ref[...])
    log_scale = 2.0 * jnp.tanh(0.5 * predicted[:, channels:])
    values = rows_ref[...] if last else rows_ref[pl.ds(pl.multiple_of(side * count, 8), count), :]
    result = (values - predicted[:, :channels]) * jnp.exp(-log_scale)
    if last:
        term = -(first_log_ref[...] + log_scale) - 0.5 * (result * result)
        loglik = jnp.sum(term.T, axis=0, keepdims=True) * (1.0 / channels) - 0.5 * math.log(
            2.0 * math.pi
        )
        outs[0][:count, :] = result
        outs[0][count:, :count] = jnp.broadcast_to(loglik, (8, count))
    else:
        out_ref, log_ref, spread_ref, edge_ref = outs
        out_ref[...] = result
        log_ref[...] = log_scale
        edge_ref[...] = result[:8]
        narrow = result.astype(jnp.bfloat16)
        for i in range(spread_ref.shape[0]):
            spread_ref[i] = narrow


def attend(layer, members, count, positions, param_gain, rows, first_log, maps, own, queries, other, shifted, in_proj, mix_pieces, param_pieces):
    pieces = len(mix_pieces)
    channels, features = in_proj.shape[1:]
    last = first_log is not None
    keys = own.shape[0]
    chunk = next(size for size in (512, 384, 256, 128, keys) if keys % size == 0)
    near = [positions, param_gain, rows] + ([first_log] if last else [])
    far = [maps, own, queries, other, shifted, in_proj, *mix_pieces, *param_pieces]
    if last:
        out_shape = jax.ShapeDtypeStruct((count + 8, channels), jnp.float32)
        out_specs = vmem()
    else:
        out_shape = (
            jax.ShapeDtypeStruct((count, channels), jnp.float32),
            jax.ShapeDtypeStruct((count, channels), jnp.float32),
            jax.ShapeDtypeStruct((members, count, channels), jnp.bfloat16),
            jax.ShapeDtypeStruct((8, channels), jnp.float32),
        )
        out_specs = (vmem(),) * 4
    cfg = {"layer": layer, "pieces": pieces, "last": last, "count": count, "chunk": chunk}
    held = [
        maps.shape[1:],
        own.shape,
        queries.shape,
        other.shape,
        shifted.shape,
        (channels, features),
        (pieces * mix_pieces[0].shape[1], features),
        (features, param_pieces[0].shape[2]),
    ]
    return pl.pallas_call(
        functools.partial(attend_kernel, cfg),
        in_specs=[vmem()] * len(near) + [pl.BlockSpec(memory_space=pl.ANY)] * len(far),
        out_specs=out_specs,
        out_shape=out_shape,
        scratch_shapes=[pltpu.VMEM(shape, jnp.bfloat16) for shape in held]
        + [pltpu.SemaphoreType.DMA((6 + 2 * pieces,))],
        compiler_params=pltpu.CompilerParams(vmem_limit_bytes=VMEM_LIMIT),
        cost_estimate=cost(
            4 * keys * (maps.shape[1] * maps.shape[2] + queries.size * 2), size_of(far) // 2
        ),
        name="attend",
    )(*near, *far)


def finish_kernel(own_ref, other_ref, final_ref, loglik_ref):
    count = final_ref.shape[0] // 2
    side = side_of()
    for ref, place in ((own_ref, side), (other_ref, 1 - side)):
        final_ref[pl.ds(pl.multiple_of(place * count, 8), count), :] = ref[:count, :]
    first = jnp.where(side == 0, own_ref[count : count + 1, :], other_ref[count : count + 1, :])
    second = jnp.where(side == 0, other_ref[count : count + 1, :], own_ref[count : count + 1, :])
    loglik_ref[...] = jnp.concatenate([first[:, :count], second[:, :count]], axis=1)


def finish(own, other):
    count, channels = own.shape[0] - 8, own.shape[1]
    return pl.pallas_call(
        finish_kernel,
        in_specs=[vmem()] * 2,
        out_specs=(vmem(), vmem()),
        out_shape=(
            jax.ShapeDtypeStruct((2 * count, channels), jnp.float32),
            jax.ShapeDtypeStruct((1, 2 * count), jnp.float32),
        ),
        name="finish",
    )(own, other)


def body(
    latents, in_proj, query_proj, key_proj, value_proj, mix_proj, param_proj, attn_gain, param_gain
):
    members, ways = lax.axis_size("seq"), lax.axis_size("head")
    rows, channels = latents.shape
    count = rows // 2

    def swap(array):
        return lax.ppermute(array, "head", [(i, i ^ 1) for i in range(ways)])

    def pieces_of(array):
        shares = [array]
        for j in range(1, ways):
            shares.append(
                lax.ppermute(array, "head", [((i + j) % ways, i) for i in range(ways)])
            )
        return shares

    def gather(spread):
        return lax.all_to_all(spread, "seq", 0, 0).reshape(members * count, channels)

    spread, edge = spread_rows(latents, members)
    edge = lax.ppermute(edge, "seq", [(i, i + 1) for i in range(members - 1)])
    own = gather(spread)
    key_pieces, value_pieces = pieces_of(key_proj), pieces_of(value_proj)
    query_pieces, mix_pieces = pieces_of(query_proj), pieces_of(mix_proj)
    param_pieces = pieces_of(param_proj)
    maps = combine(in_proj, attn_gain, key_pieces, value_pieces)
    positions = jnp.asarray(
        (np.arange(members * count) // count * rows + np.arange(members * count) % count)[None],
        jnp.int32,
    )
    weights = (in_proj, mix_pieces, param_pieces)

    shifted, queries = make_queries(0, count, latents, edge, in_proj, attn_gain, query_pieces)
    other = swap(own)
    first_out, first_log, spread, edge = attend(
        0, members, count, positions, param_gain, latents, None, maps, own, queries, other, shifted, *weights
    )

    pairs = []
    for s in range(members):
        for w in range(ways):
            if w % 2:
                pairs.append((s * ways + w, s * ways + w - 1))
            elif s > 0:
                pairs.append((s * ways + w, (s - 1) * ways + w + 1))
    edge = lax.ppermute(edge, ("seq", "head"), pairs)
    own = gather(spread)
    shifted, queries = make_queries(1, count, first_out, edge, in_proj, attn_gain, query_pieces)
    other = swap(own)
    packed = attend(
        1, members, count, positions, param_gain, first_out, first_log, maps, own, queries, other, shifted, *weights
    )
    final_latent, token_loglik = finish(packed, swap(packed))
    return (final_latent, token_loglik.reshape(rows))


def solution(mesh):
    placed = (
        P("seq", None),
        P(),
        P(None, None, "head"),
        P(None, None, "head"),
        P(None, None, "head"),
        P(None, "head", None),
        P(None, "head", None),
        P(),
        P(),
    )
    return jax.shard_map(
        body, mesh=mesh, in_specs=placed, out_specs=(P("seq", None), P("seq")), check_vma=False
    )
```

```python
import functools
import math

import jax
import jax.numpy as jnp
import numpy as np
from jax import lax
from jax.experimental import pallas as pl
from jax.experimental.pallas import tpu as pltpu
from jax.sharding import PartitionSpec as P

HS = 64

score_scale = 8.0
epsilon = 1e-06

VMEM_LIMIT = 20 * 1024 * 1024


def dot(a, b):
    return jnp.dot(a, b, preferred_element_type=jnp.float32)


def dot_nt(a, b):
    return lax.dot_general(a, b, (((1,), (1,)), ((), ())), preferred_element_type=jnp.float32)


def cat(parts, axis):
    return parts[0] if len(parts) == 1 else jnp.concatenate(parts, axis=axis)


def side_of():
    return lax.rem(lax.axis_index("head"), 2)


def on_chip(kernel, name, operands, results, flops, out_memory=pltpu.VMEM):
    near = [pltpu.with_memory_space_constraint(array, pltpu.VMEM) for array in operands]
    if out_memory is pltpu.VMEM:
        out_shape = tuple(pltpu.VMEM(shape, dtype) for shape, dtype in results)
    else:
        out_shape = tuple(jax.ShapeDtypeStruct(shape, dtype) for shape, dtype in results)
    return pl.pallas_call(
        kernel,
        in_specs=[pl.BlockSpec(memory_space=pltpu.VMEM)] * len(operands),
        out_specs=tuple(pl.BlockSpec(memory_space=pltpu.VMEM) for _ in results),
        out_shape=out_shape,
        compiler_params=pltpu.CompilerParams(vmem_limit_bytes=VMEM_LIMIT),
        cost_estimate=pl.CostEstimate(flops=int(flops), bytes_accessed=0, transcendentals=0),
        name=name,
    )(*near)


def spread_kernel(rows_ref, spread_ref, edge_ref):
    members, count, _ = spread_ref.shape
    own = rows_ref[pl.ds(pl.multiple_of(side_of() * count, 8), count), :].astype(jnp.bfloat16)
    for i in range(members):
        spread_ref[i] = own
    edge_ref[...] = rows_ref[rows_ref.shape[0] - 8 :, :]


def combine_kernel(layer, pieces, in_ref, gain_ref, *refs):
    key_refs, value_refs, out_ref = refs[:pieces], refs[pieces : 2 * pieces], refs[2 * pieces]
    base = in_ref[layer]
    channels = base.shape[0]

    def store(row, value):
        high = value.astype(jnp.bfloat16)
        rows = value.shape[0]
        out_ref[row : row + rows, :channels] = high
        out_ref[row : row + rows, channels:] = (value - high.astype(jnp.float32)).astype(
            jnp.bfloat16
        )
        return row + rows

    scaled = base.astype(jnp.float32) * gain_ref[layer : layer + 1, :]
    high = scaled.astype(jnp.bfloat16)
    low = (scaled - high.astype(jnp.float32)).astype(jnp.bfloat16)
    both = jnp.concatenate([high, low], axis=0)
    row = 0
    for group in (key_refs, value_refs):
        for first in range(0, pieces, 2):
            columns = cat([ref[layer] for ref in group[first : first + 2]], 1)
            product = dot(both, columns)
            row = store(row, (product[:channels] + product[channels:]).T)
    row = store(row, dot_nt(base, base))
    eye = lax.broadcasted_iota(jnp.int32, (channels, channels), 0) == lax.broadcasted_iota(
        jnp.int32, (channels, channels), 1
    )
    store(row, jnp.where(eye, 1.0, 0.0))


def combine(layer, in_proj, attn_gain, key_pieces, value_pieces):
    pieces = len(key_pieces)
    _, channels, features = in_proj.shape
    rows = 2 * pieces * key_pieces[0].shape[2] + 2 * channels
    return on_chip(
        functools.partial(combine_kernel, layer, pieces),
        "combine",
        [in_proj, attn_gain, *key_pieces, *value_pieces],
        [((rows, 2 * channels), jnp.bfloat16)],
        4 * channels * features * rows,
    )[0]


def queries_kernel(layer, pieces, rows_ref, edge_ref, in_ref, gain_ref, *refs):
    query_refs, shifted_ref, out_ref = refs[:pieces], refs[pieces], refs[pieces + 1]
    count = shifted_ref.shape[0]
    token = lax.broadcasted_iota(jnp.int32, (count, 1), 0)
    if layer == 0:
        start = pl.multiple_of(side_of() * count, 8)
        values = rows_ref[pl.ds(start, count), :]
        border = jnp.where(side_of() == 0, edge_ref[7:8, :], rows_ref[count - 1 : count, :])
        moved, at = pltpu.roll(values, 1, 0), 0
    else:
        values = rows_ref[...]
        border = edge_ref[0:1, :]
        moved, at = pltpu.roll(values, count - 1, 0), count - 1
    shifted = jnp.where(token == at, border, moved).astype(jnp.bfloat16)
    shifted_ref[...] = shifted
    hidden = dot(shifted, in_ref[layer])
    spread = lax.rsqrt(jnp.mean(hidden * hidden, axis=1, keepdims=True) + epsilon)
    normed = (hidden * spread * gain_ref[layer : layer + 1, :]).astype(jnp.bfloat16)
    for first in range(0, pieces, 2):
        query = dot(normed, cat([ref[layer] for ref in query_refs[first : first + 2]], 1))
        width = query.shape[1]
        head = lax.broadcasted_iota(jnp.int32, (count, width), 1) // HS
        for h in range(width // HS):
            band = jnp.where(head == h, query, 0.0)
            mean = jnp.sum(band * band, axis=1, keepdims=True) * (1.0 / HS)
            out_ref[first // 2, h * count : (h + 1) * count, :] = (
                band * lax.rsqrt(mean + epsilon)
            ).astype(jnp.bfloat16)


def make_queries(layer, count, rows, edge, in_proj, attn_gain, query_pieces):
    pieces = len(query_pieces)
    channels, features = in_proj.shape[1:]
    width = min(2, pieces) * query_pieces[0].shape[2]
    groups = pieces * query_pieces[0].shape[2] // width
    return on_chip(
        functools.partial(queries_kernel, layer, pieces),
        "queries",
        [rows, edge, in_proj, attn_gain, *query_pieces],
        [
            ((count, channels), jnp.bfloat16),
            ((groups, width // HS * count, width), jnp.bfloat16),
        ],
        2 * count * features * (channels + groups * width),
    )


def attend_rows(cfg, place, pos_ref, maps_ref, query_ref, source_ref, carry):
    count, features, size = cfg["count"], cfg["features"], cfg["chunk"]
    side = side_of()
    groups, _, group_cols = query_ref.shape
    channels = source_ref.shape[1]
    heads = group_cols // HS
    total_cols = groups * group_cols
    token = lax.broadcasted_iota(jnp.int32, (count, 1), 0)
    first_token = lax.axis_index("seq") * (2 * count) + side * count
    query_token = first_token + jnp.concatenate([token] * heads, axis=0)
    offset = (side if place == 0 else 1 - side) * count

    def one_chunk(start, carry):
        source = source_ref[pl.ds(start, size), :]
        twice = jnp.concatenate([source, source], axis=1)
        key_token = pos_ref[:, pl.ds(start, size)] + offset
        allowed = key_token < query_token if cfg["layer"] == 0 else key_token > query_token
        tail = dot_nt(maps_ref[2 * total_cols :, :], twice)
        square = jnp.sum(tail[:channels] * tail[channels:], axis=0, keepdims=True)
        scale = lax.rsqrt(jnp.maximum(square, 0.0) * (1.0 / features) + epsilon)
        scale_sq = scale * scale
        result = []
        for g in range(groups):
            low = g * group_cols
            key = dot_nt(maps_ref[low : low + group_cols, :], twice)
            value = dot_nt(maps_ref[total_cols + low : total_cols + low + group_cols, :], twice)
            keys = []
            for h in range(heads):
                one = key[h * HS : (h + 1) * HS]
                mean = jnp.sum(one * one, axis=0, keepdims=True) * (1.0 / HS)
                factor = scale * lax.rsqrt(mean * scale_sq + epsilon)
                keys.append((one * factor).astype(jnp.bfloat16))
            value = (value * scale).astype(jnp.bfloat16)
            scores = dot(query_ref[g], jnp.concatenate(keys, axis=0)) * (score_scale / HS)
            weights = jnp.where(allowed, jnp.exp(scores), 0.0)
            product = dot_nt(weights.astype(jnp.bfloat16), value)
            total = weights[:, :128]
            for lane in range(128, size, 128):
                total = total + weights[:, lane : lane + 128]
            result.append(
                (product, total)
                if carry is None
                else (carry[g][0] + product, carry[g][1] + total)
            )
        return tuple(result)

    chunks = source_ref.shape[0] // size
    carry = one_chunk(0, carry)
    if chunks <= 4:
        for c in range(1, chunks):
            carry = one_chunk(c * size, carry)
    else:
        carry = lax.fori_loop(
            1, chunks, lambda c, now: one_chunk(pl.multiple_of(c * size, size), now), carry
        )
    return carry


def first_half_kernel(cfg, pos_ref, maps_ref, query_ref, own_ref, number_ref, total_ref):
    carry = attend_rows(cfg, 0, pos_ref, maps_ref, query_ref, own_ref, None)
    for g, (number, total) in enumerate(carry):
        number_ref[g] = number
        total_ref[g] = total


def second_half_kernel(cfg, pos_ref, maps_ref, query_ref, other_ref, number_ref, total_ref, shifted_ref, in_ref, gain_ref, rows_ref, *refs):
    layer, pieces, last, count = cfg["layer"], cfg["pieces"], cfg["last"], cfg["count"]
    refs = list(refs)
    mix_refs = [refs.pop(0) for _ in range(pieces)]
    param_refs = [refs.pop(0) for _ in range(pieces)]
    side, way = side_of(), lax.axis_index("head")
    channels, features = in_ref.shape[1:]
    groups, _, group_cols = query_ref.shape
    heads = group_cols // HS
    carry = tuple((number_ref[g], total_ref[g]) for g in range(groups))
    carry = attend_rows(cfg, 1, pos_ref, maps_ref, query_ref, other_ref, carry)

    mixture = dot(shifted_ref[...], in_ref[layer])
    head = lax.broadcasted_iota(jnp.int32, (count, group_cols), 1) // HS
    for g, (number, total) in enumerate(carry):
        share_of = 1.0 / (jnp.sum(total, axis=1, keepdims=True) + 1.0)
        attended = jnp.zeros((count, group_cols), jnp.float32)
        for h in range(heads):
            band = slice(h * count, (h + 1) * count)
            attended = jnp.where(head == h, number[band] * share_of[band], attended)
        rows = cat([ref[layer] for ref in mix_refs[2 * g : 2 * g + 2]], 0)
        mixture = mixture + dot(attended.astype(jnp.bfloat16), rows)
    spread = lax.rsqrt(jnp.mean(mixture * mixture, axis=1, keepdims=True) + epsilon)
    scaled = (mixture * spread * gain_ref[layer : layer + 1, :]).astype(jnp.bfloat16)
    share = features // pieces
    param_all = refs[-1]
    for j, ref in enumerate(param_refs):
        at = pl.multiple_of(lax.rem(way + j, pieces) * share, 16)
        param_all[pl.ds(at, share), :] = ref[layer]
    predicted = dot(scaled, param_all[...])
    log_scale = 2.0 * jnp.tanh(0.5 * predicted[:, channels:])
    if last:
        first_log_ref, out_ref = refs[:2]
        values = rows_ref[...]
        result = (values - predicted[:, :channels]) * jnp.exp(-log_scale)
        term = -(first_log_ref[...] + log_scale) - 0.5 * (result * result)
        loglik = jnp.sum(term.T, axis=0, keepdims=True) * (1.0 / channels) - 0.5 * math.log(
            2.0 * math.pi
        )
        out_ref[:count, :] = result
        out_ref[count:, :count] = jnp.broadcast_to(loglik, (8, count))
    else:
        out_ref, log_ref, spread_ref, edge_ref = refs[:4]
        values = rows_ref[pl.ds(pl.multiple_of(side * count, 8), count), :]
        result = (values - predicted[:, :channels]) * jnp.exp(-log_scale)
        out_ref[...] = result
        log_ref[...] = log_scale
        edge_ref[...] = result[:8]
        narrow = result.astype(jnp.bfloat16)
        for i in range(spread_ref.shape[0]):
            spread_ref[i] = narrow


def config(layer, count, features, pieces, keys):
    chunk = next(size for size in (512, 384, 256, 128, keys) if keys % size == 0)
    return {
        "layer": layer,
        "last": layer == 1,
        "count": count,
        "features": features,
        "pieces": pieces,
        "chunk": chunk,
    }


def first_half(cfg, positions, maps, queries, own):
    groups, rows, cols = queries.shape
    return on_chip(
        functools.partial(first_half_kernel, cfg),
        "first_half",
        [positions, maps, queries, own],
        [((groups, rows, cols), jnp.float32), ((groups, rows, 128), jnp.float32)],
        2 * own.shape[0] * (maps.size + 2 * queries.size),
    )


def second_half(cfg, members, positions, maps, queries, other, sums, shifted, in_proj, param_gain, rows, mix_pieces, param_pieces, first_log=None):
    count, channels = shifted.shape
    operands = [positions, maps, queries, other, *sums, shifted, in_proj, param_gain, rows]
    operands += [*mix_pieces, *param_pieces]
    if cfg["last"]:
        operands.append(first_log)
        results = [((count + 8, channels), jnp.float32)]
    else:
        results = [
            ((count, channels), jnp.float32),
            ((count, channels), jnp.float32),
            ((members, count, channels), jnp.bfloat16),
            ((8, channels), jnp.float32),
        ]
    results.append(((cfg["features"], param_pieces[0].shape[2]), jnp.bfloat16))
    return on_chip(
        functools.partial(second_half_kernel, cfg),
        "second_half",
        operands,
        results,
        2 * other.shape[0] * (maps.size + 2 * queries.size),
    )[:-1]


def finish_kernel(own_ref, other_ref, final_ref, loglik_ref):
    count = final_ref.shape[0] // 2
    side = side_of()
    for ref, place in ((own_ref, side), (other_ref, 1 - side)):
        final_ref[pl.ds(pl.multiple_of(place * count, 8), count), :] = ref[:count, :]
    first = jnp.where(side == 0, own_ref[count : count + 1, :], other_ref[count : count + 1, :])
    second = jnp.where(side == 0, other_ref[count : count + 1, :], own_ref[count : count + 1, :])
    loglik_ref[...] = jnp.concatenate([first[:, :count], second[:, :count]], axis=1)


def body(
    latents, in_proj, query_proj, key_proj, value_proj, mix_proj, param_proj, attn_gain, param_gain
):
    members, ways = lax.axis_size("seq"), lax.axis_size("head")
    rows, channels = latents.shape
    features = in_proj.shape[2]
    count = rows // 2
    keys = members * count

    def swap(array):
        return lax.ppermute(array, "head", [(i, i ^ 1) for i in range(ways)])

    def pieces_of(array):
        shares = [array]
        for j in range(1, ways):
            shares.append(
                lax.ppermute(array, "head", [((i + j) % ways, i) for i in range(ways)])
            )
        return shares

    def gather(spread):
        return lax.all_to_all(spread, "seq", 0, 0).reshape(keys, channels)

    spread, edge = on_chip(
        spread_kernel,
        "spread_rows",
        [latents],
        [((members, count, channels), jnp.bfloat16), ((8, channels), jnp.float32)],
        keys * channels,
    )
    own = gather(spread)
    edge = lax.ppermute(edge, "seq", [(i, i + 1) for i in range(members - 1)])
    key_pieces, value_pieces = pieces_of(key_proj), pieces_of(value_proj)
    query_pieces, mix_pieces = pieces_of(query_proj), pieces_of(mix_proj)
    param_pieces = pieces_of(param_proj)
    maps = [combine(b, in_proj, attn_gain, key_pieces, value_pieces) for b in range(2)]
    shifted, queries = make_queries(0, count, latents, edge, in_proj, attn_gain, query_pieces)
    positions = jnp.asarray(
        (np.arange(keys) // count * rows + np.arange(keys) % count)[None], jnp.int32
    )
    own, maps, shifted, queries = lax.optimization_barrier((own, maps, shifted, queries))

    cfg = config(0, count, features, ways, keys)
    other = swap(own)
    sums = first_half(cfg, positions, maps[0], queries, own)
    first_out, first_log, spread, edge = second_half(
        cfg, members, positions, maps[0], queries, other, sums, shifted, in_proj, param_gain, latents, mix_pieces, param_pieces
    )

    pairs = []
    for s in range(members):
        for w in range(ways):
            if w % 2:
                pairs.append((s * ways + w, s * ways + w - 1))
            elif s > 0:
                pairs.append((s * ways + w, (s - 1) * ways + w + 1))
    own = gather(spread)
    edge = lax.ppermute(edge, ("seq", "head"), pairs)
    shifted, queries = make_queries(1, count, first_out, edge, in_proj, attn_gain, query_pieces)
    cfg = config(1, count, features, ways, keys)
    other = swap(own)
    sums = first_half(cfg, positions, maps[1], queries, own)
    (packed,) = second_half(
        cfg, members, positions, maps[1], queries, other, sums, shifted, in_proj, param_gain, first_out, mix_pieces, param_pieces, first_log
    )
    final_latent, token_loglik = on_chip(
        finish_kernel,
        "finish",
        [packed, swap(packed)],
        [((rows, channels), jnp.float32), ((1, rows), jnp.float32)],
        rows * channels,
        out_memory=None,
    )
    return (final_latent, token_loglik.reshape(rows))


def solution(mesh):
    placed = (
        P("seq", None),
        P(),
        P(None, None, "head"),
        P(None, None, "head"),
        P(None, None, "head"),
        P(None, "head", None),
        P(None, "head", None),
        P(),
        P(),
    )
    return jax.shard_map(
        body, mesh=mesh, in_specs=placed, out_specs=(P("seq", None), P("seq")), check_vma=False
    )
```

```python
import functools
import math

import jax
import jax.numpy as jnp
from jax import lax
from jax.experimental import pallas as pl
from jax.experimental.pallas import tpu as pltpu
from jax.sharding import PartitionSpec as P

HS = 64

score_scale = 8.0
epsilon = 1e-06

VMEM_LIMIT = 20 * 1024 * 1024


def dot(a, b):
    return jnp.dot(a, b, preferred_element_type=jnp.float32)


def dot_nt(a, b):
    return lax.dot_general(a, b, (((1,), (1,)), ((), ())), preferred_element_type=jnp.float32)


def cat(parts, axis):
    return parts[0] if len(parts) == 1 else jnp.concatenate(parts, axis=axis)


def side_of():
    return lax.rem(lax.axis_index("head"), 2)


def on_chip(kernel, name, operands, results, flops, out_memory=pltpu.VMEM, scratch=()):
    near = [pltpu.with_memory_space_constraint(array, pltpu.VMEM) for array in operands]
    if out_memory is pltpu.VMEM:
        out_shape = tuple(pltpu.VMEM(shape, dtype) for shape, dtype in results)
    else:
        out_shape = tuple(jax.ShapeDtypeStruct(shape, dtype) for shape, dtype in results)
    return pl.pallas_call(
        kernel,
        in_specs=[pl.BlockSpec(memory_space=pltpu.VMEM)] * len(operands),
        out_specs=tuple(pl.BlockSpec(memory_space=pltpu.VMEM) for _ in results),
        out_shape=out_shape,
        scratch_shapes=list(scratch),
        compiler_params=pltpu.CompilerParams(vmem_limit_bytes=VMEM_LIMIT),
        cost_estimate=pl.CostEstimate(flops=int(flops), bytes_accessed=0, transcendentals=0),
        name=name,
    )(*near)


def spread_kernel(rows_ref, spread_ref):
    members, count, _ = spread_ref.shape
    own = rows_ref[pl.ds(pl.multiple_of(side_of() * count, 8), count), :].astype(jnp.bfloat16)
    for i in range(members):
        spread_ref[i] = own


def gate_kernel(own_ref, *refs):
    refs[-1][...] = own_ref[...]


def gate(own, *made):
    return on_chip(gate_kernel, "gate", [own, *made], [(own.shape, own.dtype)], own.size)[0]


def combine_kernel(layer, pieces, in_ref, gain_ref, *refs):
    key_refs, value_refs, out_ref = refs[:pieces], refs[pieces : 2 * pieces], refs[2 * pieces]
    base = in_ref[layer]
    channels = base.shape[0]

    def store(row, value):
        high = value.astype(jnp.bfloat16)
        rows = value.shape[0]
        out_ref[row : row + rows, :channels] = high
        out_ref[row : row + rows, channels:] = (value - high.astype(jnp.float32)).astype(
            jnp.bfloat16
        )
        return row + rows

    scaled = base.astype(jnp.float32) * gain_ref[layer : layer + 1, :]
    high = scaled.astype(jnp.bfloat16)
    low = (scaled - high.astype(jnp.float32)).astype(jnp.bfloat16)
    both = jnp.concatenate([high, low], axis=0)
    row = 0
    for group in (key_refs, value_refs):
        for first in range(0, pieces, 2):
            columns = cat([ref[layer] for ref in group[first : first + 2]], 1)
            product = dot(both, columns)
            row = store(row, (product[:channels] + product[channels:]).T)
    row = store(row, dot_nt(base, base))
    eye = lax.broadcasted_iota(jnp.int32, (channels, channels), 0) == lax.broadcasted_iota(
        jnp.int32, (channels, channels), 1
    )
    store(row, jnp.where(eye, 1.0, 0.0))


def combine(layer, in_proj, attn_gain, key_pieces, value_pieces):
    pieces = len(key_pieces)
    _, channels, features = in_proj.shape
    rows = 2 * pieces * key_pieces[0].shape[2] + 2 * channels
    return on_chip(
        functools.partial(combine_kernel, layer, pieces),
        "combine",
        [in_proj, attn_gain, *key_pieces, *value_pieces],
        [((rows, 2 * channels), jnp.bfloat16)],
        4 * channels * features * rows,
    )[0]


def queries_kernel(layer, pieces, rows_ref, in_ref, gain_ref, *refs):
    query_refs, hidden_ref, out_ref = refs[:pieces], refs[pieces], refs[pieces + 1]
    count = hidden_ref.shape[0]
    if layer == 0:
        rows = rows_ref[pl.ds(pl.multiple_of(side_of() * count, 8), count), :]
    else:
        rows = rows_ref[...]
    hidden = dot(rows.astype(jnp.bfloat16), in_ref[layer])
    hidden_ref[...] = hidden
    spread = lax.rsqrt(jnp.mean(hidden * hidden, axis=1, keepdims=True) + epsilon)
    normed = (hidden * spread * gain_ref[layer : layer + 1, :]).astype(jnp.bfloat16)
    for first in range(0, pieces, 2):
        query = dot(normed, cat([ref[layer] for ref in query_refs[first : first + 2]], 1))
        width = query.shape[1]
        head = lax.broadcasted_iota(jnp.int32, (count, width), 1) // HS
        for h in range(width // HS):
            band = jnp.where(head == h, query, 0.0)
            mean = jnp.sum(band * band, axis=1, keepdims=True) * (1.0 / HS)
            out_ref[first // 2, h * count : (h + 1) * count, :] = (
                band * lax.rsqrt(mean + epsilon)
            ).astype(jnp.bfloat16)


def make_queries(layer, count, rows, in_proj, attn_gain, query_pieces):
    pieces = len(query_pieces)
    channels, features = in_proj.shape[1:]
    width = min(2, pieces) * query_pieces[0].shape[2]
    groups = pieces * query_pieces[0].shape[2] // width
    return on_chip(
        functools.partial(queries_kernel, layer, pieces),
        "queries",
        [rows, in_proj, attn_gain, *query_pieces],
        [
            ((count, features), jnp.float32),
            ((groups, width // HS * count, width), jnp.bfloat16),
        ],
        2 * count * features * (channels + groups * width),
    )


def attend_rows(cfg, place, maps_ref, query_ref, source_ref, carry):
    count, features, size = cfg["count"], cfg["features"], cfg["chunk"]
    side = side_of()
    groups, _, group_cols = query_ref.shape
    channels = source_ref.shape[1]
    heads = group_cols // HS
    total_cols = groups * group_cols
    token = lax.broadcasted_iota(jnp.int32, (count, 1), 0)
    first_token = lax.axis_index("seq") * (2 * count) + side * count
    query_place = first_token + jnp.concatenate([token] * heads, axis=0)
    offset = (side if place == 0 else 1 - side) * count
    lane = lax.broadcasted_iota(jnp.int32, (1, size), 1)

    def one_chunk(start, carry):
        source = source_ref[pl.ds(start, size), :]
        twice = jnp.concatenate([source, source], axis=1)
        member = ((lane + start).astype(jnp.float32) + 0.5) * (1.0 / count)
        key_place = lane + start + member.astype(jnp.int32) * count + offset
        allowed = key_place <= query_place if cfg["layer"] == 0 else key_place >= query_place
        tail = dot_nt(maps_ref[2 * total_cols :, :], twice)
        square = jnp.sum(tail[:channels] * tail[channels:], axis=0, keepdims=True)
        scale = lax.rsqrt(jnp.maximum(square, 0.0) * (1.0 / features) + epsilon)
        scale_sq = scale * scale
        result = []
        for g in range(groups):
            low = g * group_cols
            key = dot_nt(maps_ref[low : low + group_cols, :], twice)
            value = dot_nt(maps_ref[total_cols + low : total_cols + low + group_cols, :], twice)
            keys = []
            for h in range(heads):
                one = key[h * HS : (h + 1) * HS]
                mean = jnp.sum(one * one, axis=0, keepdims=True) * (1.0 / HS)
                factor = scale * lax.rsqrt(mean * scale_sq + epsilon)
                keys.append((one * factor).astype(jnp.bfloat16))
            value = (value * scale).astype(jnp.bfloat16)
            scores = dot(query_ref[g], jnp.concatenate(keys, axis=0)) * (score_scale / HS)
            weights = jnp.where(allowed, jnp.exp(scores), 0.0)
            product = dot_nt(weights.astype(jnp.bfloat16), value)
            total = weights[:, :128]
            for at in range(128, size, 128):
                total = total + weights[:, at : at + 128]
            result.append(
                (product, total)
                if carry is None
                else (carry[g][0] + product, carry[g][1] + total)
            )
        return tuple(result)

    chunks = source_ref.shape[0] // size
    carry = one_chunk(0, carry)
    if chunks <= 4:
        for c in range(1, chunks):
            carry = one_chunk(c * size, carry)
    else:
        carry = lax.fori_loop(
            1, chunks, lambda c, now: one_chunk(pl.multiple_of(c * size, size), now), carry
        )
    return carry


def first_half_kernel(cfg, maps_ref, query_ref, own_ref, number_ref, total_ref):
    carry = attend_rows(cfg, 0, maps_ref, query_ref, own_ref, None)
    for g, (number, total) in enumerate(carry):
        number_ref[g] = number
        total_ref[g] = total


def second_half_kernel(cfg, maps_ref, query_ref, other_ref, number_ref, total_ref, hidden_ref, gain_ref, latent_ref, *refs):
    layer, pieces, last, count = cfg["layer"], cfg["pieces"], cfg["last"], cfg["count"]
    refs = list(refs)
    mix_refs = [refs.pop(0) for _ in range(pieces)]
    param_refs = [refs.pop(0) for _ in range(pieces)]
    side, way, member = side_of(), lax.axis_index("head"), lax.axis_index("seq")
    members = other_ref.shape[0] // count
    features, channels = hidden_ref.shape[1], latent_ref.shape[1]
    groups, _, group_cols = query_ref.shape
    heads = group_cols // HS
    carry = tuple((number_ref[g], total_ref[g]) for g in range(groups))
    carry = attend_rows(cfg, 1, maps_ref, query_ref, other_ref, carry)

    mixture = hidden_ref[...]
    head = lax.broadcasted_iota(jnp.int32, (count, group_cols), 1) // HS
    for g, (number, total) in enumerate(carry):
        total = jnp.sum(total, axis=1, keepdims=True) + (0.0 if last else 1.0)
        share_of = 1.0 / total
        attended = jnp.zeros((count, group_cols), jnp.float32)
        for h in range(heads):
            band = slice(h * count, (h + 1) * count)
            attended = jnp.where(head == h, number[band] * share_of[band], attended)
        rows = cat([ref[layer] for ref in mix_refs[2 * g : 2 * g + 2]], 0)
        mixture = mixture + dot(attended.astype(jnp.bfloat16), rows)
    spread = lax.rsqrt(jnp.mean(mixture * mixture, axis=1, keepdims=True) + epsilon)
    scaled = (mixture * spread * gain_ref[layer : layer + 1, :]).astype(jnp.bfloat16)
    share = features // pieces
    param_all = refs[-1]
    for j, ref in enumerate(param_refs):
        at = pl.multiple_of(lax.rem(way + j, pieces) * share, 16)
        param_all[pl.ds(at, share), :] = ref[layer]
    predicted = dot(scaled, param_all[...])
    shift_mu = predicted[:, :channels]
    log_scale = 2.0 * jnp.tanh(0.5 * predicted[:, channels:])
    token = lax.broadcasted_iota(jnp.int32, (count, 1), 0)
    start = pl.multiple_of(side * count, 8)
    if last:
        held_ref, held_log_ref, edge_ref, out_ref = refs[:4]
        edge_log = edge_ref[15:16, :]
        first = (latent_ref[pl.ds(start, 8), :][:1] - edge_ref[7:8, :]) * jnp.exp(-edge_log)
        values = jnp.where(token == 0, first, pltpu.roll(held_ref[...], 1, 0))
        first_log = jnp.where(token == 0, edge_log, pltpu.roll(held_log_ref[...], 1, 0))
        result = (values - shift_mu) * jnp.exp(-log_scale)
        term = -(first_log + log_scale) - 0.5 * (result * result)
        loglik = jnp.sum(term.T, axis=0, keepdims=True) * (1.0 / channels) - 0.5 * math.log(
            2.0 * math.pi
        )
        out_ref[:count, :] = result
        out_ref[count:, :count] = jnp.broadcast_to(loglik, (8, count))
    else:
        held_ref, held_log_ref, edge_ref, spread_ref = refs[:4]
        following = pl.multiple_of(jnp.minimum(member + 1, members - 1) * count, 16)
        after = other_ref[pl.ds(following, 16), :].astype(jnp.float32)[:1]
        after = jnp.where(side == 0, latent_ref[count : count + 1, :], after)
        values = pltpu.roll(latent_ref[pl.ds(start, count), :], count - 1, 0)
        values = jnp.where(token == count - 1, after, values)
        result = (values - shift_mu) * jnp.exp(-log_scale)
        beyond = (member * 2 + side) * count + token == members * 2 * count - 1
        result = jnp.where(beyond, 0.0, result)
        held_ref[...] = result
        held_log_ref[...] = log_scale
        edge_ref[:8, :] = shift_mu[count - 8 :]
        edge_ref[8:, :] = log_scale[count - 8 :]
        narrow = result.astype(jnp.bfloat16)
        for i in range(members):
            spread_ref[i] = narrow


def config(layer, count, features, pieces, keys):
    chunk = next(size for size in (512, 384, 256, 128, keys) if keys % size == 0)
    return {
        "layer": layer,
        "last": layer == 1,
        "count": count,
        "features": features,
        "pieces": pieces,
        "chunk": chunk,
    }


def first_half(cfg, maps, queries, own):
    groups, rows, cols = queries.shape
    return on_chip(
        functools.partial(first_half_kernel, cfg),
        "first_half",
        [maps, queries, own],
        [((groups, rows, cols), jnp.float32), ((groups, rows, 128), jnp.float32)],
        2 * own.shape[0] * (maps.size + 2 * queries.size),
    )


def second_half(cfg, members, maps, queries, other, sums, hidden, param_gain, latents, mix_pieces, param_pieces, held=()):
    count, channels = cfg["count"], latents.shape[1]
    operands = [maps, queries, other, *sums, hidden, param_gain, latents]
    operands += [*mix_pieces, *param_pieces, *held]
    if cfg["last"]:
        results = [((count + 8, channels), jnp.float32)]
    else:
        results = [
            ((count, channels), jnp.float32),
            ((count, channels), jnp.float32),
            ((16, channels), jnp.float32),
            ((members, count, channels), jnp.bfloat16),
        ]
    return on_chip(
        functools.partial(second_half_kernel, cfg),
        "second_half",
        operands,
        results,
        2 * other.shape[0] * (maps.size + 2 * queries.size),
        scratch=[pltpu.VMEM((cfg["features"], param_pieces[0].shape[2]), jnp.bfloat16)],
    )


def finish_kernel(own_ref, other_ref, final_ref, loglik_ref):
    count = final_ref.shape[0] // 2
    side = side_of()
    for ref, place in ((own_ref, side), (other_ref, 1 - side)):
        final_ref[pl.ds(pl.multiple_of(place * count, 8), count), :] = ref[:count, :]
    first = jnp.where(side == 0, own_ref[count : count + 1, :], other_ref[count : count + 1, :])
    second = jnp.where(side == 0, other_ref[count : count + 1, :], own_ref[count : count + 1, :])
    loglik_ref[...] = jnp.concatenate([first[:, :count], second[:, :count]], axis=1)


def body(
    latents, in_proj, query_proj, key_proj, value_proj, mix_proj, param_proj, attn_gain, param_gain
):
    members, ways = lax.axis_size("seq"), lax.axis_size("head")
    rows, channels = latents.shape
    features = in_proj.shape[2]
    count = rows // 2
    keys = members * count

    def swap(array):
        return lax.ppermute(array, "head", [(i, i ^ 1) for i in range(ways)])

    def pieces_of(array):
        shares = [array]
        for j in range(1, ways):
            shares.append(
                lax.ppermute(array, "head", [((i + j) % ways, i) for i in range(ways)])
            )
        return shares

    def gather(spread):
        return lax.all_to_all(spread, "seq", 0, 0).reshape(keys, channels)

    (spread,) = on_chip(
        spread_kernel,
        "spread_rows",
        [latents],
        [((members, count, channels), jnp.bfloat16)],
        keys * channels,
    )
    own = gather(spread)
    key_pieces, value_pieces = pieces_of(key_proj), pieces_of(value_proj)
    query_pieces, mix_pieces = pieces_of(query_proj), pieces_of(mix_proj)
    param_pieces = pieces_of(param_proj)
    maps = [combine(b, in_proj, attn_gain, key_pieces, value_pieces) for b in range(2)]
    hidden, queries = make_queries(0, count, latents, in_proj, attn_gain, query_pieces)
    own = gate(own, *maps, queries)

    cfg = config(0, count, features, ways, keys)
    other = swap(own)
    sums = first_half(cfg, maps[0], queries, own)
    held, held_log, edge, spread = second_half(
        cfg, members, maps[0], queries, other, sums, hidden, param_gain, latents, mix_pieces, param_pieces
    )

    own = gather(spread)
    pairs = []
    for s in range(members):
        for w in range(ways):
            if w % 2 == 0:
                pairs.append((s * ways + w, s * ways + w + 1))
            elif s < members - 1:
                pairs.append((s * ways + w, (s + 1) * ways + w - 1))
    edge = lax.ppermute(edge, ("seq", "head"), pairs)
    hidden, queries = make_queries(1, count, held, in_proj, attn_gain, query_pieces)
    own = gate(own, queries)
    cfg = config(1, count, features, ways, keys)
    other = swap(own)
    sums = first_half(cfg, maps[1], queries, own)
    (packed,) = second_half(
        cfg, members, maps[1], queries, other, sums, hidden, param_gain, latents, mix_pieces, param_pieces, (held, held_log, edge)
    )
    final_latent, token_loglik = on_chip(
        finish_kernel,
        "finish",
        [packed, swap(packed)],
        [((rows, channels), jnp.float32), ((1, rows), jnp.float32)],
        rows * channels,
        out_memory=None,
    )
    return (final_latent, token_loglik.reshape(rows))


def solution(mesh):
    placed = (
        P("seq", None),
        P(),
        P(None, None, "head"),
        P(None, None, "head"),
        P(None, None, "head"),
        P(None, "head", None),
        P(None, "head", None),
        P(),
        P(),
    )
    return jax.shard_map(
        body, mesh=mesh, in_specs=placed, out_specs=(P("seq", None), P("seq")), check_vma=False
    )
```

```python
import functools
import math

import jax
import jax.numpy as jnp
from jax import lax
from jax.experimental import pallas as pl
from jax.experimental.pallas import tpu as pltpu
from jax.sharding import PartitionSpec as P

HS = 64

score_scale = 8.0
epsilon = 1e-06

VMEM_LIMIT = 20 * 1024 * 1024


def dot(a, b):
    return jnp.dot(a, b, preferred_element_type=jnp.float32)


def dot_nt(a, b):
    return lax.dot_general(a, b, (((1,), (1,)), ((), ())), preferred_element_type=jnp.float32)


def cat(parts, axis):
    return parts[0] if len(parts) == 1 else jnp.concatenate(parts, axis=axis)


def side_of():
    return lax.rem(lax.axis_index("head"), 2)


def on_chip(kernel, name, operands, results, flops, out_memory=pltpu.VMEM, scratch=()):
    near = [pltpu.with_memory_space_constraint(array, pltpu.VMEM) for array in operands]
    if out_memory is pltpu.VMEM:
        out_shape = tuple(pltpu.VMEM(shape, dtype) for shape, dtype in results)
    else:
        out_shape = tuple(jax.ShapeDtypeStruct(shape, dtype) for shape, dtype in results)
    return pl.pallas_call(
        kernel,
        in_specs=[pl.BlockSpec(memory_space=pltpu.VMEM)] * len(operands),
        out_specs=tuple(pl.BlockSpec(memory_space=pltpu.VMEM) for _ in results),
        out_shape=out_shape,
        scratch_shapes=list(scratch),
        compiler_params=pltpu.CompilerParams(vmem_limit_bytes=VMEM_LIMIT),
        cost_estimate=pl.CostEstimate(flops=int(flops), bytes_accessed=0, transcendentals=0),
        name=name,
    )(*near)


def spread_kernel(rows_ref, spread_ref):
    members, count, _ = spread_ref.shape
    own = rows_ref[pl.ds(pl.multiple_of(side_of() * count, 8), count), :].astype(jnp.bfloat16)
    for i in range(members):
        spread_ref[i] = own


def gate_kernel(own_ref, *refs):
    refs[-1][...] = own_ref[...]


def gate(own, *made):
    return on_chip(gate_kernel, "gate", [own, *made], [(own.shape, own.dtype)], own.size)[0]


def combine_kernel(layer, pieces, in_ref, gain_ref, *refs):
    key_refs, value_refs, out_ref = refs[:pieces], refs[pieces : 2 * pieces], refs[2 * pieces]
    base = in_ref[layer]
    channels = base.shape[0]

    def store(row, value):
        high = value.astype(jnp.bfloat16)
        rows = value.shape[0]
        out_ref[row : row + rows, :channels] = high
        out_ref[row : row + rows, channels:] = (value - high.astype(jnp.float32)).astype(
            jnp.bfloat16
        )
        return row + rows

    scaled = base.astype(jnp.float32) * gain_ref[layer : layer + 1, :]
    high = scaled.astype(jnp.bfloat16)
    low = (scaled - high.astype(jnp.float32)).astype(jnp.bfloat16)
    both = jnp.concatenate([high, low], axis=0)
    row = 0
    for group in (key_refs, value_refs):
        for first in range(0, pieces, 2):
            columns = cat([ref[layer] for ref in group[first : first + 2]], 1)
            product = dot(both, columns)
            row = store(row, (product[:channels] + product[channels:]).T)
    row = store(row, dot_nt(base, base))
    eye = lax.broadcasted_iota(jnp.int32, (channels, channels), 0) == lax.broadcasted_iota(
        jnp.int32, (channels, channels), 1
    )
    store(row, jnp.where(eye, 1.0, 0.0))


def combine(layer, in_proj, attn_gain, key_pieces, value_pieces):
    pieces = len(key_pieces)
    _, channels, features = in_proj.shape
    rows = 2 * pieces * key_pieces[0].shape[2] + 2 * channels
    return on_chip(
        functools.partial(combine_kernel, layer, pieces),
        "combine",
        [in_proj, attn_gain, *key_pieces, *value_pieces],
        [((rows, 2 * channels), jnp.bfloat16)],
        4 * channels * features * rows,
    )[0]


def store_queries(layer, rows, in_ref, gain_ref, query_refs, hidden_ref, out_ref):
    count = hidden_ref.shape[0]
    hidden = dot(rows, in_ref[layer])
    hidden_ref[...] = hidden
    spread = lax.rsqrt(jnp.mean(hidden * hidden, axis=1, keepdims=True) + epsilon)
    normed = (hidden * spread * gain_ref[layer : layer + 1, :]).astype(jnp.bfloat16)
    for first in range(0, len(query_refs), 2):
        query = dot(normed, cat([ref[layer] for ref in query_refs[first : first + 2]], 1))
        width = query.shape[1]
        head = lax.broadcasted_iota(jnp.int32, (count, width), 1) // HS
        for h in range(width // HS):
            band = jnp.where(head == h, query, 0.0)
            mean = jnp.sum(band * band, axis=1, keepdims=True) * (1.0 / HS)
            out_ref[first // 2, h * count : (h + 1) * count, :] = (
                band * lax.rsqrt(mean + epsilon)
            ).astype(jnp.bfloat16)


def queries_kernel(pieces, rows_ref, in_ref, gain_ref, *refs):
    count = refs[pieces].shape[0]
    rows = rows_ref[pl.ds(pl.multiple_of(side_of() * count, 8), count), :].astype(jnp.bfloat16)
    store_queries(0, rows, in_ref, gain_ref, refs[:pieces], refs[pieces], refs[pieces + 1])


def query_shapes(count, in_proj, query_pieces):
    pieces, head_cols = len(query_pieces), query_pieces[0].shape[2]
    width = min(2, pieces) * head_cols
    groups = pieces * head_cols // width
    return [
        ((count, in_proj.shape[2]), jnp.float32),
        ((groups, width // HS * count, width), jnp.bfloat16),
    ]


def make_queries(count, rows, in_proj, attn_gain, query_pieces):
    results = query_shapes(count, in_proj, query_pieces)
    return on_chip(
        functools.partial(queries_kernel, len(query_pieces)),
        "queries",
        [rows, in_proj, attn_gain, *query_pieces],
        results,
        2 * in_proj.shape[2] * math.prod(results[1][0]),
    )


def attend_rows(cfg, place, maps_ref, query_ref, source_ref, carry):
    count, features, size = cfg["count"], cfg["features"], cfg["chunk"]
    side = side_of()
    groups, _, group_cols = query_ref.shape
    channels = source_ref.shape[2]
    heads = group_cols // HS
    total_cols = groups * group_cols
    token = lax.broadcasted_iota(jnp.int32, (count, 1), 0)
    first_token = lax.axis_index("seq") * (2 * count) + side * count
    query_place = first_token + jnp.concatenate([token] * heads, axis=0)
    offset = (side if place == 0 else 1 - side) * count
    lane = lax.broadcasted_iota(jnp.int32, (1, size), 1)

    def one_chunk(start, carry):
        source = source_ref[pl.ds(start // count, size // count), :count, :]
        source = source.reshape(size, channels)
        twice = jnp.concatenate([source, source], axis=1)
        member = ((lane + start).astype(jnp.float32) + 0.5) * (1.0 / count)
        key_place = lane + start + member.astype(jnp.int32) * count + offset
        allowed = key_place <= query_place if cfg["layer"] == 0 else key_place >= query_place
        tail = dot_nt(maps_ref[2 * total_cols :, :], twice)
        square = jnp.sum(tail[:channels] * tail[channels:], axis=0, keepdims=True)
        scale = lax.rsqrt(jnp.maximum(square, 0.0) * (1.0 / features) + epsilon)
        scale_sq = scale * scale
        result = []
        for g in range(groups):
            low = g * group_cols
            key = dot_nt(maps_ref[low : low + group_cols, :], twice)
            value = dot_nt(maps_ref[total_cols + low : total_cols + low + group_cols, :], twice)
            keys = []
            for h in range(heads):
                one = key[h * HS : (h + 1) * HS]
                mean = jnp.sum(one * one, axis=0, keepdims=True) * (1.0 / HS)
                factor = scale * lax.rsqrt(mean * scale_sq + epsilon)
                keys.append((one * factor).astype(jnp.bfloat16))
            value = (value * scale).astype(jnp.bfloat16)
            scores = dot(query_ref[g], jnp.concatenate(keys, axis=0)) * (score_scale / HS)
            weights = jnp.where(allowed, jnp.exp(scores), 0.0)
            product = dot_nt(weights.astype(jnp.bfloat16), value)
            total = weights[:, :128]
            for at in range(128, size, 128):
                total = total + weights[:, at : at + 128]
            result.append(
                (product, total)
                if carry is None
                else (carry[g][0] + product, carry[g][1] + total)
            )
        return tuple(result)

    chunks = source_ref.shape[0] * count // size
    carry = one_chunk(0, carry)
    if chunks <= 4:
        for c in range(1, chunks):
            carry = one_chunk(c * size, carry)
    else:
        carry = lax.fori_loop(
            1, chunks, lambda c, now: one_chunk(c * size, now), carry
        )
    return carry


def first_half_kernel(cfg, maps_ref, query_ref, own_ref, number_ref, total_ref):
    carry = attend_rows(cfg, 0, maps_ref, query_ref, own_ref, None)
    for g, (number, total) in enumerate(carry):
        number_ref[g] = number
        total_ref[g] = total


def second_half_kernel(cfg, maps_ref, query_ref, other_ref, number_ref, total_ref, hidden_ref, gain_ref, latent_ref, *refs):
    layer, pieces, last, count = cfg["layer"], cfg["pieces"], cfg["last"], cfg["count"]
    refs = list(refs)
    mix_refs = [refs.pop(0) for _ in range(pieces)]
    param_refs = [refs.pop(0) for _ in range(pieces)]
    side, way, member = side_of(), lax.axis_index("head"), lax.axis_index("seq")
    members = other_ref.shape[0]
    features, channels = hidden_ref.shape[1], latent_ref.shape[1]
    groups, _, group_cols = query_ref.shape
    heads = group_cols // HS
    carry = tuple((number_ref[g], total_ref[g]) for g in range(groups))
    carry = attend_rows(cfg, 1, maps_ref, query_ref, other_ref, carry)

    mixture = hidden_ref[...]
    head = lax.broadcasted_iota(jnp.int32, (count, group_cols), 1) // HS
    for g, (number, total) in enumerate(carry):
        total = jnp.sum(total, axis=1, keepdims=True) + (0.0 if last else 1.0)
        share_of = 1.0 / total
        attended = jnp.zeros((count, group_cols), jnp.float32)
        for h in range(heads):
            band = slice(h * count, (h + 1) * count)
            attended = jnp.where(head == h, number[band] * share_of[band], attended)
        rows = cat([ref[layer] for ref in mix_refs[2 * g : 2 * g + 2]], 0)
        mixture = mixture + dot(attended.astype(jnp.bfloat16), rows)
    spread = lax.rsqrt(jnp.mean(mixture * mixture, axis=1, keepdims=True) + epsilon)
    scaled = (mixture * spread * gain_ref[layer : layer + 1, :]).astype(jnp.bfloat16)
    share = features // pieces
    param_all = refs[-1]
    for j, ref in enumerate(param_refs):
        at = pl.multiple_of(lax.rem(way + j, pieces) * share, 16)
        param_all[pl.ds(at, share), :] = ref[layer]
    predicted = dot(scaled, param_all[...])
    shift_mu = predicted[:, :channels]
    log_scale = 2.0 * jnp.tanh(0.5 * predicted[:, channels:])
    token = lax.broadcasted_iota(jnp.int32, (count, 1), 0)
    start = pl.multiple_of(side * count, 8)
    if last:
        held_ref, held_log_ref, out_ref = refs[:3]
        before = member - 1 + side
        edge = other_ref[jnp.maximum(before, 0), count:, :].astype(jnp.float32)
        edge = jnp.where(before >= 0, edge[0:2] + edge[2:4] + edge[4:6], 0.0)
        edge_log = edge[1:2]
        first = (latent_ref[pl.ds(start, 8), :][:1] - edge[0:1]) * jnp.exp(-edge_log)
        values = jnp.where(token == 0, first, pltpu.roll(held_ref[...], 1, 0))
        first_log = jnp.where(token == 0, edge_log, pltpu.roll(held_log_ref[...], 1, 0))
        result = (values - shift_mu) * jnp.exp(-log_scale)
        term = -(first_log + log_scale) - 0.5 * (result * result)
        loglik = jnp.sum(term.T, axis=0, keepdims=True) * (1.0 / channels) - 0.5 * math.log(
            2.0 * math.pi
        )
        out_ref[:count, :] = result
        out_ref[count:, :count] = jnp.broadcast_to(loglik, (8, count))
    else:
        in_ref, attn_gain_ref = refs[:2]
        query_refs = refs[2 : 2 + pieces]
        held_ref, held_log_ref, spread_ref, hidden_out_ref, query_out_ref = refs[2 + pieces : 7 + pieces]
        following = jnp.minimum(member + 1, members - 1)
        after = other_ref[following, :16, :].astype(jnp.float32)[:1]
        after = jnp.where(side == 0, latent_ref[count : count + 1, :], after)
        values = pltpu.roll(latent_ref[pl.ds(start, count), :], count - 1, 0)
        values = jnp.where(token == count - 1, after, values)
        result = (values - shift_mu) * jnp.exp(-log_scale)
        beyond = (member * 2 + side) * count + token == members * 2 * count - 1
        result = jnp.where(beyond, 0.0, result)
        held_ref[...] = result
        held_log_ref[...] = log_scale
        narrow = result.astype(jnp.bfloat16)
        edge = jnp.concatenate([shift_mu[count - 1 :], log_scale[count - 1 :]], axis=0)
        terms = []
        for _ in range(3):
            terms.append(edge.astype(jnp.bfloat16).astype(jnp.float32))
            edge = edge - terms[-1]
        rest = jnp.zeros((16 - 6, channels), jnp.float32)
        edge = jnp.concatenate(terms + [rest], axis=0).astype(jnp.bfloat16)
        for i in range(members):
            spread_ref[i, :count, :] = narrow
            spread_ref[i, count:, :] = edge
        store_queries(1, narrow, in_ref, attn_gain_ref, query_refs, hidden_out_ref, query_out_ref)


def config(layer, count, features, pieces, members):
    per_chunk = next(size for size in (8, 4, 2, 1) if members % size == 0)
    return {
        "layer": layer,
        "last": layer == 1,
        "count": count,
        "features": features,
        "pieces": pieces,
        "chunk": per_chunk * count,
    }


def first_half(cfg, maps, queries, own):
    groups, rows, cols = queries.shape
    return on_chip(
        functools.partial(first_half_kernel, cfg),
        "first_half",
        [maps, queries, own],
        [((groups, rows, cols), jnp.float32), ((groups, rows, 128), jnp.float32)],
        2 * own.shape[0] * cfg["count"] * (maps.size + 2 * queries.size),
    )


def second_half(cfg, maps, queries, other, sums, hidden, param_gain, latents, mix_pieces, param_pieces, extra):
    count, channels = cfg["count"], latents.shape[1]
    operands = [maps, queries, other, *sums, hidden, param_gain, latents]
    operands += [*mix_pieces, *param_pieces, *extra]
    if cfg["last"]:
        results = [((count + 8, channels), jnp.float32)]
    else:
        results = [
            ((count, channels), jnp.float32),
            ((count, channels), jnp.float32),
            ((other.shape[0], count + 16, channels), jnp.bfloat16),
            *query_shapes(count, extra[0], extra[2:]),
        ]
    return on_chip(
        functools.partial(second_half_kernel, cfg),
        "second_half",
        operands,
        results,
        2 * other.shape[0] * count * (maps.size + 2 * queries.size),
        scratch=[pltpu.VMEM((cfg["features"], param_pieces[0].shape[2]), jnp.bfloat16)],
    )


def finish_kernel(own_ref, other_ref, final_ref, loglik_ref):
    count = final_ref.shape[0] // 2
    side = side_of()
    for ref, place in ((own_ref, side), (other_ref, 1 - side)):
        final_ref[pl.ds(pl.multiple_of(place * count, 8), count), :] = ref[:count, :]
    first = jnp.where(side == 0, own_ref[count : count + 1, :], other_ref[count : count + 1, :])
    second = jnp.where(side == 0, other_ref[count : count + 1, :], own_ref[count : count + 1, :])
    loglik_ref[...] = jnp.concatenate([first[:, :count], second[:, :count]], axis=1)


def body(
    latents, in_proj, query_proj, key_proj, value_proj, mix_proj, param_proj, attn_gain, param_gain
):
    members, ways = lax.axis_size("seq"), lax.axis_size("head")
    rows, channels = latents.shape
    features = in_proj.shape[2]
    count = rows // 2
    keys = members * count

    def swap(array):
        return lax.ppermute(array, "head", [(i, i ^ 1) for i in range(ways)])

    def pieces_of(array):
        shares = [array]
        for j in range(1, ways):
            shares.append(
                lax.ppermute(array, "head", [((i + j) % ways, i) for i in range(ways)])
            )
        return shares

    def gather(spread):
        return lax.all_to_all(spread, "seq", 0, 0)

    (spread,) = on_chip(
        spread_kernel,
        "spread_rows",
        [latents],
        [((members, count, channels), jnp.bfloat16)],
        keys * channels,
    )
    own = gather(spread)
    key_pieces, value_pieces = pieces_of(key_proj), pieces_of(value_proj)
    query_pieces, mix_pieces = pieces_of(query_proj), pieces_of(mix_proj)
    param_pieces = pieces_of(param_proj)
    maps = [combine(b, in_proj, attn_gain, key_pieces, value_pieces) for b in range(2)]
    hidden, queries = make_queries(count, latents, in_proj, attn_gain, query_pieces)
    own = gate(own, *maps, queries)

    cfg = config(0, count, features, ways, members)
    other = swap(own)
    sums = first_half(cfg, maps[0], queries, own)
    shared = (param_gain, latents, mix_pieces, param_pieces)
    held, held_log, spread, hidden, queries = second_half(
        cfg, maps[0], queries, other, sums, hidden, *shared, (in_proj, attn_gain, *query_pieces)
    )
    own = gather(spread)
    cfg = config(1, count, features, ways, members)
    other = swap(own)
    sums = first_half(cfg, maps[1], queries, own)
    (packed,) = second_half(
        cfg, maps[1], queries, other, sums, hidden, *shared, (held, held_log)
    )
    final_latent, token_loglik = on_chip(
        finish_kernel,
        "finish",
        [packed, swap(packed)],
        [((rows, channels), jnp.float32), ((1, rows), jnp.float32)],
        rows * channels,
        out_memory=None,
    )
    return (final_latent, token_loglik.reshape(rows))


def solution(mesh):
    placed = (
        P("seq", None),
        P(),
        P(None, None, "head"),
        P(None, None, "head"),
        P(None, None, "head"),
        P(None, "head", None),
        P(None, "head", None),
        P(),
        P(),
    )
    return jax.shard_map(
        body, mesh=mesh, in_specs=placed, out_specs=(P("seq", None), P("seq")), check_vma=False
    )
```

```python
import functools
import math

import jax
import jax.numpy as jnp
from jax import lax
from jax.experimental import pallas as pl
from jax.experimental.pallas import tpu as pltpu
from jax.sharding import PartitionSpec as P

HS = 64

score_scale = 8.0
epsilon = 1e-06

VMEM_LIMIT = 20 * 1024 * 1024


def dot(a, b):
    return jnp.dot(a, b, preferred_element_type=jnp.float32)


def dot_nt(a, b):
    return lax.dot_general(a, b, (((1,), (1,)), ((), ())), preferred_element_type=jnp.float32)


def cat(parts, axis):
    return parts[0] if len(parts) == 1 else jnp.concatenate(parts, axis=axis)


def side_of():
    return lax.rem(lax.axis_index("head"), 2)


def on_chip(kernel, name, operands, results, flops, out_memory=pltpu.VMEM, scratch=()):
    near = [pltpu.with_memory_space_constraint(array, pltpu.VMEM) for array in operands]
    if out_memory is pltpu.VMEM:
        out_shape = tuple(pltpu.VMEM(shape, dtype) for shape, dtype in results)
    else:
        out_shape = tuple(jax.ShapeDtypeStruct(shape, dtype) for shape, dtype in results)
    return pl.pallas_call(
        kernel,
        in_specs=[pl.BlockSpec(memory_space=pltpu.VMEM)] * len(operands),
        out_specs=tuple(pl.BlockSpec(memory_space=pltpu.VMEM) for _ in results),
        out_shape=out_shape,
        scratch_shapes=list(scratch),
        compiler_params=pltpu.CompilerParams(vmem_limit_bytes=VMEM_LIMIT),

        name=name,
    )(*near)


def narrow_kernel(rows_ref, own_ref):
    count = own_ref.shape[0]
    own_ref[...] = rows_ref[pl.ds(pl.multiple_of(side_of() * count, 8), count), :].astype(
        jnp.bfloat16
    )


def arrange_kernel(planes, *refs):
    place = lax.axis_index("seq") // (lax.axis_size("seq") // planes)
    for step in range(planes):
        refs[-1][place ^ step] = refs[step][...]


def gates_kernel(many, *refs):
    for source, target in zip(refs[:many], refs[-many:]):
        target[...] = source[...]


def gate_all(rows, made):
    return on_chip(
        functools.partial(gates_kernel, len(rows)),
        "gate",
        [*rows, *made],
        [(piece.shape, piece.dtype) for piece in rows],
        0,
    )


def turned(step, bits):
    return sum(((step >> b) & 1) << (bits - 1 - b) for b in range(bits))


def chip_of(step, per_plane, other):
    bits = per_plane.bit_length() - 1
    side = side_of()
    first = side == (1 if other else 0)
    return (lax.axis_index("seq") % per_plane) ^ jnp.where(first, step, turned(step, bits))


def combine_kernel(layer, pieces, in_ref, gain_ref, *refs):
    key_refs, value_refs, out_ref = refs[:pieces], refs[pieces : 2 * pieces], refs[2 * pieces]
    base = in_ref[layer]
    channels = base.shape[0]

    def store(row, value):
        high = value.astype(jnp.bfloat16)
        rows = value.shape[0]
        out_ref[row : row + rows, :channels] = high
        out_ref[row : row + rows, channels:] = (value - high.astype(jnp.float32)).astype(
            jnp.bfloat16
        )
        return row + rows

    scaled = base.astype(jnp.float32) * gain_ref[layer : layer + 1, :]
    high = scaled.astype(jnp.bfloat16)
    low = (scaled - high.astype(jnp.float32)).astype(jnp.bfloat16)
    both = jnp.concatenate([high, low], axis=0)
    row = 0
    for group in (key_refs, value_refs):
        for first in range(0, pieces, 2):
            columns = cat([ref[layer] for ref in group[first : first + 2]], 1)
            product = dot(both, columns)
            row = store(row, (product[:channels] + product[channels:]).T)
    row = store(row, dot_nt(base, base))
    eye = lax.broadcasted_iota(jnp.int32, (channels, channels), 0) == lax.broadcasted_iota(
        jnp.int32, (channels, channels), 1
    )
    store(row, jnp.where(eye, 1.0, 0.0))


def combine(layer, in_proj, attn_gain, key_pieces, value_pieces):
    pieces = len(key_pieces)
    _, channels, features = in_proj.shape
    rows = 2 * pieces * key_pieces[0].shape[2] + 2 * channels
    return on_chip(
        functools.partial(combine_kernel, layer, pieces),
        "combine",
        [in_proj, attn_gain, *key_pieces, *value_pieces],
        [((rows, 2 * channels), jnp.bfloat16)],
        4 * channels * features * rows,
    )[0]


def store_queries(layer, rows, in_ref, gain_ref, query_refs, hidden_ref, out_ref):
    count = hidden_ref.shape[0]
    hidden = dot(rows, in_ref[layer])
    hidden_ref[...] = hidden
    spread = lax.rsqrt(jnp.mean(hidden * hidden, axis=1, keepdims=True) + epsilon)
    normed = (hidden * spread * gain_ref[layer : layer + 1, :]).astype(jnp.bfloat16)
    for first in range(0, len(query_refs), 2):
        query = dot(normed, cat([ref[layer] for ref in query_refs[first : first + 2]], 1))
        width = query.shape[1]
        head = lax.broadcasted_iota(jnp.int32, (count, width), 1) // HS
        for h in range(width // HS):
            band = jnp.where(head == h, query, 0.0)
            mean = jnp.sum(band * band, axis=1, keepdims=True) * (1.0 / HS)
            out_ref[first // 2, h * count : (h + 1) * count, :] = (
                band * lax.rsqrt(mean + epsilon)
            ).astype(jnp.bfloat16)


def queries_kernel(layer, pieces, rows_ref, in_ref, gain_ref, *refs):
    rows = rows_ref[: refs[pieces].shape[0], :]
    store_queries(layer, rows, in_ref, gain_ref, refs[:pieces], refs[pieces], refs[pieces + 1])


def query_shapes(count, in_proj, query_pieces):
    pieces, head_cols = len(query_pieces), query_pieces[0].shape[2]
    width = min(2, pieces) * head_cols
    groups = pieces * head_cols // width
    return [
        ((count, in_proj.shape[2]), jnp.float32),
        ((groups, width // HS * count, width), jnp.bfloat16),
    ]


def make_queries(layer, count, rows, in_proj, attn_gain, query_pieces):
    results = query_shapes(count, in_proj, query_pieces)
    return on_chip(
        functools.partial(queries_kernel, layer, len(query_pieces)),
        "queries",
        [rows, in_proj, attn_gain, *query_pieces],
        results,
        2 * in_proj.shape[2] * math.prod(results[1][0]),
    )


def attend_rows(cfg, maps_ref, query_ref, pieces, carry):
    count, features, planes, per_plane = cfg["count"], cfg["features"], cfg["planes"], cfg["per_plane"]
    side = side_of()
    groups, _, group_cols = query_ref.shape
    heads = group_cols // HS
    total_cols = groups * group_cols
    size = planes * count
    token = lax.broadcasted_iota(jnp.int32, (count, 1), 0)
    first_token = lax.axis_index("seq") * (2 * count) + side * count
    query_place = first_token + jnp.concatenate([token] * heads, axis=0)
    lane = lax.broadcasted_iota(jnp.int32, (1, size), 1)
    plane = ((lane.astype(jnp.float32) + 0.5) * (1.0 / count)).astype(jnp.int32)
    base_place = lane + plane * (2 * per_plane * count - count)

    def one_chunk(some, carry):
        sources, places = [], []
        for rows, step, other in some:
            rows = rows[:, :count, :].reshape(size, rows.shape[2])
            sources.append(jnp.concatenate([rows, rows], axis=1))
            offset = chip_of(step, per_plane, other) * 2 + (1 - side if other else side)
            places.append(base_place + offset * count)
        twice, key_place = cat(sources, 0), cat(places, 1)
        channels = twice.shape[1] // 2
        allowed = key_place <= query_place if cfg["layer"] == 0 else key_place >= query_place
        tail = dot_nt(maps_ref[2 * total_cols :, :], twice)
        square = jnp.sum(tail[:channels] * tail[channels:], axis=0, keepdims=True)
        scale = lax.rsqrt(jnp.maximum(square, 0.0) * (1.0 / features) + epsilon)
        scale_sq = scale * scale
        result = []
        for g in range(groups):
            low = g * group_cols
            key = dot_nt(maps_ref[low : low + group_cols, :], twice)
            value = dot_nt(maps_ref[total_cols + low : total_cols + low + group_cols, :], twice)
            keys = []
            for h in range(heads):
                one = key[h * HS : (h + 1) * HS]
                mean = jnp.sum(one * one, axis=0, keepdims=True) * (1.0 / HS)
                factor = scale * lax.rsqrt(mean * scale_sq + epsilon)
                keys.append((one * factor).astype(jnp.bfloat16))
            value = (value * scale).astype(jnp.bfloat16)
            scores = dot(query_ref[g], jnp.concatenate(keys, axis=0)) * (score_scale / HS)
            weights = jnp.where(allowed, jnp.exp(scores), 0.0)
            product = dot_nt(weights.astype(jnp.bfloat16), value)
            total = weights[:, :128]
            for at in range(128, weights.shape[1], 128):
                total = total + weights[:, at : at + 128]
            result.append(
                (product, total)
                if carry is None
                else (carry[g][0] + product, carry[g][1] + total)
            )
        return tuple(result)

    if len(pieces) <= 4:
        for at in range(0, len(pieces), 2):
            some = [(ref[...], step, other) for ref, step, other in pieces[at : at + 2]]
            carry = one_chunk(some, carry)
        return carry
    held, (_, first, other) = cfg["held"], pieces[0]
    for at, (ref, _, _) in enumerate(pieces):
        held[at] = ref[...]
    if carry is None:
        carry = tuple(
            (
                jnp.zeros((heads * count, group_cols), jnp.float32),
                jnp.zeros((heads * count, 128), jnp.float32),
            )
            for _ in range(groups)
        )
    return lax.fori_loop(
        0, len(pieces), lambda at, now: one_chunk([(held[at], first + at, other)], now), carry
    )


def partial_kernel(cfg, kinds, resume, maps_ref, query_ref, *refs):
    refs = list(refs)
    pieces = [(refs.pop(0), step, other) for step, other in kinds]
    carry = None
    if resume:
        number_in, total_in = refs.pop(0), refs.pop(0)
        carry = tuple((number_in[g], total_in[g]) for g in range(query_ref.shape[0]))
    number_ref, total_ref = refs[:2]
    cfg = dict(cfg, held=refs[2] if len(refs) > 2 else None)
    carry = attend_rows(cfg, maps_ref, query_ref, pieces, carry)
    for g, (number, total) in enumerate(carry):
        number_ref[g] = number
        total_ref[g] = total


def chosen_rows(others, per_plane, place, rows):
    plane, chip = place // per_plane, place % per_plane
    result = None
    for step, ref in enumerate(others):
        value = ref[plane, rows, :].astype(jnp.float32)
        here = chip_of(step, per_plane, True) == chip
        result = value if result is None else jnp.where(here, value, result)
    return result


def second_half_kernel(cfg, kinds, maps_ref, query_ref, number_ref, total_ref, hidden_ref, gain_ref, latent_ref, *refs):
    layer, pieces, last, count = cfg["layer"], cfg["pieces"], cfg["last"], cfg["count"]
    per_plane = cfg["per_plane"]
    refs = list(refs)
    others = [refs.pop(0) for _ in range(per_plane)]
    mix_refs = [refs.pop(0) for _ in range(pieces)]
    param_refs = [refs.pop(0) for _ in range(pieces)]
    param_all = refs.pop(3)
    cfg = dict(cfg, held=refs[-1])
    side, way, member = side_of(), lax.axis_index("head"), lax.axis_index("seq")
    members = cfg["planes"] * per_plane
    features, channels = hidden_ref.shape[1], latent_ref.shape[1]
    groups, _, group_cols = query_ref.shape
    heads = group_cols // HS
    carry = tuple((number_ref[g], total_ref[g]) for g in range(groups))
    carry = attend_rows(
        cfg, maps_ref, query_ref, [(others[step], step, True) for step in kinds], carry
    )

    mixture = hidden_ref[...]
    head = lax.broadcasted_iota(jnp.int32, (count, group_cols), 1) // HS
    for g, (number, total) in enumerate(carry):
        total = jnp.sum(total, axis=1, keepdims=True) + (0.0 if last else 1.0)
        share_of = 1.0 / total
        attended = jnp.zeros((count, group_cols), jnp.float32)
        for h in range(heads):
            band = slice(h * count, (h + 1) * count)
            attended = jnp.where(head == h, number[band] * share_of[band], attended)
        rows = cat([ref[layer] for ref in mix_refs[2 * g : 2 * g + 2]], 0)
        mixture = mixture + dot(attended.astype(jnp.bfloat16), rows)
    spread = lax.rsqrt(jnp.mean(mixture * mixture, axis=1, keepdims=True) + epsilon)
    scaled = (mixture * spread * gain_ref[layer : layer + 1, :]).astype(jnp.bfloat16)
    share = features // pieces
    for j, ref in enumerate(param_refs):
        at = pl.multiple_of(lax.rem(way + j, pieces) * share, 16)
        param_all[pl.ds(at, share), :] = ref[layer]
    predicted = dot(scaled, param_all[...])
    shift_mu = predicted[:, :channels]
    log_scale = 2.0 * jnp.tanh(0.5 * predicted[:, channels:])
    token = lax.broadcasted_iota(jnp.int32, (count, 1), 0)
    start = pl.multiple_of(side * count, 8)
    if last:
        held_ref, held_log_ref, out_ref = refs[:3]
        before = member - 1 + side
        edge = chosen_rows(others, per_plane, jnp.maximum(before, 0), slice(count, count + 16))
        edge = jnp.where(before >= 0, edge[0:2] + edge[2:4] + edge[4:6], 0.0)
        edge_log = edge[1:2]
        first = (latent_ref[pl.ds(start, 8), :][:1] - edge[0:1]) * jnp.exp(-edge_log)
        values = jnp.where(token == 0, first, pltpu.roll(held_ref[...], 1, 0))
        first_log = jnp.where(token == 0, edge_log, pltpu.roll(held_log_ref[...], 1, 0))
        result = (values - shift_mu) * jnp.exp(-log_scale)
        term = -(first_log + log_scale) - 0.5 * (result * result)
        loglik = jnp.sum(term.T, axis=0, keepdims=True) * (1.0 / channels) - 0.5 * math.log(
            2.0 * math.pi
        )
        out_ref[:count, :] = result
        out_ref[count:, :count] = jnp.broadcast_to(loglik, (8, count))
    else:
        held_ref, held_log_ref, narrow_ref = refs[:3]
        following = jnp.minimum(member + 1, members - 1)
        after = chosen_rows(others, per_plane, following, slice(0, 16))[:1]
        after = jnp.where(side == 0, latent_ref[count : count + 1, :], after)
        values = pltpu.roll(latent_ref[pl.ds(start, count), :], count - 1, 0)
        values = jnp.where(token == count - 1, after, values)
        result = (values - shift_mu) * jnp.exp(-log_scale)
        beyond = (member * 2 + side) * count + token == members * 2 * count - 1
        result = jnp.where(beyond, 0.0, result)
        held_ref[...] = result
        held_log_ref[...] = log_scale
        narrow = result.astype(jnp.bfloat16)
        edge = jnp.concatenate([shift_mu[count - 1 :], log_scale[count - 1 :]], axis=0)
        terms = []
        for _ in range(3):
            terms.append(edge.astype(jnp.bfloat16).astype(jnp.float32))
            edge = edge - terms[-1]
        rest = jnp.zeros((16 - 6, channels), jnp.float32)
        edge = jnp.concatenate(terms + [rest], axis=0).astype(jnp.bfloat16)
        narrow_ref[:count, :] = narrow
        narrow_ref[count:, :] = edge


def config(layer, count, features, pieces, planes, per_plane):
    return {
        "layer": layer,
        "last": layer == 1,
        "count": count,
        "features": features,
        "pieces": pieces,
        "planes": planes,
        "per_plane": per_plane,
    }


def attend_flops(kinds, piece, maps, queries):
    return 2 * len(kinds) * piece.shape[0] * piece.shape[1] * (maps.size + 2 * queries.size)


def held_pieces(kinds, piece):
    return [pltpu.VMEM((len(kinds), *piece.shape), piece.dtype)] if len(kinds) > 4 else []


def attend(cfg, maps, queries, pieces, sums=()):
    groups, rows, cols = queries.shape
    kinds = tuple((step, other) for _, step, other in pieces)
    return on_chip(
        functools.partial(partial_kernel, cfg, kinds, len(sums) > 0),
        "attend",
        [maps, queries, *[piece for piece, _, _ in pieces], *sums],
        [((groups, rows, cols), jnp.float32), ((groups, rows, 128), jnp.float32)],
        attend_flops(kinds, pieces[0][0], maps, queries),
        scratch=held_pieces(kinds, pieces[0][0]),
    )


def second_half(cfg, kinds, maps, queries, sums, hidden, param_gain, latents, others, mix_pieces, param_pieces, held=()):
    count, channels = cfg["count"], latents.shape[1]
    operands = [maps, queries, *sums, hidden, param_gain, latents]
    operands += [*others, *mix_pieces, *param_pieces, *held]
    if cfg["last"]:
        results = [((count + 8, channels), jnp.float32)]
    else:
        results = [
            ((count, channels), jnp.float32),
            ((count, channels), jnp.float32),
            ((count + 16, channels), jnp.bfloat16),
        ]
    if cfg["last"]:
        assert len(held) == 2
    return on_chip(
        functools.partial(second_half_kernel, cfg, kinds),
        "second_half",
        operands,
        results,
        attend_flops(kinds, others[0], maps, queries),
        scratch=[pltpu.VMEM((cfg["features"], param_pieces[0].shape[2]), jnp.bfloat16)]
        + held_pieces(kinds, others[0]),
    )


def finish_kernel(own_ref, other_ref, final_ref, loglik_ref):
    count = final_ref.shape[0] // 2
    side = side_of()
    for ref, place in ((own_ref, side), (other_ref, 1 - side)):
        final_ref[pl.ds(pl.multiple_of(place * count, 8), count), :] = ref[:count, :]
    first = jnp.where(side == 0, own_ref[count : count + 1, :], other_ref[count : count + 1, :])
    second = jnp.where(side == 0, other_ref[count : count + 1, :], own_ref[count : count + 1, :])
    loglik_ref[...] = jnp.concatenate([first[:, :count], second[:, :count]], axis=1)


def body(
    latents, in_proj, query_proj, key_proj, value_proj, mix_proj, param_proj, attn_gain, param_gain
):
    members, ways = lax.axis_size("seq"), lax.axis_size("head")
    rows, channels = latents.shape
    features = in_proj.shape[2]
    count = rows // 2

    def swap(array):
        return lax.ppermute(array, "head", [(i, i ^ 1) for i in range(ways)])

    def pieces_of(array):
        shares = [array]
        for j in range(1, ways):
            shares.append(
                lax.ppermute(array, "head", [((i + j) % ways, i) for i in range(ways)])
            )
        return shares

    planes = 4 if members % 4 == 0 else 1
    per_plane = members // planes
    bits = per_plane.bit_length() - 1

    def gather(own, *made):
        parts = [own] + [
            lax.ppermute(own, "seq", [(i, i ^ (b * per_plane)) for i in range(members)])
            for b in range(1, planes)
        ]
        (mine,) = on_chip(
            functools.partial(arrange_kernel, planes),
            "arrange",
            parts + list(made),
            [((planes, *own.shape), own.dtype)],
            planes * own.size,
        )
        arrived = [mine]
        for step in range(1, per_plane):
            pairs = []
            for i in range(members):
                for w in range(ways):
                    to = i ^ (turned(step, bits) if w % 2 else step)
                    pairs.append((i * ways + w, to * ways + w))
            arrived.append(lax.ppermute(mine, ("seq", "head"), pairs))
        return arrived

    def run(layer, own, maps, made, *rest):
        cfg = config(layer, count, features, ways, planes, per_plane)
        hidden, queries = made
        mine = gather(own, maps, *made)
        others = [swap(mine[0])]
        sums = attend(cfg, maps, queries, [(mine[0], 0, False), (others[0], 0, True)])
        if per_plane <= 4:
            rows = gate_all(mine[1:], sums)
            others += [swap(piece) for piece in rows]
            batch = [(piece, step + 1, False) for step, piece in enumerate(rows)]
            sums = attend(cfg, maps, queries, batch, sums)
            kinds = tuple(range(1, per_plane))
        else:
            others += [swap(rows) for rows in mine[1:]]
            batch = [(mine[step], step, False) for step in range(1, per_plane)]
            sums = attend(cfg, maps, queries, batch, sums)
            kinds = tuple(range(1, per_plane))
        return second_half(
            cfg, kinds, maps, queries, sums, hidden, param_gain, latents, others, mix_pieces, param_pieces, *rest
        )

    (own,) = on_chip(
        narrow_kernel, "narrow", [latents], [((count, channels), jnp.bfloat16)], count * channels
    )
    key_pieces, value_pieces = pieces_of(key_proj), pieces_of(value_proj)
    query_pieces, mix_pieces = pieces_of(query_proj), pieces_of(mix_proj)
    param_pieces = pieces_of(param_proj)
    maps = [combine(b, in_proj, attn_gain, key_pieces, value_pieces) for b in range(2)]
    made = make_queries(0, count, own, in_proj, attn_gain, query_pieces)
    held, held_log, own = run(0, own, maps[0], made)
    made = make_queries(1, count, own, in_proj, attn_gain, query_pieces)
    (packed,) = run(1, own, maps[1], made, (held, held_log))
    final_latent, token_loglik = on_chip(
        finish_kernel,
        "finish",
        [packed, swap(packed)],
        [((rows, channels), jnp.float32), ((1, rows), jnp.float32)],
        rows * channels,
        out_memory=None,
    )
    return (final_latent, token_loglik.reshape(rows))


def solution(mesh):
    placed = (
        P("seq", None),
        P(),
        P(None, None, "head"),
        P(None, None, "head"),
        P(None, None, "head"),
        P(None, "head", None),
        P(None, "head", None),
        P(),
        P(),
    )
    return jax.shard_map(
        body, mesh=mesh, in_specs=placed, out_specs=(P("seq", None), P("seq")), check_vma=False
    )
```

```python
import functools
import math

import jax
import jax.numpy as jnp
from jax import lax
from jax.experimental import pallas as pl
from jax.experimental.pallas import tpu as pltpu
from jax.sharding import PartitionSpec as P

HS = 64

score_scale = 8.0
epsilon = 1e-06

VMEM_LIMIT = 32 * 1024 * 1024


def dot(a, b):
    return jnp.dot(a, b, preferred_element_type=jnp.float32)


def dot_nt(a, b):
    return lax.dot_general(a, b, (((1,), (1,)), ((), ())), preferred_element_type=jnp.float32)


def cat(parts, axis):
    return parts[0] if len(parts) == 1 else jnp.concatenate(parts, axis=axis)


def side_of():
    return lax.rem(lax.axis_index("head"), 2)


def on_chip(kernel, name, operands, results, far=(), scratch=(), out_memory=pltpu.VMEM):
    near = [pltpu.with_memory_space_constraint(array, pltpu.VMEM) for array in operands]
    far = [pltpu.with_memory_space_constraint(array, pltpu.HBM) for array in far]
    if out_memory is pltpu.VMEM:
        out_shape = tuple(pltpu.VMEM(shape, dtype) for shape, dtype in results)
    else:
        out_shape = tuple(jax.ShapeDtypeStruct(shape, dtype) for shape, dtype in results)
    return pl.pallas_call(
        kernel,
        in_specs=[pl.BlockSpec(memory_space=pltpu.VMEM)] * len(near)
        + [pl.BlockSpec(memory_space=pl.ANY)] * len(far),
        out_specs=tuple(pl.BlockSpec(memory_space=pltpu.VMEM) for _ in results),
        out_shape=out_shape,
        scratch_shapes=list(scratch),
        compiler_params=pltpu.CompilerParams(vmem_limit_bytes=VMEM_LIMIT),
        name=name,
    )(*near, *far)


def fetch(sources, targets, sems):
    copies = []
    for at, (source, target) in enumerate(zip(sources, targets)):
        copies.append(pltpu.make_async_copy(source, target, sems.at[at]))
        copies[-1].start()
    return copies


def half_kernel(rows_ref, own_ref, sems):
    count = own_ref.shape[0]
    half = rows_ref.at[pl.ds(pl.multiple_of(side_of() * count, 8), count)]
    for copy in fetch([half], [own_ref], sems):
        copy.wait()


def arrange_kernel(planes, *refs):
    place = lax.axis_index("seq") // (lax.axis_size("seq") // planes)
    for step in range(planes):
        rows = refs[step][...]
        refs[-2][place ^ step] = rows
        refs[-1][place ^ step] = rows.astype(jnp.bfloat16)


def gates_kernel(many, *refs):
    for source, target in zip(refs[:many], refs[-many:]):
        target[...] = source[...]


def gate_all(rows, made):
    results = [(piece.shape, piece.dtype) for piece in rows]
    return on_chip(functools.partial(gates_kernel, len(rows)), "gate", [*rows, *made], results)


def turned(step, bits):
    return sum(((step >> b) & 1) << (bits - 1 - b) for b in range(bits))


def chip_of(step, per_plane, other):
    bits = per_plane.bit_length() - 1
    first = side_of() == (1 if other else 0)
    return (lax.axis_index("seq") % per_plane) ^ jnp.where(first, step, turned(step, bits))


def prepare_kernel(pieces, in_src, gain_src, *refs):
    sources, refs = refs[: 3 * pieces], refs[3 * pieces :]
    maps_refs, (in_ref, gain_ref, query_ref, buffer, sems) = refs[:-5], refs[-5:]
    layers, channels, _ = in_ref.shape
    targets = [in_ref, gain_ref] + [buffer.at[at] for at in range(2 * pieces)]
    targets += [query_ref.at[at] for at in range(pieces)]
    copies = fetch([in_src, gain_src, *sources], targets, sems)
    for copy in copies[: 2 + 2 * pieces]:
        copy.wait()
    eye = lax.broadcasted_iota(jnp.int32, (channels, channels), 0) == lax.broadcasted_iota(
        jnp.int32, (channels, channels), 1
    )
    for layer in range(layers):
        out_ref = maps_refs[layer]

        def store(row, value, out_ref=out_ref):
            high = value.astype(jnp.bfloat16)
            rows = value.shape[0]
            out_ref[row : row + rows, :channels] = high
            out_ref[row : row + rows, channels:] = (value - high.astype(jnp.float32)).astype(
                jnp.bfloat16
            )
            return row + rows

        base = in_ref[layer]
        scaled = base.astype(jnp.float32) * gain_ref[layer : layer + 1, :]
        high = scaled.astype(jnp.bfloat16)
        low = (scaled - high.astype(jnp.float32)).astype(jnp.bfloat16)
        both = jnp.concatenate([high, low], axis=0)
        row = 0
        for first in range(0, 2 * pieces, 2):
            pair = cat([buffer[first, layer], buffer[first + 1, layer]], 1)
            product = dot(both, pair)
            row = store(row, (product[:channels] + product[channels:]).T)
        row = store(row, dot_nt(base, base))
        store(row, jnp.where(eye, 1.0, 0.0))
    for copy in copies[2 + 2 * pieces :]:
        copy.wait()


def prepare(in_proj, attn_gain, key_pieces, value_pieces, query_pieces):
    pieces = len(key_pieces)
    layers, channels, features = in_proj.shape
    columns = key_pieces[0].shape[2]
    rows = 2 * pieces * columns + 2 * channels
    *maps, in_all, gains, query_all = on_chip(
        functools.partial(prepare_kernel, pieces),
        "prepare",
        [],
        [((rows, 2 * channels), jnp.bfloat16)] * layers
        + [
            (in_proj.shape, in_proj.dtype),
            (attn_gain.shape, attn_gain.dtype),
            ((pieces, *query_pieces[0].shape), jnp.bfloat16),
        ],
        far=[in_proj, attn_gain, *key_pieces, *value_pieces, *query_pieces],
        scratch=[
            pltpu.VMEM((2 * pieces, layers, features, columns), jnp.bfloat16),
            pltpu.SemaphoreType.DMA((3 * pieces + 2,)),
        ],
    )
    return maps, (in_all, gains, query_all)


def queries_kernel(layer, planes, rows_ref, in_ref, gain_ref, query_ref, hidden_ref, out_ref):
    if planes == rows_ref.shape[0]:
        rows = rows_ref[...]
    else:
        count = hidden_ref.shape[0]
        place = lax.axis_index("seq") // (lax.axis_size("seq") // rows_ref.shape[0])
        rows = rows_ref[place, :count, :]
    rows = rows.reshape(hidden_ref.shape[0], rows_ref.shape[2])
    count = rows.shape[0] // planes
    hidden = dot(rows, in_ref[layer])
    hidden_ref[...] = hidden
    spread = lax.rsqrt(jnp.mean(hidden * hidden, axis=1, keepdims=True) + epsilon)
    normed = (hidden * spread * gain_ref[layer : layer + 1, :]).astype(jnp.bfloat16)
    for first in range(0, query_ref.shape[0], 2):
        query = dot(normed, cat([query_ref[at, layer] for at in range(first, first + 2)], 1))
        width = query.shape[1]
        heads = width // HS
        head = lax.broadcasted_iota(jnp.int32, (1, width), 1) // HS
        same = head == lax.broadcasted_iota(jnp.int32, (width, 1), 0) // HS
        same = jnp.where(same, 1.0, 0.0).astype(jnp.bfloat16)
        square = query * query
        high = square.astype(jnp.bfloat16)
        low = (square - high.astype(jnp.float32)).astype(jnp.bfloat16)
        mean = (dot(high, same) + dot(low, same)) * (1.0 / HS)
        query = query * lax.rsqrt(mean + epsilon)
        for h in range(heads):
            band = jnp.where(head == h, query, 0.0).astype(jnp.bfloat16)
            for p in range(planes):
                row = (p * heads + h) * count
                out_ref[first // 2, row : row + count, :] = band[p * count : (p + 1) * count]


def make_queries(layer, planes, count, rows, weights):
    in_all, _, query_all = weights
    width = 2 * query_all.shape[3]
    return on_chip(
        functools.partial(queries_kernel, layer, planes),
        "queries",
        [rows, *weights],
        [
            ((planes * count, in_all.shape[2]), jnp.float32),
            ((query_all.shape[0] // 2, planes * width // HS * count, width), jnp.bfloat16),
        ],
    )


def attend_some(cfg, maps_ref, query_ref, some, start, sums):
    count, features, planes, per_plane = cfg["count"], cfg["features"], cfg["planes"], cfg["per_plane"]
    layer, side = cfg["layer"], side_of()
    groups, _, group_cols = query_ref.shape
    heads = group_cols // HS
    band = heads * count
    total_cols = groups * group_cols
    stride = 2 * per_plane * count
    token = lax.broadcasted_iota(jnp.int32, (count, 1), 0)
    member = lax.axis_index("seq")
    query_place = (member % per_plane * 2 + side) * count + jnp.concatenate([token] * heads, axis=0)
    offsets = [
        (chip_of(step, per_plane, other) * 2 + (1 - side if other else side)) * count
        for _, step, other in some
    ]
    if layer == 0:
        size = len(some) * count
        lane = lax.broadcasted_iota(jnp.int32, (1, size), 1)
        key_place = lane + offsets[0]
        for at in range(1, len(some)):
            key_place = jnp.where(lane >= at * count, lane - at * count + offsets[at], key_place)
        allowed = key_place <= query_place
        parts = [cat([rows[p, :count, :] for rows, _, _ in some], 0) for p in range(planes)]
        low_rows = [p * band for p in range(planes)]
    else:
        size = len(some) * planes * count
        lane = lax.broadcasted_iota(jnp.int32, (1, planes * count), 1)
        plane = ((lane.astype(jnp.float32) + 0.5) * (1.0 / count)).astype(jnp.int32)
        base_place = lane + plane * (stride - count)
        key_place = jnp.concatenate([base_place + offset for offset in offsets], axis=1)
        allowed = key_place >= query_place + member // per_plane * stride
        rows = [rows[:, :count, :].reshape(planes * count, rows.shape[2]) for rows, _, _ in some]
        parts, low_rows = [cat(rows, 0)], [0]

    def keys_and_values(source, g):
        low = g * group_cols
        twice = jnp.concatenate([source, source], axis=1)
        channels = source.shape[1]
        tail = dot_nt(maps_ref[2 * total_cols :, :], twice)
        square = jnp.sum(tail[:channels] * tail[channels:], axis=0, keepdims=True)
        scale = lax.rsqrt(jnp.maximum(square, 0.0) * (1.0 / features) + epsilon)
        scale_sq = scale * scale
        key = dot_nt(maps_ref[low : low + group_cols, :], twice)
        value = dot_nt(maps_ref[total_cols + low : total_cols + low + group_cols, :], twice)
        keys = []
        for h in range(heads):
            one = key[h * HS : (h + 1) * HS]
            mean = jnp.sum(one * one, axis=0, keepdims=True) * (1.0 / HS)
            factor = scale * lax.rsqrt(mean * scale_sq + epsilon) * (score_scale / HS)
            keys.append((one * factor).astype(jnp.bfloat16))
        return jnp.concatenate(keys, axis=0), (value * scale).astype(jnp.bfloat16)

    for g in range(groups):
        if size % 128 == 0 and len(parts) > 1:
            key, value = keys_and_values(cat(parts, 0), g)
            made = [
                (key[:, p * size : (p + 1) * size], value[:, p * size : (p + 1) * size])
                for p in range(len(parts))
            ]
        else:
            made = [keys_and_values(part, g) for part in parts]
        for index, ((key, value), low_row) in enumerate(zip(made, low_rows)):
            scores = dot(query_ref[g, low_row:, :], key)
            weights = jnp.exp(scores)
            first = jnp.where(allowed, weights[:band], 0.0)
            weights = first if weights.shape[0] == band else cat([first, weights[band:]], 0)
            product = dot_nt(weights.astype(jnp.bfloat16), value)
            lanes = [weights[:, at : at + 128] for at in range(0, weights.shape[1], 128)]
            news = [product, sum(part for part in lanes if part.shape[1] == 128)]
            news += [part for part in lanes if part.shape[1] < 128]
            for at, (old_ref, new_ref) in enumerate(sums):
                if start and index == 0:
                    old = None if old_ref is None else old_ref[g]
                else:
                    old = new_ref[g, low_row:, :]
                if at < len(news):
                    new = news[at] if old is None else old + news[at]
                else:
                    new = jnp.zeros(new_ref.shape[1:], jnp.float32) if old is None else old
                if at < len(news) or (start and index == 0):
                    new_ref[g, low_row:, :] = new


def sum_shapes(cfg, queries):
    groups, rows, cols = queries.shape
    shapes = [(groups, rows, cols), (groups, rows, 128)]
    rest = 2 * cfg["count"] % 128
    return shapes + ([(groups, rows, rest)] if cfg["layer"] == 0 and rest else [])


def attend_kernel(cfg, kinds, resume, maps_ref, query_ref, *refs):
    refs = list(refs)
    pieces = [(refs.pop(0), step, other) for step, other in kinds]
    many = len(refs) // 2 if resume else len(refs)
    olds = refs[:many] if resume else [None] * many
    sums = list(zip(olds, refs[-many:]))
    some = [(ref[...], step, other) for ref, step, other in pieces]
    attend_some(cfg, maps_ref, query_ref, some, True, sums)


def attend(cfg, maps, queries, pieces, sums=()):
    kinds = tuple((step, other) for _, step, other in pieces)
    return on_chip(
        functools.partial(attend_kernel, cfg, kinds, len(sums) > 0),
        "attend",
        [maps, queries, *[piece for piece, _, _ in pieces], *sums],
        [(shape, jnp.float32) for shape in sum_shapes(cfg, queries)],
    )


def chosen_rows(others, per_plane, place, rows):
    plane, chip = place // per_plane, place % per_plane
    result = None
    for step, ref in enumerate(others):
        value = ref[plane, rows, :].astype(jnp.float32)
        here = chip_of(step, per_plane, True) == chip
        result = value if result is None else jnp.where(here, value, result)
    return result


def second_half_kernel(cfg, kinds, many, maps_ref, query_ref, hidden_ref, gain_ref, latent_ref, *refs):
    layer, pieces, last, count = cfg["layer"], cfg["pieces"], cfg["last"], cfg["count"]
    planes, per_plane = cfg["planes"], cfg["per_plane"]
    refs = list(refs)
    olds = [refs.pop(0) for _ in range(many)]
    rows_of = {False: [refs.pop(0) for _ in range(per_plane)]}
    rows_of[True] = others = [refs.pop(0) for _ in range(per_plane)]
    mix_refs = [refs.pop(0) for _ in range(pieces)]
    param_refs = [refs.pop(0) for _ in range(pieces)]
    param_all = refs.pop(3)
    sums = list(zip(olds, [refs.pop(3) for _ in range(many)]))
    side, way, member = side_of(), lax.axis_index("head"), lax.axis_index("seq")
    members = planes * per_plane
    features, channels = hidden_ref.shape[1], latent_ref.shape[-1]
    groups, _, group_cols = query_ref.shape
    heads = group_cols // HS
    if len(kinds) <= 8:
        some = [(rows_of[other][step][...], step, other) for step, other in kinds]
        attend_some(cfg, maps_ref, query_ref, some, True, sums)
    else:
        for old, new in sums:
            new[...] = old[...]
        for buffer, other in zip(refs[-2:], (False, True)):
            for step in range(1, per_plane):
                buffer[step] = rows_of[other][step][...]

        def one_step(step, nothing):
            pair = [(refs[-2][step], step, False), (refs[-1][step], step, True)]
            attend_some(cfg, maps_ref, query_ref, pair, False, sums)
            return nothing

        lax.fori_loop(1, per_plane, one_step, 0)

    mixture = hidden_ref[...]
    bands = mixture.shape[0] // count
    head = lax.broadcasted_iota(jnp.int32, (1, group_cols), 1) // HS
    for g in range(groups):
        total = sum(jnp.sum(new[g], axis=1, keepdims=True) for _, new in sums[1:])
        share_of = 1.0 / (total + (0.0 if last else 1.0))
        number_ref = sums[0][1]
        attended = []
        for p in range(bands):
            one = jnp.zeros((count, group_cols), jnp.float32)
            for h in range(heads):
                band = slice((p * heads + h) * count, (p * heads + h + 1) * count)
                one = jnp.where(head == h, number_ref[g, band, :] * share_of[band], one)
            attended.append(one)
        rows = cat([ref[layer] for ref in mix_refs[2 * g : 2 * g + 2]], 0)
        mixture = mixture + dot(cat(attended, 0).astype(jnp.bfloat16), rows)
    spread = lax.rsqrt(jnp.mean(mixture * mixture, axis=1, keepdims=True) + epsilon)
    scaled = (mixture * spread * gain_ref[layer : layer + 1, :]).astype(jnp.bfloat16)
    share = features // pieces
    for j, ref in enumerate(param_refs):
        at = pl.multiple_of(lax.rem(way + j, pieces) * share, 16)
        param_all[pl.ds(at, share), :] = ref[layer]
    predicted = dot(scaled, param_all[...])
    shift_all = predicted[:, :channels]
    log_all = 2.0 * jnp.tanh(0.5 * predicted[:, channels:])
    token = lax.broadcasted_iota(jnp.int32, (count, 1), 0)
    if last:
        held_ref, held_log_ref, out_ref = refs[:3]
        plane = member // per_plane
        before = member - 1 + side
        edge = chosen_rows(others, per_plane, jnp.maximum(before, 0), slice(count, count + 16))
        edge = jnp.where(before >= 0, edge[0:2] + edge[2:4] + edge[4:6], 0.0)
        edge_log = edge[1:2]
        first = (latent_ref[plane, :8, :][:1] - edge[0:1]) * jnp.exp(-edge_log)
        values = jnp.where(token == 0, first, pltpu.roll(held_ref[plane], 1, 0))
        first_log = jnp.where(token == 0, edge_log, pltpu.roll(held_log_ref[plane], 1, 0))
        result = (values - shift_all) * jnp.exp(-log_all)
        term = -(first_log + log_all) - 0.5 * (result * result)
        loglik = jnp.sum(term.T, axis=0, keepdims=True) * (1.0 / channels) - 0.5 * math.log(
            2.0 * math.pi
        )
        out_ref[:count, :] = result
        out_ref[count:, :count] = jnp.broadcast_to(loglik, (8, count))
        return
    held_ref, held_log_ref, narrow_ref = refs[:3]
    for p in range(planes):
        shift_mu = shift_all[p * count : (p + 1) * count]
        log_scale = log_all[p * count : (p + 1) * count]
        following = p * per_plane + member % per_plane + side
        after = chosen_rows(others, per_plane, jnp.minimum(following, members - 1), slice(0, 16))
        values = pltpu.roll(latent_ref[p], count - 1, 0)
        values = jnp.where(token == count - 1, after[:1], values)
        result = (values - shift_mu) * jnp.exp(-log_scale)
        if p == planes - 1:
            result = jnp.where((following == members) & (token == count - 1), 0.0, result)
        held_ref[p] = result
        held_log_ref[p] = log_scale
        edge = jnp.concatenate([shift_mu[count - 1 :], log_scale[count - 1 :]], axis=0)
        terms = []
        for _ in range(3):
            terms.append(edge.astype(jnp.bfloat16).astype(jnp.float32))
            edge = edge - terms[-1]
        rest = jnp.zeros((16 - 6, channels), jnp.float32)
        narrow_ref[p, :count, :] = result.astype(jnp.bfloat16)
        narrow_ref[p, count:, :] = jnp.concatenate(terms + [rest], axis=0).astype(jnp.bfloat16)


def second_half(cfg, kinds, maps, queries, sums, hidden, param_gain, latents, mine, others, mix_pieces, param_pieces, held=()):
    count, planes, channels = cfg["count"], cfg["planes"], latents.shape[-1]
    operands = [maps, queries, hidden, param_gain, latents, *sums, *mine, *others]
    operands += [*mix_pieces, *param_pieces, *held]
    if cfg["last"]:
        results = [((count + 8, channels), jnp.float32)]
    else:
        results = [
            ((planes, count, channels), jnp.float32),
            ((planes, count, channels), jnp.float32),
            ((planes, count + 16, channels), jnp.bfloat16),
        ]
    scratch = [pltpu.VMEM((cfg["features"], param_pieces[0].shape[2]), jnp.bfloat16)]
    scratch += [pltpu.VMEM(one.shape, jnp.float32) for one in sums]
    if len(kinds) > 8:
        scratch += [pltpu.VMEM((len(mine), *mine[0].shape), jnp.bfloat16)] * 2
    return on_chip(
        functools.partial(second_half_kernel, cfg, kinds, len(sums)),
        "second_half",
        operands,
        results,
        scratch=scratch,
    )


def finish_kernel(own_ref, other_ref, final_ref, loglik_ref):
    count = final_ref.shape[0] // 2
    side = side_of()
    for ref, place in ((own_ref, side), (other_ref, 1 - side)):
        final_ref[pl.ds(pl.multiple_of(place * count, 8), count), :] = ref[:count, :]
    first = jnp.where(side == 0, own_ref[count : count + 1, :], other_ref[count : count + 1, :])
    second = jnp.where(side == 0, other_ref[count : count + 1, :], own_ref[count : count + 1, :])
    loglik_ref[...] = jnp.concatenate([first[:, :count], second[:, :count]], axis=1)


def body(
    latents, in_proj, query_proj, key_proj, value_proj, mix_proj, param_proj, attn_gain, param_gain
):
    members, ways = lax.axis_size("seq"), lax.axis_size("head")
    rows, channels = latents.shape
    features = in_proj.shape[2]
    count = rows // 2
    planes = 4 if members % 4 == 0 else 1
    per_plane = members // planes
    bits = per_plane.bit_length() - 1

    def swap(array):
        return lax.ppermute(array, "head", [(i, i ^ 1) for i in range(ways)])

    def pieces_of(array):
        shares = [array]
        for j in range(1, ways):
            shares.append(
                lax.ppermute(array, "head", [((i + j) % ways, i) for i in range(ways)])
            )
        return shares

    def in_plane(mine):
        arrived = []
        for step in range(1, per_plane):
            pairs = []
            for i in range(members):
                for w in range(ways):
                    to = i ^ (turned(step, bits) if w % 2 else step)
                    pairs.append((i * ways + w, to * ways + w))
            arrived.append(lax.ppermute(mine, ("seq", "head"), pairs))
        return arrived

    def run(layer, mine, maps, made, latents, *rest):
        cfg = {
            "layer": layer,
            "last": layer == 1,
            "count": count,
            "features": features,
            "pieces": ways,
            "planes": planes,
            "per_plane": per_plane,
        }
        hidden, queries = made
        arrived = in_plane(mine)
        others = [swap(mine)]
        sums = attend(cfg, maps, queries, [(mine, 0, False), (others[0], 0, True)])
        mines = [mine]
        if per_plane > 1:
            arrived = gate_all(arrived, sums)
            mines += arrived
            others += [swap(piece) for piece in arrived]
        kinds = [(step, False) for step in range(1, per_plane)]
        kinds += [(step, True) for step in range(1, per_plane)]
        if per_plane == 4:
            sums = attend(cfg, maps, queries, [(mines[1], 1, False), (mines[2], 2, False)], sums)
            kinds = kinds[2:]
        return second_half(
            cfg, tuple(kinds), maps, queries, sums, hidden, param_gain, latents, mines, others, mix_pieces, param_pieces, *rest
        )

    (own,) = on_chip(
        half_kernel,
        "half",
        [],
        [((count, channels), jnp.float32)],
        far=[latents],
        scratch=[pltpu.SemaphoreType.DMA((1,))],
    )
    parts = [own] + [
        lax.ppermute(own, "seq", [(i, i ^ (b * per_plane)) for i in range(members)])
        for b in range(1, planes)
    ]
    key_pieces, value_pieces = pieces_of(key_proj), pieces_of(value_proj)
    query_pieces, mix_pieces = pieces_of(query_proj), pieces_of(mix_proj)
    param_pieces = pieces_of(param_proj)
    maps, weights = prepare(in_proj, attn_gain, key_pieces, value_pieces, query_pieces)
    wide, mine = on_chip(
        functools.partial(arrange_kernel, planes),
        "arrange",
        [*parts, maps[0]],
        [((planes, count, channels), jnp.float32), ((planes, count, channels), jnp.bfloat16)],
    )
    made = make_queries(0, planes, count, mine, weights)
    held, held_log, mine = run(0, mine, maps[0], made, wide)
    made = make_queries(1, 1, count, mine, weights)
    (packed,) = run(1, mine, maps[1], made, wide, (held, held_log))
    final_latent, token_loglik = on_chip(
        finish_kernel,
        "finish",
        [packed, swap(packed)],
        [((rows, channels), jnp.float32), ((1, rows), jnp.float32)],
        out_memory=None,
    )
    return (final_latent, token_loglik.reshape(rows))


def solution(mesh):
    placed = (
        P("seq", None),
        P(),
        P(None, None, "head"),
        P(None, None, "head"),
        P(None, None, "head"),
        P(None, "head", None),
        P(None, "head", None),
        P(),
        P(),
    )
    return jax.shard_map(
        body, mesh=mesh, in_specs=placed, out_specs=(P("seq", None), P("seq")), check_vma=False
    )
```

```python
import functools
import math

import jax
import jax.numpy as jnp
from jax import lax
from jax.experimental import pallas as pl
from jax.experimental.pallas import tpu as pltpu
from jax.sharding import PartitionSpec as P

HS = 64

score_scale = 8.0
epsilon = 1e-06

VMEM_LIMIT = 32 * 1024 * 1024


def dot(a, b):
    return jnp.dot(a, b, preferred_element_type=jnp.float32)


def dot_nt(a, b):
    return lax.dot_general(a, b, (((1,), (1,)), ((), ())), preferred_element_type=jnp.float32)


def cat(parts, axis):
    return parts[0] if len(parts) == 1 else jnp.concatenate(parts, axis=axis)


def side_of():
    return lax.rem(lax.axis_index("head"), 2)


def on_chip(kernel, name, operands, results, far=(), scratch=(), out_memory=pltpu.VMEM):
    near = [pltpu.with_memory_space_constraint(array, pltpu.VMEM) for array in operands]
    far = [pltpu.with_memory_space_constraint(array, pltpu.HBM) for array in far]
    if out_memory is pltpu.VMEM:
        out_shape = tuple(pltpu.VMEM(shape, dtype) for shape, dtype in results)
    else:
        out_shape = tuple(jax.ShapeDtypeStruct(shape, dtype) for shape, dtype in results)
    return pl.pallas_call(
        kernel,
        in_specs=[pl.BlockSpec(memory_space=pltpu.VMEM)] * len(near)
        + [pl.BlockSpec(memory_space=pl.ANY)] * len(far),
        out_specs=tuple(pl.BlockSpec(memory_space=pltpu.VMEM) for _ in results),
        out_shape=out_shape,
        scratch_shapes=list(scratch),
        compiler_params=pltpu.CompilerParams(vmem_limit_bytes=VMEM_LIMIT),
        name=name,
    )(*near, *far)


def fetch(sources, targets, sems):
    copies = []
    for at, (source, target) in enumerate(zip(sources, targets)):
        copies.append(pltpu.make_async_copy(source, target, sems.at[at]))
        copies[-1].start()
    return copies


def round_kernel(rows_ref, out_ref, buffer, sems):
    for copy in fetch([rows_ref], [buffer], sems):
        copy.wait()
    out_ref[...] = buffer[...].astype(jnp.bfloat16)


def arrange_kernel(planes, *refs):
    place = lax.axis_index("seq") // (lax.axis_size("seq") // planes)
    mine_ref, other_ref = refs[-2:]
    count = mine_ref.shape[1]
    for step in range(planes):
        first, second = refs[step][:count, :], refs[step][count:, :]
        mine_ref[place ^ step] = jnp.where(side_of() == 0, first, second)
        other_ref[place ^ step] = jnp.where(side_of() == 0, second, first)


def gates_kernel(many, *refs):
    for source, target in zip(refs[:many], refs[-many:]):
        target[...] = source[...]


def gate_all(rows, made):
    results = [(piece.shape, piece.dtype) for piece in rows]
    return on_chip(functools.partial(gates_kernel, len(rows)), "gate", [*rows, *made], results)


def turned(step, bits):
    return sum(((step >> b) & 1) << (bits - 1 - b) for b in range(bits))


def chip_of(step, per_plane, other):
    bits = per_plane.bit_length() - 1
    first = side_of() == (1 if other else 0)
    return (lax.axis_index("seq") % per_plane) ^ jnp.where(first, step, turned(step, bits))


def make_maps(layer, in_ref, gain_ref, weights, out_ref):
    channels = in_ref.shape[1]

    def store(row, value):
        high = value.astype(jnp.bfloat16)
        rows = value.shape[0]
        out_ref[row : row + rows, :channels] = high
        out_ref[row : row + rows, channels:] = (value - high.astype(jnp.float32)).astype(
            jnp.bfloat16
        )
        return row + rows

    base = in_ref[layer]
    scaled = base.astype(jnp.float32) * gain_ref[layer : layer + 1, :]
    high = scaled.astype(jnp.bfloat16)
    low = (scaled - high.astype(jnp.float32)).astype(jnp.bfloat16)
    both = jnp.concatenate([high, low], axis=0)
    row = 0
    for first in range(0, weights.shape[0], 2):
        product = dot(both, cat([weights[first], weights[first + 1]], 1))
        row = store(row, (product[:channels] + product[channels:]).T)
    row = store(row, dot_nt(base, base))
    eye = lax.broadcasted_iota(jnp.int32, (channels, channels), 0) == lax.broadcasted_iota(
        jnp.int32, (channels, channels), 1
    )
    store(row, jnp.where(eye, 1.0, 0.0))


def prepare_kernel(pieces, in_src, gain_src, *refs):
    sources, refs = refs[: 3 * pieces], refs[3 * pieces :]
    maps_ref, in_ref, gain_ref, query_ref, later_ref, buffer, sems = refs
    both = list(sources[: 2 * pieces])
    near = [in_src, gain_src] + [source.at[0] for source in both]
    targets = [in_ref, gain_ref] + [buffer.at[at] for at in range(2 * pieces)]
    near += list(sources[2 * pieces :]) + [source.at[1] for source in both]
    targets += [query_ref.at[at] for at in range(pieces)]
    targets += [later_ref.at[at] for at in range(2 * pieces)]
    copies = fetch(near, targets, sems)
    for copy in copies[: 2 + 2 * pieces]:
        copy.wait()
    make_maps(0, in_ref, gain_ref, buffer, maps_ref)
    for copy in copies[2 + 2 * pieces :]:
        copy.wait()


def prepare(in_proj, attn_gain, key_pieces, value_pieces, query_pieces):
    pieces = len(key_pieces)
    _, channels, features = in_proj.shape
    columns = key_pieces[0].shape[2]
    rows = 2 * pieces * columns + 2 * channels
    buffer = (2 * pieces, features, columns)
    return on_chip(
        functools.partial(prepare_kernel, pieces),
        "prepare",
        [],
        [
            ((rows, 2 * channels), jnp.bfloat16),
            (in_proj.shape, in_proj.dtype),
            (attn_gain.shape, attn_gain.dtype),
            ((pieces, *query_pieces[0].shape), jnp.bfloat16),
            (buffer, jnp.bfloat16),
        ],
        far=[in_proj, attn_gain, *key_pieces, *value_pieces, *query_pieces],
        scratch=[pltpu.VMEM(buffer, jnp.bfloat16), pltpu.SemaphoreType.DMA((5 * pieces + 2,))],
    )


def second_maps_kernel(after_ref, in_ref, gain_ref, weights_ref, out_ref):
    make_maps(1, in_ref, gain_ref, weights_ref, out_ref)


def queries_kernel(layer, planes, rows_ref, in_ref, gain_ref, query_ref, hidden_ref, out_ref):
    if planes == rows_ref.shape[0]:
        rows = rows_ref[...]
    else:
        count = hidden_ref.shape[0]
        place = lax.axis_index("seq") // (lax.axis_size("seq") // rows_ref.shape[0])
        rows = rows_ref[place, :count, :]
    rows = rows.reshape(hidden_ref.shape[0], rows_ref.shape[2])
    count = rows.shape[0] // planes
    hidden = dot(rows, in_ref[layer])
    hidden_ref[...] = hidden
    spread = lax.rsqrt(jnp.mean(hidden * hidden, axis=1, keepdims=True) + epsilon)
    normed = (hidden * spread * gain_ref[layer : layer + 1, :]).astype(jnp.bfloat16)
    for first in range(0, query_ref.shape[0], 2):
        query = dot(normed, cat([query_ref[at, layer] for at in range(first, first + 2)], 1))
        width = query.shape[1]
        heads = width // HS
        head = lax.broadcasted_iota(jnp.int32, (1, width), 1) // HS
        same = head == lax.broadcasted_iota(jnp.int32, (width, 1), 0) // HS
        same = jnp.where(same, 1.0, 0.0).astype(jnp.bfloat16)
        square = query * query
        high = square.astype(jnp.bfloat16)
        low = (square - high.astype(jnp.float32)).astype(jnp.bfloat16)
        mean = (dot(high, same) + dot(low, same)) * (1.0 / HS)
        query = query * lax.rsqrt(mean + epsilon)
        for h in range(heads):
            band = jnp.where(head == h, query, 0.0).astype(jnp.bfloat16)
            for p in range(planes):
                row = (p * heads + h) * count
                out_ref[first // 2, row : row + count, :] = band[p * count : (p + 1) * count]


def make_queries(layer, planes, count, rows, weights):
    in_all, _, query_all = weights
    width = 2 * query_all.shape[3]
    return on_chip(
        functools.partial(queries_kernel, layer, planes),
        "queries",
        [rows, *weights],
        [
            ((planes * count, in_all.shape[2]), jnp.float32),
            ((query_all.shape[0] // 2, planes * width // HS * count, width), jnp.bfloat16),
        ],
    )


def attend_some(cfg, maps_ref, query_ref, some, start, sums):
    count, features, planes, per_plane = cfg["count"], cfg["features"], cfg["planes"], cfg["per_plane"]
    layer, side = cfg["layer"], side_of()
    groups, _, group_cols = query_ref.shape
    heads = group_cols // HS
    band = heads * count
    total_cols = groups * group_cols
    stride = 2 * per_plane * count
    token = lax.broadcasted_iota(jnp.int32, (count, 1), 0)
    member = lax.axis_index("seq")
    query_place = (member % per_plane * 2 + side) * count + jnp.concatenate([token] * heads, axis=0)
    offsets = [
        (chip_of(step, per_plane, other) * 2 + (1 - side if other else side)) * count
        for _, step, other in some
    ]
    if layer == 0:
        size = len(some) * count
        lane = lax.broadcasted_iota(jnp.int32, (1, size), 1)
        key_place = lane + offsets[0]
        for at in range(1, len(some)):
            key_place = jnp.where(lane >= at * count, lane - at * count + offsets[at], key_place)
        allowed = key_place <= query_place
        parts = [cat([rows[p, :count, :] for rows, _, _ in some], 0) for p in range(planes)]
        low_rows = [p * band for p in range(planes)]
    else:
        size = len(some) * planes * count
        lane = lax.broadcasted_iota(jnp.int32, (1, planes * count), 1)
        plane = ((lane.astype(jnp.float32) + 0.5) * (1.0 / count)).astype(jnp.int32)
        base_place = lane + plane * (stride - count)
        key_place = jnp.concatenate([base_place + offset for offset in offsets], axis=1)
        allowed = key_place >= query_place + member // per_plane * stride
        rows = [rows[:, :count, :].reshape(planes * count, rows.shape[2]) for rows, _, _ in some]
        parts, low_rows = [cat(rows, 0)], [0]

    def keys_and_values(source, g):
        low = g * group_cols
        twice = jnp.concatenate([source, source], axis=1)
        channels = source.shape[1]
        tail = dot_nt(maps_ref[2 * total_cols :, :], twice)
        square = jnp.sum(tail[:channels] * tail[channels:], axis=0, keepdims=True)
        scale = lax.rsqrt(jnp.maximum(square, 0.0) * (1.0 / features) + epsilon)
        scale_sq = scale * scale
        key = dot_nt(maps_ref[low : low + group_cols, :], twice)
        value = dot_nt(maps_ref[total_cols + low : total_cols + low + group_cols, :], twice)
        keys = []
        for h in range(heads):
            one = key[h * HS : (h + 1) * HS]
            mean = jnp.sum(one * one, axis=0, keepdims=True) * (1.0 / HS)
            factor = scale * lax.rsqrt(mean * scale_sq + epsilon) * (score_scale / HS)
            keys.append((one * factor).astype(jnp.bfloat16))
        return jnp.concatenate(keys, axis=0), (value * scale).astype(jnp.bfloat16)

    for g in range(groups):
        if size % 128 == 0 and len(parts) > 1:
            key, value = keys_and_values(cat(parts, 0), g)
            made = [
                (key[:, p * size : (p + 1) * size], value[:, p * size : (p + 1) * size])
                for p in range(len(parts))
            ]
        else:
            made = [keys_and_values(part, g) for part in parts]
        for index, ((key, value), low_row) in enumerate(zip(made, low_rows)):
            scores = dot(query_ref[g, low_row:, :], key)
            weights = jnp.exp(scores)
            first = jnp.where(allowed, weights[:band], 0.0)
            weights = first if weights.shape[0] == band else cat([first, weights[band:]], 0)
            product = dot_nt(weights.astype(jnp.bfloat16), value)
            lanes = [weights[:, at : at + 128] for at in range(0, weights.shape[1], 128)]
            news = [product, sum(part for part in lanes if part.shape[1] == 128)]
            news += [part for part in lanes if part.shape[1] < 128]
            for at, (old_ref, new_ref) in enumerate(sums):
                if start and index == 0:
                    old = None if old_ref is None else old_ref[g]
                else:
                    old = new_ref[g, low_row:, :]
                if at < len(news):
                    new = news[at] if old is None else old + news[at]
                else:
                    new = jnp.zeros(new_ref.shape[1:], jnp.float32) if old is None else old
                if at < len(news) or (start and index == 0):
                    new_ref[g, low_row:, :] = new


def sum_shapes(cfg, queries):
    groups, rows, cols = queries.shape
    shapes = [(groups, rows, cols), (groups, rows, 128)]
    rest = 2 * cfg["count"] % 128
    return shapes + ([(groups, rows, rest)] if cfg["layer"] == 0 and rest else [])


def attend_kernel(cfg, kinds, resume, maps_ref, query_ref, *refs):
    refs = list(refs)
    pieces = [(refs.pop(0), step, other) for step, other in kinds]
    many = len(refs) // 2 if resume else len(refs)
    olds = refs[:many] if resume else [None] * many
    sums = list(zip(olds, refs[-many:]))
    some = [(ref[...], step, other) for ref, step, other in pieces]
    attend_some(cfg, maps_ref, query_ref, some, True, sums)


def attend(cfg, maps, queries, pieces, sums=()):
    kinds = tuple((step, other) for _, step, other in pieces)
    return on_chip(
        functools.partial(attend_kernel, cfg, kinds, len(sums) > 0),
        "attend",
        [maps, queries, *[piece for piece, _, _ in pieces], *sums],
        [(shape, jnp.float32) for shape in sum_shapes(cfg, queries)],
    )


def chosen_rows(others, per_plane, place, rows):
    plane, chip = place // per_plane, place % per_plane
    result = None
    for step, ref in enumerate(others):
        value = ref[plane, rows, :].astype(jnp.float32)
        here = chip_of(step, per_plane, True) == chip
        result = value if result is None else jnp.where(here, value, result)
    return result


def second_half_kernel(cfg, kinds, many, maps_ref, query_ref, hidden_ref, gain_ref, latent_ref, *refs):
    layer, pieces, last, count = cfg["layer"], cfg["pieces"], cfg["last"], cfg["count"]
    planes, per_plane = cfg["planes"], cfg["per_plane"]
    refs = list(refs)
    olds = [refs.pop(0) for _ in range(many)]
    rows_of = {False: [refs.pop(0) for _ in range(per_plane)]}
    rows_of[True] = others = [refs.pop(0) for _ in range(per_plane)]
    mix_refs = [refs.pop(0) for _ in range(pieces)]
    param_refs = [refs.pop(0) for _ in range(pieces)]
    param_all = refs.pop(3)
    sums = list(zip(olds, [refs.pop(3) for _ in range(many)]))
    side, way, member = side_of(), lax.axis_index("head"), lax.axis_index("seq")
    members = planes * per_plane
    features, channels = hidden_ref.shape[1], latent_ref.shape[-1]
    groups, _, group_cols = query_ref.shape
    heads = group_cols // HS
    if len(kinds) <= 8:
        some = [(rows_of[other][step][...], step, other) for step, other in kinds]
        attend_some(cfg, maps_ref, query_ref, some, True, sums)
    else:
        for old, new in sums:
            new[...] = old[...]
        for buffer, other in zip(refs[-2:], (False, True)):
            for step in range(1, per_plane):
                buffer[step] = rows_of[other][step][...]

        def one_step(step, nothing):
            pair = [(refs[-2][step], step, False), (refs[-1][step], step, True)]
            attend_some(cfg, maps_ref, query_ref, pair, False, sums)
            return nothing

        lax.fori_loop(1, per_plane, one_step, 0)

    mixture = hidden_ref[...]
    bands = mixture.shape[0] // count
    head = lax.broadcasted_iota(jnp.int32, (1, group_cols), 1) // HS
    for g in range(groups):
        total = sum(jnp.sum(new[g], axis=1, keepdims=True) for _, new in sums[1:])
        share_of = 1.0 / (total + (0.0 if last else 1.0))
        number_ref = sums[0][1]
        attended = []
        for p in range(bands):
            one = jnp.zeros((count, group_cols), jnp.float32)
            for h in range(heads):
                band = slice((p * heads + h) * count, (p * heads + h + 1) * count)
                one = jnp.where(head == h, number_ref[g, band, :] * share_of[band], one)
            attended.append(one)
        rows = cat([ref[layer] for ref in mix_refs[2 * g : 2 * g + 2]], 0)
        mixture = mixture + dot(cat(attended, 0).astype(jnp.bfloat16), rows)
    spread = lax.rsqrt(jnp.mean(mixture * mixture, axis=1, keepdims=True) + epsilon)
    scaled = (mixture * spread * gain_ref[layer : layer + 1, :]).astype(jnp.bfloat16)
    share = features // pieces
    for j, ref in enumerate(param_refs):
        at = pl.multiple_of(lax.rem(way + j, pieces) * share, 16)
        param_all[pl.ds(at, share), :] = ref[layer]
    predicted = dot(scaled, param_all[...])
    shift_all = predicted[:, :channels]
    log_all = 2.0 * jnp.tanh(0.5 * predicted[:, channels:])
    token = lax.broadcasted_iota(jnp.int32, (count, 1), 0)
    if last:
        held_ref, held_log_ref, out_ref = refs[:3]
        before = member - 1 + side
        edge = chosen_rows(others, per_plane, jnp.maximum(before, 0), slice(count, count + 16))
        edge = jnp.where(before >= 0, edge[0:2] + edge[2:4] + edge[4:6], 0.0)
        edge_log = edge[1:2]
        start = pl.multiple_of(side * count, 8)
        first = (latent_ref[pl.ds(start, 8), :][:1] - edge[0:1]) * jnp.exp(-edge_log)
        values = jnp.where(token == 0, first, pltpu.roll(held_ref[...], 1, 0))
        first_log = jnp.where(token == 0, edge_log, pltpu.roll(held_log_ref[...], 1, 0))
        result = (values - shift_all) * jnp.exp(-log_all)
        term = -(first_log + log_all) - 0.5 * (result * result)
        loglik = jnp.sum(term.T, axis=0, keepdims=True) * (1.0 / channels) - 0.5 * math.log(
            2.0 * math.pi
        )
        out_ref[:count, :] = result
        out_ref[count:, :count] = jnp.broadcast_to(loglik, (8, count))
        return
    held_ref, held_log_ref, narrow_ref = refs[:3]
    own = latent_ref[pl.ds(pl.multiple_of(side * count, 8), count), :]
    for p in range(planes):
        shift_mu = shift_all[p * count : (p + 1) * count]
        log_scale = log_all[p * count : (p + 1) * count]
        following = p * per_plane + member % per_plane + side
        after = chosen_rows(others, per_plane, jnp.minimum(following, members - 1), slice(0, 16))
        here = member // per_plane == p
        values = jnp.where(here, own, rows_of[False][0][p, :count, :].astype(jnp.float32))
        values = pltpu.roll(values, count - 1, 0)
        values = jnp.where(token == count - 1, after[:1], values)
        result = (values - shift_mu) * jnp.exp(-log_scale)
        if p == planes - 1:
            result = jnp.where((following == members) & (token == count - 1), 0.0, result)

        @pl.when(here)
        def keep(result=result, log_scale=log_scale):
            held_ref[...] = result
            held_log_ref[...] = log_scale

        edge = jnp.concatenate([shift_mu[count - 1 :], log_scale[count - 1 :]], axis=0)
        terms = []
        for _ in range(3):
            terms.append(edge.astype(jnp.bfloat16).astype(jnp.float32))
            edge = edge - terms[-1]
        rest = jnp.zeros((16 - 6, channels), jnp.float32)
        narrow_ref[p, :count, :] = result.astype(jnp.bfloat16)
        narrow_ref[p, count:, :] = jnp.concatenate(terms + [rest], axis=0).astype(jnp.bfloat16)


def second_half(cfg, kinds, maps, queries, sums, hidden, param_gain, latents, mine, others, mix_pieces, param_pieces, held=()):
    count, planes, channels = cfg["count"], cfg["planes"], latents.shape[-1]
    operands = [maps, queries, hidden, param_gain, latents, *sums, *mine, *others]
    operands += [*mix_pieces, *param_pieces, *held]
    if cfg["last"]:
        results = [((count + 8, channels), jnp.float32)]
    else:
        results = [
            ((count, channels), jnp.float32),
            ((count, channels), jnp.float32),
            ((planes, count + 16, channels), jnp.bfloat16),
        ]
    scratch = [pltpu.VMEM((cfg["features"], param_pieces[0].shape[2]), jnp.bfloat16)]
    scratch += [pltpu.VMEM(one.shape, jnp.float32) for one in sums]
    if len(kinds) > 8:
        scratch += [pltpu.VMEM((len(mine), *mine[0].shape), jnp.bfloat16)] * 2
    return on_chip(
        functools.partial(second_half_kernel, cfg, kinds, len(sums)),
        "second_half",
        operands,
        results,
        scratch=scratch,
    )


def finish_kernel(own_ref, other_ref, final_ref, loglik_ref):
    count = final_ref.shape[0] // 2
    side = side_of()
    for ref, place in ((own_ref, side), (other_ref, 1 - side)):
        final_ref[pl.ds(pl.multiple_of(place * count, 8), count), :] = ref[:count, :]
    first = jnp.where(side == 0, own_ref[count : count + 1, :], other_ref[count : count + 1, :])
    second = jnp.where(side == 0, other_ref[count : count + 1, :], own_ref[count : count + 1, :])
    loglik_ref[...] = jnp.concatenate([first[:, :count], second[:, :count]], axis=1)


def body(
    latents, in_proj, query_proj, key_proj, value_proj, mix_proj, param_proj, attn_gain, param_gain
):
    members, ways = lax.axis_size("seq"), lax.axis_size("head")
    rows, channels = latents.shape
    features = in_proj.shape[2]
    count = rows // 2
    planes = 4 if members % 4 == 0 else 1
    per_plane = members // planes
    bits = per_plane.bit_length() - 1

    def swap(array):
        return lax.ppermute(array, "head", [(i, i ^ 1) for i in range(ways)])

    def pieces_of(array):
        shares = [array]
        for j in range(1, ways):
            shares.append(
                lax.ppermute(array, "head", [((i + j) % ways, i) for i in range(ways)])
            )
        return shares

    def in_plane(mine):
        arrived = []
        for step in range(1, per_plane):
            pairs = []
            for i in range(members):
                for w in range(ways):
                    to = i ^ (turned(step, bits) if w % 2 else step)
                    pairs.append((i * ways + w, to * ways + w))
            arrived.append(lax.ppermute(mine, ("seq", "head"), pairs))
        return arrived

    def run(layer, mine, sibling, maps, made, latents, *rest):
        cfg = {
            "layer": layer,
            "last": layer == 1,
            "count": count,
            "features": features,
            "pieces": ways,
            "planes": planes,
            "per_plane": per_plane,
        }
        hidden, queries = made
        arrived = in_plane(mine)
        if per_plane == 4:
            early = [(mine, 0, False)] + ([(sibling, 0, True)] if layer == 0 else [])
            sums = attend(cfg, maps, queries, early)
            first, second, *own = gate_all(arrived[:2] + ([] if layer == 0 else [mine]), sums)
            others = [sibling if layer == 0 else swap(own[0]), swap(first)]
            if layer == 0:
                others.append(swap(second))
            sums = attend(cfg, maps, queries, [(first, 1, False), (second, 2, False)], sums)
            third, *again = gate_all(arrived[2:] + ([] if layer == 0 else [second]), sums)
            if layer == 1:
                others.append(swap(again[0]))
            others.append(swap(third))
            more = [(third, 3, False)] + ([] if layer == 0 else [(others[0], 0, True)])
            sums = attend(cfg, maps, queries, more + [(others[1], 1, True)], sums)
            mines = [mine, first, second, third]
            kinds = [(2, True), (3, True)]
        else:
            others = [swap(mine) if layer == 1 else sibling]
            sums = attend(cfg, maps, queries, [(mine, 0, False), (others[0], 0, True)])
            mines = [mine]
            if per_plane > 1:
                arrived = gate_all(arrived, sums)
                mines += arrived
                others += [swap(piece) for piece in arrived]
            kinds = [(step, False) for step in range(1, per_plane)]
            kinds += [(step, True) for step in range(1, per_plane)]
        return second_half(
            cfg, tuple(kinds), maps, queries, sums, hidden, param_gain, latents, mines, others, mix_pieces, param_pieces, *rest
        )

    (rounded,) = on_chip(
        round_kernel,
        "round",
        [],
        [(latents.shape, jnp.bfloat16)],
        far=[latents],
        scratch=[pltpu.VMEM(latents.shape, jnp.float32), pltpu.SemaphoreType.DMA((1,))],
    )
    parts = [rounded] + [
        lax.ppermute(rounded, "seq", [(i, i ^ (b * per_plane)) for i in range(members)])
        for b in range(1, planes)
    ]
    key_pieces, value_pieces = pieces_of(key_proj), pieces_of(value_proj)
    query_pieces, mix_pieces = pieces_of(query_proj), pieces_of(mix_proj)
    param_pieces = pieces_of(param_proj)
    maps, *weights, later = prepare(in_proj, attn_gain, key_pieces, value_pieces, query_pieces)
    shape = (planes, count, channels)
    mine, sibling = on_chip(
        functools.partial(arrange_kernel, planes),
        "arrange",
        [*parts, maps],
        [(shape, jnp.bfloat16), (shape, jnp.bfloat16)],
    )
    made = make_queries(0, planes, count, mine, weights)
    held, held_log, mine = run(0, mine, sibling, maps, made, latents)
    (maps,) = on_chip(
        second_maps_kernel, "second_maps", [mine, *weights[:2], later], [(maps.shape, maps.dtype)]
    )
    made = make_queries(1, 1, count, mine, weights)
    (packed,) = run(1, mine, None, maps, made, latents, (held, held_log))
    final_latent, token_loglik = on_chip(
        finish_kernel,
        "finish",
        [packed, swap(packed)],
        [((rows, channels), jnp.float32), ((1, rows), jnp.float32)],
        out_memory=None,
    )
    return (final_latent, token_loglik.reshape(rows))


def solution(mesh):
    placed = (
        P("seq", None),
        P(),
        P(None, None, "head"),
        P(None, None, "head"),
        P(None, None, "head"),
        P(None, "head", None),
        P(None, "head", None),
        P(),
        P(),
    )
    return jax.shard_map(
        body, mesh=mesh, in_specs=placed, out_specs=(P("seq", None), P("seq")), check_vma=False
    )
```

```python
import functools
import math

import jax
import jax.numpy as jnp
from jax import lax
from jax.experimental import pallas as pl
from jax.experimental.pallas import tpu as pltpu
from jax.sharding import PartitionSpec as P

HS = 64

score_scale = 8.0
epsilon = 1e-06

VMEM_LIMIT = 32 * 1024 * 1024


def dot(a, b):
    return jnp.dot(a, b, preferred_element_type=jnp.float32)


def dot_nt(a, b):
    return lax.dot_general(a, b, (((1,), (1,)), ((), ())), preferred_element_type=jnp.float32)


def cat(parts, axis):
    return parts[0] if len(parts) == 1 else jnp.concatenate(parts, axis=axis)


def side_of():
    return lax.rem(lax.axis_index("head"), 2)


def on_chip(kernel, name, operands, results, far=(), after=(), scratch=(), out_memory=pltpu.VMEM):
    near = [pltpu.with_memory_space_constraint(array, pltpu.VMEM) for array in operands]
    far = [pltpu.with_memory_space_constraint(array, pltpu.HBM) for array in far]
    if out_memory is pltpu.VMEM:
        out_shape = tuple(pltpu.VMEM(shape, dtype) for shape, dtype in results)
    else:
        out_shape = tuple(jax.ShapeDtypeStruct(shape, dtype) for shape, dtype in results)
    return pl.pallas_call(
        kernel,
        in_specs=[pl.BlockSpec(memory_space=pltpu.VMEM)] * len(near)
        + [pl.BlockSpec(memory_space=pl.ANY)] * (len(far) + len(after)),
        out_specs=tuple(pl.BlockSpec(memory_space=pltpu.VMEM) for _ in results),
        out_shape=out_shape,
        scratch_shapes=list(scratch),
        compiler_params=pltpu.CompilerParams(vmem_limit_bytes=VMEM_LIMIT),
        name=name,
    )(*near, *far, *after)


def fetch(sources, targets, sems):
    copies = []
    for at, (source, target) in enumerate(zip(sources, targets)):
        copies.append(pltpu.make_async_copy(source, target, sems.at[at]))
        copies[-1].start()
    return copies


def round_kernel(rows_ref, out_ref, buffer, sems):
    for copy in fetch([rows_ref], [buffer], sems):
        copy.wait()
    out_ref[...] = buffer[...].astype(jnp.bfloat16)


def arrange_kernel(planes, *refs):
    place = lax.axis_index("seq") // (lax.axis_size("seq") // planes)
    mine_ref, other_ref, maps_ref = refs[-3:]
    maps_ref[...] = refs[planes][...]
    count = mine_ref.shape[1]
    for step in range(planes):
        first, second = refs[step][:count, :], refs[step][count:, :]
        mine_ref[place ^ step] = jnp.where(side_of() == 0, first, second)
        other_ref[place ^ step] = jnp.where(side_of() == 0, second, first)


def gates_kernel(many, *refs):
    for source, target in zip(refs[:many], refs[-many:]):
        target[...] = source[...]


def gate_all(rows, made):
    results = [(piece.shape, piece.dtype) for piece in rows]
    return on_chip(functools.partial(gates_kernel, len(rows)), "gate", [*rows, *made], results)


def turned(step, bits):
    return sum(((step >> b) & 1) << (bits - 1 - b) for b in range(bits))


def chip_of(step, per_plane, other):
    bits = per_plane.bit_length() - 1
    first = side_of() == (1 if other else 0)
    return (lax.axis_index("seq") % per_plane) ^ jnp.where(first, step, turned(step, bits))


def prepare_kernel(in_src, gain_src, key_src, value_src, query_src, *refs):
    in_ref, tail_ref, maps_ref, gain_ref, buffer, sems = refs[-6:]
    layers, channels, _ = in_ref.shape
    weights = (key_src, value_src, query_src)
    sources = [in_src, gain_src] + [src.at[b] for b in range(layers) for src in weights]
    targets = [in_ref, gain_ref] + [buffer.at[b, at] for b in range(layers) for at in range(3)]
    copies = fetch(sources, targets, sems)
    for copy in copies[:2]:
        copy.wait()
    eye = lax.broadcasted_iota(jnp.int32, (channels, channels), 0) == lax.broadcasted_iota(
        jnp.int32, (channels, channels), 1
    )

    def store(ref, row, value):
        high = value.astype(jnp.bfloat16)
        rows = slice(row, row + value.shape[0])
        ref[rows, :channels] = high
        ref[rows, channels:] = (value - high.astype(jnp.float32)).astype(jnp.bfloat16)

    for layer in range(layers):
        base = in_ref[layer]
        store(tail_ref.at[layer], 0, dot_nt(base, base))
        store(tail_ref.at[layer], channels, jnp.where(eye, 1.0, 0.0))
        scaled = base.astype(jnp.float32) * gain_ref[layer : layer + 1, :]
        high = scaled.astype(jnp.bfloat16)
        low = (scaled - high.astype(jnp.float32)).astype(jnp.bfloat16)
        both = jnp.concatenate([high, low], axis=0)
        for at in range(3):
            copies[2 + 3 * layer + at].wait()
        product = dot(both, cat([buffer[layer, at] for at in range(3)], 1))
        store(maps_ref.at[layer], 0, (product[:channels] + product[channels:]).T)


def prepare(in_proj, attn_gain, key_proj, value_proj, query_proj, after):
    layers, channels, features = in_proj.shape
    columns = key_proj.shape[2]
    return on_chip(
        prepare_kernel,
        "prepare",
        [],
        [
            (in_proj.shape, jnp.bfloat16),
            ((layers, 2 * channels, 2 * channels), jnp.bfloat16),
            ((layers, 3 * columns, 2 * channels), jnp.bfloat16),
        ],
        far=[in_proj, attn_gain, key_proj, value_proj, query_proj],
        after=after,
        scratch=[
            pltpu.VMEM(attn_gain.shape, jnp.float32),
            pltpu.VMEM((layers, 3, features, columns), jnp.bfloat16),
            pltpu.SemaphoreType.DMA((2 + 3 * layers,)),
        ],
    )


def join_kernel(pieces, tail_ref, *refs):
    sources, outs = refs[:pieces], refs[pieces:]
    layers = tail_ref.shape[0]
    columns = sources[0].shape[1] // 3
    for layer in range(layers):
        maps_ref, query_ref = outs[2 * layer : 2 * layer + 2]
        total = pieces * columns
        for j, source in enumerate(sources):
            for at in range(2):
                row = at * total + j * columns
                maps_ref[row : row + columns, :] = source[layer, at * columns : (at + 1) * columns]
            query_ref[j * columns : (j + 1) * columns, :] = source[layer, 2 * columns :]
        maps_ref[2 * total :, :] = tail_ref[layer]


def join(tail, pieces):
    layers, rows, width = pieces[0].shape
    total = len(pieces) * rows // 3
    results = [((2 * total + tail.shape[1], width), jnp.bfloat16), ((total, width), jnp.bfloat16)]
    return on_chip(
        functools.partial(join_kernel, len(pieces)), "join", [tail, *pieces], results * layers
    )


def queries_kernel(layer, planes, rows_ref, in_ref, maps_ref, hidden_ref, out_ref):
    if planes == rows_ref.shape[0]:
        rows = rows_ref[...]
    else:
        count = hidden_ref.shape[0]
        place = lax.axis_index("seq") // (lax.axis_size("seq") // rows_ref.shape[0])
        rows = rows_ref[place, :count, :]
    rows = rows.reshape(hidden_ref.shape[0], rows_ref.shape[2])
    count = rows.shape[0] // planes
    hidden = dot(rows, in_ref[layer])
    hidden_ref[...] = hidden
    spread = lax.rsqrt(jnp.mean(hidden * hidden, axis=1, keepdims=True) + epsilon)
    twice = jnp.concatenate([rows, rows], axis=1)
    groups, _, width = out_ref.shape
    heads = width // HS
    head = lax.broadcasted_iota(jnp.int32, (1, width), 1) // HS
    same = head == lax.broadcasted_iota(jnp.int32, (width, 1), 0) // HS
    same = jnp.where(same, 1.0, 0.0).astype(jnp.bfloat16)
    for g in range(groups):
        query = dot_nt(twice, maps_ref[g * width : (g + 1) * width, :]) * spread
        square = query * query
        high = square.astype(jnp.bfloat16)
        low = (square - high.astype(jnp.float32)).astype(jnp.bfloat16)
        mean = (dot(high, same) + dot(low, same)) * (1.0 / HS)
        query = query * lax.rsqrt(mean + epsilon)
        for h in range(heads):
            band = jnp.where(head == h, query, 0.0).astype(jnp.bfloat16)
            for p in range(planes):
                row = (p * heads + h) * count
                out_ref[g, row : row + count, :] = band[p * count : (p + 1) * count]


def make_queries(layer, planes, count, rows, in_all, maps, width):
    return on_chip(
        functools.partial(queries_kernel, layer, planes),
        "queries",
        [rows, in_all, maps],
        [
            ((planes * count, in_all.shape[2]), jnp.float32),
            ((maps.shape[0] // width, planes * width // HS * count, width), jnp.bfloat16),
        ],
    )


def attend_some(cfg, maps_ref, query_ref, some, start, sums):
    count, features, planes, per_plane = cfg["count"], cfg["features"], cfg["planes"], cfg["per_plane"]
    layer, side = cfg["layer"], side_of()
    groups, _, group_cols = query_ref.shape
    heads = group_cols // HS
    band = heads * count
    total_cols = groups * group_cols
    stride = 2 * per_plane * count
    token = lax.broadcasted_iota(jnp.int32, (count, 1), 0)
    member = lax.axis_index("seq")
    query_place = (member % per_plane * 2 + side) * count + jnp.concatenate([token] * heads, axis=0)
    offsets = [
        (chip_of(step, per_plane, other) * 2 + (1 - side if other else side)) * count
        for _, step, other in some
    ]
    if layer == 0:
        size = len(some) * count
        lane = lax.broadcasted_iota(jnp.int32, (1, size), 1)
        key_place = lane + offsets[0]
        for at in range(1, len(some)):
            key_place = jnp.where(lane >= at * count, lane - at * count + offsets[at], key_place)
        allowed = key_place <= query_place
        parts = [cat([rows[p, :count, :] for rows, _, _ in some], 0) for p in range(planes)]
        low_rows = [p * band for p in range(planes)]
    else:
        size = len(some) * planes * count
        lane = lax.broadcasted_iota(jnp.int32, (1, planes * count), 1)
        plane = ((lane.astype(jnp.float32) + 0.5) * (1.0 / count)).astype(jnp.int32)
        base_place = lane + plane * (stride - count)
        key_place = jnp.concatenate([base_place + offset for offset in offsets], axis=1)
        allowed = key_place >= query_place + member // per_plane * stride
        rows = [rows[:, :count, :].reshape(planes * count, rows.shape[2]) for rows, _, _ in some]
        parts, low_rows = [cat(rows, 0)], [0]

    def keys_and_values(source, g):
        low = g * group_cols
        twice = jnp.concatenate([source, source], axis=1)
        channels = source.shape[1]
        tail = dot_nt(maps_ref[2 * total_cols :, :], twice)
        square = jnp.sum(tail[:channels] * tail[channels:], axis=0, keepdims=True)
        scale = lax.rsqrt(jnp.maximum(square, 0.0) * (1.0 / features) + epsilon)
        scale_sq = scale * scale
        key = dot_nt(maps_ref[low : low + group_cols, :], twice)
        value = dot_nt(maps_ref[total_cols + low : total_cols + low + group_cols, :], twice)
        keys = []
        for h in range(heads):
            one = key[h * HS : (h + 1) * HS]
            mean = jnp.sum(one * one, axis=0, keepdims=True) * (1.0 / HS)
            factor = scale * lax.rsqrt(mean * scale_sq + epsilon) * (score_scale / HS)
            keys.append((one * factor).astype(jnp.bfloat16))
        return jnp.concatenate(keys, axis=0), (value * scale).astype(jnp.bfloat16)

    for g in range(groups):
        if size % 128 == 0 and len(parts) > 1:
            key, value = keys_and_values(cat(parts, 0), g)
            made = [
                (key[:, p * size : (p + 1) * size], value[:, p * size : (p + 1) * size])
                for p in range(len(parts))
            ]
        else:
            made = [keys_and_values(part, g) for part in parts]
        for index, ((key, value), low_row) in enumerate(zip(made, low_rows)):
            scores = dot(query_ref[g, low_row:, :], key)
            weights = jnp.exp(scores)
            first = jnp.where(allowed, weights[:band], 0.0)
            weights = first if weights.shape[0] == band else cat([first, weights[band:]], 0)
            product = dot_nt(weights.astype(jnp.bfloat16), value)
            lanes = [weights[:, at : at + 128] for at in range(0, weights.shape[1], 128)]
            news = [product, sum(part for part in lanes if part.shape[1] == 128)]
            news += [part for part in lanes if part.shape[1] < 128]
            for at, (old_ref, new_ref) in enumerate(sums):
                if start and index == 0:
                    old = None if old_ref is None else old_ref[g]
                else:
                    old = new_ref[g, low_row:, :]
                if at < len(news):
                    new = news[at] if old is None else old + news[at]
                else:
                    new = jnp.zeros(new_ref.shape[1:], jnp.float32) if old is None else old
                if at < len(news) or (start and index == 0):
                    new_ref[g, low_row:, :] = new


def sum_shapes(cfg, queries):
    groups, rows, cols = queries.shape
    shapes = [(groups, rows, cols), (groups, rows, 128)]
    rest = 2 * cfg["count"] % 128
    return shapes + ([(groups, rows, rest)] if cfg["layer"] == 0 and rest else [])


def attend_kernel(cfg, kinds, resume, maps_ref, query_ref, *refs):
    refs = list(refs)
    pieces = [(refs.pop(0), step, other) for step, other in kinds]
    many = len(refs) // 2 if resume else len(refs)
    olds = refs[:many] if resume else [None] * many
    sums = list(zip(olds, refs[-many:]))
    some = [(ref[...], step, other) for ref, step, other in pieces]
    attend_some(cfg, maps_ref, query_ref, some, True, sums)


def attend(cfg, maps, queries, pieces, sums=()):
    kinds = tuple((step, other) for _, step, other in pieces)
    return on_chip(
        functools.partial(attend_kernel, cfg, kinds, len(sums) > 0),
        "attend",
        [maps, queries, *[piece for piece, _, _ in pieces], *sums],
        [(shape, jnp.float32) for shape in sum_shapes(cfg, queries)],
    )


def chosen_rows(others, per_plane, place, rows):
    plane, chip = place // per_plane, place % per_plane
    result = None
    for step, ref in enumerate(others):
        value = ref[plane, rows, :].astype(jnp.float32)
        here = chip_of(step, per_plane, True) == chip
        result = value if result is None else jnp.where(here, value, result)
    return result


def second_half_kernel(cfg, kinds, many, maps_ref, query_ref, hidden_ref, gain_ref, latent_ref, *refs):
    layer, pieces, last, count = cfg["layer"], cfg["pieces"], cfg["last"], cfg["count"]
    planes, per_plane = cfg["planes"], cfg["per_plane"]
    refs = list(refs)
    olds = [refs.pop(0) for _ in range(many)]
    rows_of = {False: [refs.pop(0) for _ in range(per_plane)]}
    rows_of[True] = others = [refs.pop(0) for _ in range(per_plane)]
    mix_refs = [refs.pop(0) for _ in range(pieces)]
    param_refs = [refs.pop(0) for _ in range(pieces)]
    param_all = refs.pop(3)
    sums = list(zip(olds, [refs.pop(3) for _ in range(many)]))
    side, way, member = side_of(), lax.axis_index("head"), lax.axis_index("seq")
    members = planes * per_plane
    features, channels = hidden_ref.shape[1], latent_ref.shape[-1]
    groups, _, group_cols = query_ref.shape
    heads = group_cols // HS
    if len(kinds) <= 8:
        some = [(rows_of[other][step][...], step, other) for step, other in kinds]
        attend_some(cfg, maps_ref, query_ref, some, True, sums)
    else:
        for old, new in sums:
            new[...] = old[...]
        for buffer, other in zip(refs[-2:], (False, True)):
            for step in range(1, per_plane):
                buffer[step] = rows_of[other][step][...]

        def one_step(step, nothing):
            pair = [(refs[-2][step], step, False), (refs[-1][step], step, True)]
            attend_some(cfg, maps_ref, query_ref, pair, False, sums)
            return nothing

        lax.fori_loop(1, per_plane, one_step, 0)

    mixture = hidden_ref[...]
    bands = mixture.shape[0] // count
    head = lax.broadcasted_iota(jnp.int32, (1, group_cols), 1) // HS
    for g in range(groups):
        total = sum(jnp.sum(new[g], axis=1, keepdims=True) for _, new in sums[1:])
        share_of = 1.0 / (total + (0.0 if last else 1.0))
        number_ref = sums[0][1]
        attended = []
        for p in range(bands):
            one = jnp.zeros((count, group_cols), jnp.float32)
            for h in range(heads):
                band = slice((p * heads + h) * count, (p * heads + h + 1) * count)
                one = jnp.where(head == h, number_ref[g, band, :] * share_of[band], one)
            attended.append(one)
        rows = cat([ref[layer] for ref in mix_refs[2 * g : 2 * g + 2]], 0)
        mixture = mixture + dot(cat(attended, 0).astype(jnp.bfloat16), rows)
    spread = lax.rsqrt(jnp.mean(mixture * mixture, axis=1, keepdims=True) + epsilon)
    scaled = (mixture * spread * gain_ref[layer : layer + 1, :]).astype(jnp.bfloat16)
    share = features // pieces
    for j, ref in enumerate(param_refs):
        at = pl.multiple_of(lax.rem(way + j, pieces) * share, 16)
        param_all[pl.ds(at, share), :] = ref[layer]
    predicted = dot(scaled, param_all[...])
    shift_all = predicted[:, :channels]
    log_all = 2.0 * jnp.tanh(0.5 * predicted[:, channels:])
    token = lax.broadcasted_iota(jnp.int32, (count, 1), 0)
    if last:
        held_ref, held_log_ref, out_ref = refs[:3]
        before = member - 1 + side
        edge = chosen_rows(others, per_plane, jnp.maximum(before, 0), slice(count, count + 16))
        edge = jnp.where(before >= 0, edge[0:2] + edge[2:4] + edge[4:6], 0.0)
        edge_log = edge[1:2]
        start = pl.multiple_of(side * count, 8)
        first = (latent_ref[pl.ds(start, 8), :][:1] - edge[0:1]) * jnp.exp(-edge_log)
        values = jnp.where(token == 0, first, pltpu.roll(held_ref[...], 1, 0))
        first_log = jnp.where(token == 0, edge_log, pltpu.roll(held_log_ref[...], 1, 0))
        result = (values - shift_all) * jnp.exp(-log_all)
        term = -(first_log + log_all) - 0.5 * (result * result)
        loglik = jnp.sum(term.T, axis=0, keepdims=True) * (1.0 / channels) - 0.5 * math.log(
            2.0 * math.pi
        )
        out_ref[:count, :] = result
        out_ref[count:, :count] = jnp.broadcast_to(loglik, (8, count))
        return
    held_ref, held_log_ref, narrow_ref = refs[:3]
    own = latent_ref[pl.ds(pl.multiple_of(side * count, 8), count), :]
    for p in range(planes):
        shift_mu = shift_all[p * count : (p + 1) * count]
        log_scale = log_all[p * count : (p + 1) * count]
        following = p * per_plane + member % per_plane + side
        after = chosen_rows(others, per_plane, jnp.minimum(following, members - 1), slice(0, 16))
        here = member // per_plane == p
        values = jnp.where(here, own, rows_of[False][0][p, :count, :].astype(jnp.float32))
        values = pltpu.roll(values, count - 1, 0)
        values = jnp.where(token == count - 1, after[:1], values)
        result = (values - shift_mu) * jnp.exp(-log_scale)
        if p == planes - 1:
            result = jnp.where((following == members) & (token == count - 1), 0.0, result)

        @pl.when(here)
        def keep(result=result, log_scale=log_scale):
            held_ref[...] = result
            held_log_ref[...] = log_scale

        edge = jnp.concatenate([shift_mu[count - 1 :], log_scale[count - 1 :]], axis=0)
        terms = []
        for _ in range(3):
            terms.append(edge.astype(jnp.bfloat16).astype(jnp.float32))
            edge = edge - terms[-1]
        rest = jnp.zeros((16 - 6, channels), jnp.float32)
        narrow_ref[p, :count, :] = result.astype(jnp.bfloat16)
        narrow_ref[p, count:, :] = jnp.concatenate(terms + [rest], axis=0).astype(jnp.bfloat16)


def second_half(cfg, kinds, maps, queries, sums, hidden, param_gain, latents, mine, others, mix_pieces, param_pieces, held=()):
    count, planes, channels = cfg["count"], cfg["planes"], latents.shape[-1]
    operands = [maps, queries, hidden, param_gain, latents, *sums, *mine, *others]
    operands += [*mix_pieces, *param_pieces, *held]
    if cfg["last"]:
        results = [((count + 8, channels), jnp.float32)]
    else:
        results = [
            ((count, channels), jnp.float32),
            ((count, channels), jnp.float32),
            ((planes, count + 16, channels), jnp.bfloat16),
        ]
    scratch = [pltpu.VMEM((cfg["features"], param_pieces[0].shape[2]), jnp.bfloat16)]
    scratch += [pltpu.VMEM(one.shape, jnp.float32) for one in sums]
    if len(kinds) > 8:
        scratch += [pltpu.VMEM((len(mine), *mine[0].shape), jnp.bfloat16)] * 2
    return on_chip(
        functools.partial(second_half_kernel, cfg, kinds, len(sums)),
        "second_half",
        operands,
        results,
        scratch=scratch,
    )


def finish_kernel(own_ref, other_ref, final_ref, loglik_ref):
    count = final_ref.shape[0] // 2
    side = side_of()
    for ref, place in ((own_ref, side), (other_ref, 1 - side)):
        final_ref[pl.ds(pl.multiple_of(place * count, 8), count), :] = ref[:count, :]
    first = jnp.where(side == 0, own_ref[count : count + 1, :], other_ref[count : count + 1, :])
    second = jnp.where(side == 0, other_ref[count : count + 1, :], own_ref[count : count + 1, :])
    loglik_ref[...] = jnp.concatenate([first[:, :count], second[:, :count]], axis=1)


def body(
    latents, in_proj, query_proj, key_proj, value_proj, mix_proj, param_proj, attn_gain, param_gain
):
    members, ways = lax.axis_size("seq"), lax.axis_size("head")
    rows, channels = latents.shape
    features = in_proj.shape[2]
    count = rows // 2
    planes = 4 if members % 4 == 0 else 1
    per_plane = members // planes
    bits = per_plane.bit_length() - 1

    def swap(array):
        return lax.ppermute(array, "head", [(i, i ^ 1) for i in range(ways)])

    def pieces_of(array):
        shares = [array]
        for j in range(1, ways):
            shares.append(
                lax.ppermute(array, "head", [((i + j) % ways, i) for i in range(ways)])
            )
        return shares

    def in_plane(mine):
        arrived = []
        for step in range(1, per_plane):
            pairs = []
            for i in range(members):
                for w in range(ways):
                    to = i ^ (turned(step, bits) if w % 2 else step)
                    pairs.append((i * ways + w, to * ways + w))
            arrived.append(lax.ppermute(mine, ("seq", "head"), pairs))
        return arrived

    def run(layer, mine, sibling, maps, made, latents, *rest):
        cfg = {
            "layer": layer,
            "last": layer == 1,
            "count": count,
            "features": features,
            "pieces": ways,
            "planes": planes,
            "per_plane": per_plane,
        }
        hidden, queries = made
        arrived = in_plane(mine)
        if per_plane == 4:
            early = [(mine, 0, False)] + ([(sibling, 0, True)] if layer == 0 else [])
            sums = attend(cfg, maps, queries, early)
            first, second, *own = gate_all(arrived[:2] + ([] if layer == 0 else [mine]), sums)
            others = [sibling if layer == 0 else swap(own[0]), swap(first)]
            if layer == 0:
                others.append(swap(second))
            sums = attend(cfg, maps, queries, [(first, 1, False), (second, 2, False)], sums)
            third, *again = gate_all(arrived[2:] + ([] if layer == 0 else [second]), sums)
            if layer == 1:
                others.append(swap(again[0]))
            others.append(swap(third))
            more = [(third, 3, False)] + ([] if layer == 0 else [(others[0], 0, True)])
            sums = attend(cfg, maps, queries, more + [(others[1], 1, True)], sums)
            mines = [mine, first, second, third]
            kinds = [(2, True), (3, True)]
        else:
            others = [swap(mine) if layer == 1 else sibling]
            sums = attend(cfg, maps, queries, [(mine, 0, False), (others[0], 0, True)])
            mines = [mine]
            if per_plane > 1:
                arrived = gate_all(arrived, sums)
                mines += arrived
                others += [swap(piece) for piece in arrived]
            kinds = [(step, False) for step in range(1, per_plane)]
            kinds += [(step, True) for step in range(1, per_plane)]
        return second_half(
            cfg, tuple(kinds), maps, queries, sums, hidden, param_gain, latents, mines, others, mix_pieces, param_pieces, *rest
        )

    (rounded,) = on_chip(
        round_kernel,
        "round",
        [],
        [(latents.shape, jnp.bfloat16)],
        far=[latents],
        scratch=[pltpu.VMEM(latents.shape, jnp.float32), pltpu.SemaphoreType.DMA((1,))],
    )
    parts = [rounded] + [
        lax.ppermute(rounded, "seq", [(i, i ^ (b * per_plane)) for i in range(members)])
        for b in range(1, planes)
    ]
    mix_pieces, param_pieces = pieces_of(mix_proj), pieces_of(param_proj)
    in_all, tail, own_maps = prepare(
        in_proj, attn_gain, key_proj, value_proj, query_proj, []
    )
    shape = (planes, count, channels)
    mine, sibling, own_maps = on_chip(
        functools.partial(arrange_kernel, planes),
        "arrange",
        [*parts, own_maps],
        [(shape, jnp.bfloat16), (shape, jnp.bfloat16), (own_maps.shape, jnp.bfloat16)],
        after=mix_pieces[1:] + param_pieces[1:],
    )
    first_maps, first_query, second_maps, second_query = join(tail, pieces_of(own_maps))
    width = 2 * key_proj.shape[2]
    made = make_queries(0, planes, count, mine, in_all, first_query, width)
    held, held_log, mine = run(0, mine, sibling, first_maps, made, latents)
    made = make_queries(1, 1, count, mine, in_all, second_query, width)
    (packed,) = run(1, mine, None, second_maps, made, latents, (held, held_log))
    final_latent, token_loglik = on_chip(
        finish_kernel,
        "finish",
        [packed, swap(packed)],
        [((rows, channels), jnp.float32), ((1, rows), jnp.float32)],
        out_memory=None,
    )
    return (final_latent, token_loglik.reshape(rows))


def solution(mesh):
    placed = (
        P("seq", None),
        P(),
        P(None, None, "head"),
        P(None, None, "head"),
        P(None, None, "head"),
        P(None, "head", None),
        P(None, "head", None),
        P(),
        P(),
    )
    return jax.shard_map(
        body, mesh=mesh, in_specs=placed, out_specs=(P("seq", None), P("seq")), check_vma=False
    )
```

```python
import functools
import math

import jax
import jax.numpy as jnp
from jax import lax
from jax.experimental import pallas as pl
from jax.experimental.pallas import tpu as pltpu
from jax.sharding import PartitionSpec as P

HS = 64

score_scale = 8.0
epsilon = 1e-06

VMEM_LIMIT = 32 * 1024 * 1024


def dot(a, b):
    return jnp.dot(a, b, preferred_element_type=jnp.float32)


def dot_nt(a, b):
    return lax.dot_general(a, b, (((1,), (1,)), ((), ())), preferred_element_type=jnp.float32)


def cat(parts, axis):
    return parts[0] if len(parts) == 1 else jnp.concatenate(parts, axis=axis)


def side_of():
    return lax.rem(lax.axis_index("head"), 2)


def on_chip(kernel, name, operands, results, far=(), after=(), scratch=(), out_memory=pltpu.VMEM):
    near = [pltpu.with_memory_space_constraint(array, pltpu.VMEM) for array in operands]
    far = [pltpu.with_memory_space_constraint(array, pltpu.HBM) for array in far]
    if out_memory is pltpu.VMEM:
        out_shape = tuple(pltpu.VMEM(shape, dtype) for shape, dtype in results)
    else:
        out_shape = tuple(jax.ShapeDtypeStruct(shape, dtype) for shape, dtype in results)
    return pl.pallas_call(
        kernel,
        in_specs=[pl.BlockSpec(memory_space=pltpu.VMEM)] * len(near)
        + [pl.BlockSpec(memory_space=pl.ANY)] * (len(far) + len(after)),
        out_specs=tuple(pl.BlockSpec(memory_space=pltpu.VMEM) for _ in results),
        out_shape=out_shape,
        scratch_shapes=list(scratch),
        compiler_params=pltpu.CompilerParams(vmem_limit_bytes=VMEM_LIMIT),
        name=name,
    )(*near, *far, *after)


def fetch(sources, targets, sems):
    copies = []
    for at, (source, target) in enumerate(zip(sources, targets)):
        copies.append(pltpu.make_async_copy(source, target, sems.at[at]))
        copies[-1].start()
    return copies


def round_kernel(rows_ref, out_ref, buffer, sems):
    for copy in fetch([rows_ref], [buffer], sems):
        copy.wait()
    out_ref[...] = buffer[...].astype(jnp.bfloat16)


def arrange_kernel(planes, *refs):
    place = lax.axis_index("seq") // (lax.axis_size("seq") // planes)
    mine_ref, other_ref, maps_ref = refs[-3:]
    maps_ref[...] = refs[planes][...]
    count = mine_ref.shape[0] // planes
    for step in range(planes):
        first, second = refs[step][:count, :], refs[step][count:, :]
        at = pl.ds(pl.multiple_of((place ^ step) * count, 16), count)
        mine_ref[at, :] = jnp.where(side_of() == 0, first, second)
        other_ref[at, :] = jnp.where(side_of() == 0, second, first)


def gates_kernel(many, *refs):
    for source, target in zip(refs[:many], refs[-many:]):
        target[...] = source[...]


def gate_all(rows, made):
    results = [(piece.shape, piece.dtype) for piece in rows]
    return on_chip(functools.partial(gates_kernel, len(rows)), "gate", [*rows, *made], results)


def turned(step, bits):
    return sum(((step >> b) & 1) << (bits - 1 - b) for b in range(bits))


def chip_of(step, per_plane, other):
    bits = per_plane.bit_length() - 1
    first = side_of() == (1 if other else 0)
    return (lax.axis_index("seq") % per_plane) ^ jnp.where(first, step, turned(step, bits))


def prepare_kernel(in_src, gain_src, key_src, value_src, query_src, *refs):
    in_ref, tail_ref, maps_ref, gain_ref, buffer, sems = refs[-6:]
    layers, channels, _ = in_ref.shape
    weights = (key_src, value_src, query_src)
    sources = [in_src, gain_src] + [src.at[b] for b in range(layers) for src in weights]
    targets = [in_ref, gain_ref] + [buffer.at[b, at] for b in range(layers) for at in range(3)]
    copies = fetch(sources, targets, sems)
    for copy in copies[:2]:
        copy.wait()
    eye = lax.broadcasted_iota(jnp.int32, (channels, channels), 0) == lax.broadcasted_iota(
        jnp.int32, (channels, channels), 1
    )

    def store(ref, row, value):
        high = value.astype(jnp.bfloat16)
        rows = slice(row, row + value.shape[0])
        ref[rows, :channels] = high
        ref[rows, channels:] = (value - high.astype(jnp.float32)).astype(jnp.bfloat16)

    for layer in range(layers):
        base = in_ref[layer]
        store(tail_ref.at[layer], 0, dot_nt(base, base))
        store(tail_ref.at[layer], channels, jnp.where(eye, 1.0, 0.0))
        scaled = base.astype(jnp.float32) * gain_ref[layer : layer + 1, :]
        high = scaled.astype(jnp.bfloat16)
        low = (scaled - high.astype(jnp.float32)).astype(jnp.bfloat16)
        both = jnp.concatenate([high, low], axis=0)
        for at in range(3):
            copies[2 + 3 * layer + at].wait()
        product = dot(both, cat([buffer[layer, at] for at in range(3)], 1))
        store(maps_ref.at[layer], 0, (product[:channels] + product[channels:]).T)


def prepare(in_proj, attn_gain, key_proj, value_proj, query_proj, after):
    layers, channels, features = in_proj.shape
    columns = key_proj.shape[2]
    return on_chip(
        prepare_kernel,
        "prepare",
        [],
        [
            (in_proj.shape, jnp.bfloat16),
            ((layers, 2 * channels, 2 * channels), jnp.bfloat16),
            ((layers, 3 * columns, 2 * channels), jnp.bfloat16),
        ],
        far=[in_proj, attn_gain, key_proj, value_proj, query_proj],
        after=after,
        scratch=[
            pltpu.VMEM(attn_gain.shape, jnp.float32),
            pltpu.VMEM((layers, 3, features, columns), jnp.bfloat16),
            pltpu.SemaphoreType.DMA((2 + 3 * layers,)),
        ],
    )


def join_kernel(pieces, tail_ref, *refs):
    sources, outs = refs[:pieces], refs[pieces:]
    layers = tail_ref.shape[0]
    columns = sources[0].shape[1] // 3
    for layer in range(layers):
        maps_ref, query_ref = outs[2 * layer : 2 * layer + 2]
        total = pieces * columns
        for j, source in enumerate(sources):
            for at in range(2):
                row = at * total + j * columns
                maps_ref[row : row + columns, :] = source[layer, at * columns : (at + 1) * columns]
            query_ref[j * columns : (j + 1) * columns, :] = source[layer, 2 * columns :]
        maps_ref[2 * total :, :] = tail_ref[layer]


def join(tail, pieces):
    layers, rows, width = pieces[0].shape
    total = len(pieces) * rows // 3
    results = [((2 * total + tail.shape[1], width), jnp.bfloat16), ((total, width), jnp.bfloat16)]
    return on_chip(
        functools.partial(join_kernel, len(pieces)), "join", [tail, *pieces], results * layers
    )


def queries_kernel(layer, planes, rows_ref, in_ref, maps_ref, hidden_ref, out_ref):
    total = hidden_ref.shape[0]
    count = total // planes
    if layer == 0:
        rows = rows_ref[...]
    else:
        place = lax.axis_index("seq") // (lax.axis_size("seq") // (rows_ref.shape[0] // count))
        rows = rows_ref[pl.ds(pl.multiple_of(place * count, 16), count), :]
    hidden = dot(rows, in_ref[layer])
    hidden_ref[...] = hidden
    spread = lax.rsqrt(jnp.mean(hidden * hidden, axis=1, keepdims=True) + epsilon)
    twice = jnp.concatenate([rows, rows], axis=1)
    groups, _, width = out_ref.shape
    heads = width // HS
    head = lax.broadcasted_iota(jnp.int32, (1, width), 1) // HS
    same = head == lax.broadcasted_iota(jnp.int32, (width, 1), 0) // HS
    same = jnp.where(same, 1.0, 0.0).astype(jnp.bfloat16)
    for g in range(groups):
        query = dot_nt(twice, maps_ref[g * width : (g + 1) * width, :]) * spread
        square = query * query
        high = square.astype(jnp.bfloat16)
        low = (square - high.astype(jnp.float32)).astype(jnp.bfloat16)
        mean = (dot(high, same) + dot(low, same)) * (1.0 / HS)
        query = query * lax.rsqrt(mean + epsilon)
        for h in range(heads):
            band = jnp.where(head == h, query, 0.0).astype(jnp.bfloat16)
            for p in range(planes):
                row = (p * heads + h) * count
                out_ref[g, row : row + count, :] = band[p * count : (p + 1) * count]


def make_queries(layer, planes, count, rows, in_all, maps, width):
    return on_chip(
        functools.partial(queries_kernel, layer, planes),
        "queries",
        [rows, in_all, maps],
        [
            ((planes * count, in_all.shape[2]), jnp.float32),
            ((maps.shape[0] // width, planes * width // HS * count, width), jnp.bfloat16),
        ],
    )


def attend_some(cfg, maps_ref, query_ref, some, start, sums):
    count, features, planes, per_plane = cfg["count"], cfg["features"], cfg["planes"], cfg["per_plane"]
    layer, side = cfg["layer"], side_of()
    groups, _, group_cols = query_ref.shape
    heads = group_cols // HS
    band = heads * count
    total_cols = groups * group_cols
    stride = 2 * per_plane * count
    token = lax.broadcasted_iota(jnp.int32, (count, 1), 0)
    member = lax.axis_index("seq")
    query_place = (member % per_plane * 2 + side) * count + jnp.concatenate([token] * heads, axis=0)
    offsets = [
        (chip_of(step, per_plane, other) * 2 + (1 - side if other else side)) * count
        for _, step, other in some
    ]
    if layer == 0:
        size = len(some) * count
        lane = lax.broadcasted_iota(jnp.int32, (1, size), 1)
        key_place = lane + offsets[0]
        for at in range(1, len(some)):
            key_place = jnp.where(lane >= at * count, lane - at * count + offsets[at], key_place)
        allowed = key_place <= query_place
        parts = [
            cat([rows[p * count : (p + 1) * count] for rows, _, _ in some], 0)
            for p in range(planes)
        ]
        low_rows = [p * band for p in range(planes)]
    else:
        size = len(some) * planes * count
        lane = lax.broadcasted_iota(jnp.int32, (1, planes * count), 1)
        plane = ((lane.astype(jnp.float32) + 0.5) * (1.0 / count)).astype(jnp.int32)
        base_place = lane + plane * (stride - count)
        key_place = jnp.concatenate([base_place + offset for offset in offsets], axis=1)
        allowed = key_place >= query_place + member // per_plane * stride
        parts, low_rows = [cat([rows[: planes * count] for rows, _, _ in some], 0)], [0]

    def keys_and_values(source, g):
        low = g * group_cols
        twice = jnp.concatenate([source, source], axis=1)
        channels = source.shape[1]
        tail = dot_nt(maps_ref[2 * total_cols :, :], twice)
        square = jnp.sum(tail[:channels] * tail[channels:], axis=0, keepdims=True)
        scale = lax.rsqrt(jnp.maximum(square, 0.0) * (1.0 / features) + epsilon)
        scale_sq = scale * scale
        key = dot_nt(maps_ref[low : low + group_cols, :], twice)
        value = dot_nt(maps_ref[total_cols + low : total_cols + low + group_cols, :], twice)
        keys = []
        for h in range(heads):
            one = key[h * HS : (h + 1) * HS]
            mean = jnp.sum(one * one, axis=0, keepdims=True) * (1.0 / HS)
            factor = scale * lax.rsqrt(mean * scale_sq + epsilon) * (score_scale / HS)
            keys.append((one * factor).astype(jnp.bfloat16))
        return jnp.concatenate(keys, axis=0), (value * scale).astype(jnp.bfloat16)

    for g in range(groups):
        if size % 128 == 0 and len(parts) > 1:
            key, value = keys_and_values(cat(parts, 0), g)
            made = [
                (key[:, p * size : (p + 1) * size], value[:, p * size : (p + 1) * size])
                for p in range(len(parts))
            ]
        else:
            made = [keys_and_values(part, g) for part in parts]
        for index, ((key, value), low_row) in enumerate(zip(made, low_rows)):
            scores = dot(query_ref[g, low_row:, :], key)
            weights = jnp.exp(scores)
            first = jnp.where(allowed, weights[:band], 0.0)
            weights = first if weights.shape[0] == band else cat([first, weights[band:]], 0)
            product = dot_nt(weights.astype(jnp.bfloat16), value)
            lanes = [weights[:, at : at + 128] for at in range(0, weights.shape[1], 128)]
            news = [product, sum(part for part in lanes if part.shape[1] == 128)]
            news += [part for part in lanes if part.shape[1] < 128]
            for at, (old_ref, new_ref) in enumerate(sums):
                if start and index == 0:
                    old = None if old_ref is None else old_ref[g]
                else:
                    old = new_ref[g, low_row:, :]
                if at < len(news):
                    new = news[at] if old is None else old + news[at]
                else:
                    new = jnp.zeros(new_ref.shape[1:], jnp.float32) if old is None else old
                if at < len(news) or (start and index == 0):
                    new_ref[g, low_row:, :] = new


def sum_shapes(cfg, queries):
    groups, rows, cols = queries.shape
    shapes = [(groups, rows, cols), (groups, rows, 128)]
    rest = 2 * cfg["count"] % 128
    return shapes + ([(groups, rows, rest)] if cfg["layer"] == 0 and rest else [])


def attend_kernel(cfg, kinds, resume, maps_ref, query_ref, *refs):
    refs = list(refs)
    pieces = [(refs.pop(0), step, other) for step, other in kinds]
    many = len(refs) // 2 if resume else len(refs)
    olds = refs[:many] if resume else [None] * many
    sums = list(zip(olds, refs[-many:]))
    some = [(ref[...], step, other) for ref, step, other in pieces]
    attend_some(cfg, maps_ref, query_ref, some, True, sums)


def attend(cfg, maps, queries, pieces, sums=()):
    kinds = tuple((step, other) for _, step, other in pieces)
    return on_chip(
        functools.partial(attend_kernel, cfg, kinds, len(sums) > 0),
        "attend",
        [maps, queries, *[piece for piece, _, _ in pieces], *sums],
        [(shape, jnp.float32) for shape in sum_shapes(cfg, queries)],
    )


def chosen_rows(others, per_plane, chip, start):
    result = None
    for step, ref in enumerate(others):
        value = ref[pl.ds(start, 16), :].astype(jnp.float32)
        here = chip_of(step, per_plane, True) == chip
        result = value if result is None else jnp.where(here, value, result)
    return result


def second_half_kernel(cfg, kinds, many, maps_ref, query_ref, hidden_ref, gain_ref, latent_ref, *refs):
    layer, pieces, last, count = cfg["layer"], cfg["pieces"], cfg["last"], cfg["count"]
    planes, per_plane = cfg["planes"], cfg["per_plane"]
    refs = list(refs)
    olds = [refs.pop(0) for _ in range(many)]
    rows_of = {False: [refs.pop(0) for _ in range(per_plane)]}
    rows_of[True] = others = [refs.pop(0) for _ in range(per_plane)]
    mix_refs = [refs.pop(0) for _ in range(pieces)]
    param_refs = [refs.pop(0) for _ in range(pieces)]
    param_all = refs.pop(3)
    sums = list(zip(olds, [refs.pop(3) for _ in range(many)]))
    side, way, member = side_of(), lax.axis_index("head"), lax.axis_index("seq")
    members = planes * per_plane
    features, channels = hidden_ref.shape[1], latent_ref.shape[-1]
    groups, _, group_cols = query_ref.shape
    heads = group_cols // HS
    if len(kinds) <= 8:
        some = [(rows_of[other][step][...], step, other) for step, other in kinds]
        attend_some(cfg, maps_ref, query_ref, some, True, sums)
    else:
        for old, new in sums:
            new[...] = old[...]
        for buffer, other in zip(refs[-2:], (False, True)):
            for step in range(1, per_plane):
                buffer[step] = rows_of[other][step][...]

        def one_step(step, nothing):
            pair = [(refs[-2][step], step, False), (refs[-1][step], step, True)]
            attend_some(cfg, maps_ref, query_ref, pair, False, sums)
            return nothing

        lax.fori_loop(1, per_plane, one_step, 0)

    mixture = hidden_ref[...]
    bands = mixture.shape[0] // count
    head = lax.broadcasted_iota(jnp.int32, (1, group_cols), 1) // HS
    for g in range(groups):
        total = sum(jnp.sum(new[g], axis=1, keepdims=True) for _, new in sums[1:])
        share_of = 1.0 / (total + (0.0 if last else 1.0))
        number_ref = sums[0][1]
        attended = []
        for p in range(bands):
            one = jnp.zeros((count, group_cols), jnp.float32)
            for h in range(heads):
                band = slice((p * heads + h) * count, (p * heads + h + 1) * count)
                one = jnp.where(head == h, number_ref[g, band, :] * share_of[band], one)
            attended.append(one)
        rows = cat([ref[layer] for ref in mix_refs[2 * g : 2 * g + 2]], 0)
        mixture = mixture + dot(cat(attended, 0).astype(jnp.bfloat16), rows)
    spread = lax.rsqrt(jnp.mean(mixture * mixture, axis=1, keepdims=True) + epsilon)
    scaled = (mixture * spread * gain_ref[layer : layer + 1, :]).astype(jnp.bfloat16)
    share = features // pieces
    for j, ref in enumerate(param_refs):
        at = pl.multiple_of(lax.rem(way + j, pieces) * share, 16)
        param_all[pl.ds(at, share), :] = ref[layer]
    predicted = dot(scaled, param_all[...])
    shift_all = predicted[:, :channels]
    log_all = 2.0 * jnp.tanh(0.5 * predicted[:, channels:])
    token = lax.broadcasted_iota(jnp.int32, (count, 1), 0)
    if last:
        held_ref, held_log_ref, out_ref = refs[:3]
        before = member - 1 + side
        chip = (before + per_plane) % per_plane
        edge = chosen_rows(others, per_plane, chip, planes * count)
        edge = jnp.where(before >= 0, edge[0:2] + edge[2:4] + edge[4:6], 0.0)
        edge_log = edge[1:2]
        start = pl.multiple_of(side * count, 8)
        first = (latent_ref[pl.ds(start, 8), :][:1] - edge[0:1]) * jnp.exp(-edge_log)
        values = jnp.where(token == 0, first, pltpu.roll(held_ref[...], 1, 0))
        first_log = jnp.where(token == 0, edge_log, pltpu.roll(held_log_ref[...], 1, 0))
        result = (values - shift_all) * jnp.exp(-log_all)
        term = -(first_log + log_all) - 0.5 * (result * result)
        loglik = jnp.sum(term.T, axis=0, keepdims=True) * (1.0 / channels) - 0.5 * math.log(
            2.0 * math.pi
        )
        out_ref[:count, :] = result
        out_ref[count:, :count] = jnp.broadcast_to(loglik, (8, count))
        return
    held_ref, held_log_ref, narrow_ref = refs[:3]
    narrow_ref[planes * count :, :] = jnp.zeros((16, channels), jnp.bfloat16)
    own = latent_ref[pl.ds(pl.multiple_of(side * count, 8), count), :]
    for p in range(planes):
        shift_mu = shift_all[p * count : (p + 1) * count]
        log_scale = log_all[p * count : (p + 1) * count]
        following = p * per_plane + member % per_plane + side
        following_row = pl.multiple_of(jnp.minimum(following, members - 1) // per_plane * count, 16)
        after = chosen_rows(others, per_plane, following % per_plane, following_row)
        here = member // per_plane == p
        rows = rows_of[False][0][p * count : (p + 1) * count, :]
        values = jnp.where(here, own, rows.astype(jnp.float32))
        values = pltpu.roll(values, count - 1, 0)
        values = jnp.where(token == count - 1, after[:1], values)
        result = (values - shift_mu) * jnp.exp(-log_scale)
        if p == planes - 1:
            result = jnp.where((following == members) & (token == count - 1), 0.0, result)

        @pl.when(here)
        def keep(result=result, log_scale=log_scale):
            held_ref[...] = result
            held_log_ref[...] = log_scale

        narrow_ref[p * count : (p + 1) * count, :] = result.astype(jnp.bfloat16)

        @pl.when(member // per_plane - (member % per_plane + side) // per_plane == p)
        def send(shift_mu=shift_mu, log_scale=log_scale):
            edge = jnp.concatenate([shift_mu[count - 1 :], log_scale[count - 1 :]], axis=0)
            terms = []
            for _ in range(3):
                terms.append(edge.astype(jnp.bfloat16).astype(jnp.float32))
                edge = edge - terms[-1]
            rest = jnp.zeros((16 - 6, channels), jnp.float32)
            rows = jnp.concatenate(terms + [rest], axis=0)
            narrow_ref[planes * count :, :] = rows.astype(jnp.bfloat16)


def second_half(cfg, kinds, maps, queries, sums, hidden, param_gain, latents, mine, others, mix_pieces, param_pieces, held=()):
    count, planes, channels = cfg["count"], cfg["planes"], latents.shape[-1]
    operands = [maps, queries, hidden, param_gain, latents, *sums, *mine, *others]
    operands += [*mix_pieces, *param_pieces, *held]
    if cfg["last"]:
        results = [((count + 8, channels), jnp.float32)]
    else:
        results = [
            ((count, channels), jnp.float32),
            ((count, channels), jnp.float32),
            ((planes * count + 16, channels), jnp.bfloat16),
        ]
    scratch = [pltpu.VMEM((cfg["features"], param_pieces[0].shape[2]), jnp.bfloat16)]
    scratch += [pltpu.VMEM(one.shape, jnp.float32) for one in sums]
    if len(kinds) > 8:
        scratch += [pltpu.VMEM((len(mine), *mine[0].shape), jnp.bfloat16)] * 2
    return on_chip(
        functools.partial(second_half_kernel, cfg, kinds, len(sums)),
        "second_half",
        operands,
        results,
        scratch=scratch,
    )


def finish_kernel(own_ref, other_ref, final_ref, loglik_ref):
    count = final_ref.shape[0] // 2
    side = side_of()
    for ref, place in ((own_ref, side), (other_ref, 1 - side)):
        final_ref[pl.ds(pl.multiple_of(place * count, 8), count), :] = ref[:count, :]
    first = jnp.where(side == 0, own_ref[count : count + 1, :], other_ref[count : count + 1, :])
    second = jnp.where(side == 0, other_ref[count : count + 1, :], own_ref[count : count + 1, :])
    loglik_ref[...] = jnp.concatenate([first[:, :count], second[:, :count]], axis=1)


def body(
    latents, in_proj, query_proj, key_proj, value_proj, mix_proj, param_proj, attn_gain, param_gain
):
    members, ways = lax.axis_size("seq"), lax.axis_size("head")
    rows, channels = latents.shape
    features = in_proj.shape[2]
    count = rows // 2
    planes = 4 if members % 4 == 0 else 1
    per_plane = members // planes
    bits = per_plane.bit_length() - 1

    def swap(array):
        return lax.ppermute(array, "head", [(i, i ^ 1) for i in range(ways)])

    def pieces_of(array):
        shares = [array]
        for j in range(1, ways):
            shares.append(
                lax.ppermute(array, "head", [((i + j) % ways, i) for i in range(ways)])
            )
        return shares

    def in_plane(mine):
        arrived = []
        for step in range(1, per_plane):
            pairs = []
            for i in range(members):
                for w in range(ways):
                    to = i ^ (turned(step, bits) if w % 2 else step)
                    pairs.append((i * ways + w, to * ways + w))
            arrived.append(lax.ppermute(mine, ("seq", "head"), pairs))
        return arrived

    def run(layer, mine, sibling, maps, made, latents, *rest):
        cfg = {
            "layer": layer,
            "last": layer == 1,
            "count": count,
            "features": features,
            "pieces": ways,
            "planes": planes,
            "per_plane": per_plane,
        }
        hidden, queries = made
        arrived = in_plane(mine)
        if per_plane == 4:
            one, two, three = (1, 2, 3)
            if layer == 1:
                sibling = swap(mine)
            others = {0: sibling}
            early = [(mine, 0, False)] + [(sibling, 0, True)]
            sums = attend(cfg, maps, queries, early)
            mines = {0: mine}
            mines[one], mines[two] = gate_all([arrived[one - 1], arrived[two - 1]], sums)
            others[one] = swap(mines[one])
            others[two] = swap(mines[two])
            batch = [(mines[one], one, False), (mines[two], two, False)]
            sums = attend(cfg, maps, queries, batch, sums)
            (mines[three],) = gate_all([arrived[three - 1]], sums)
            others[three] = swap(mines[three])
            batch = [(mines[three], three, False), (others[one], one, True)]
            sums = attend(cfg, maps, queries, batch, sums)
            kinds = [(two, True), (three, True)]
            mines, others = [[each[step] for step in range(4)] for each in (mines, others)]
        else:
            others = [swap(mine) if layer == 1 else sibling]
            sums = attend(cfg, maps, queries, [(mine, 0, False), (others[0], 0, True)])
            mines = [mine]
            if per_plane > 1:
                arrived = gate_all(arrived, sums)
                mines += arrived
                others += [swap(piece) for piece in arrived]
            kinds = [(step, False) for step in range(1, per_plane)]
            kinds += [(step, True) for step in range(1, per_plane)]
        return second_half(
            cfg, tuple(kinds), maps, queries, sums, hidden, param_gain, latents, mines, others, mix_pieces, param_pieces, *rest
        )

    (rounded,) = on_chip(
        round_kernel,
        "round",
        [],
        [(latents.shape, jnp.bfloat16)],
        far=[latents],
        scratch=[pltpu.VMEM(latents.shape, jnp.float32), pltpu.SemaphoreType.DMA((1,))],
    )
    parts = [rounded] + [
        lax.ppermute(rounded, "seq", [(i, i ^ (b * per_plane)) for i in range(members)])
        for b in range(1, planes)
    ]
    mix_pieces, param_pieces = pieces_of(mix_proj), pieces_of(param_proj)
    in_all, tail, own_maps = prepare(
        in_proj, attn_gain, key_proj, value_proj, query_proj, []
    )
    shape = (planes * count, channels)
    mine, sibling, own_maps = on_chip(
        functools.partial(arrange_kernel, planes),
        "arrange",
        [*parts, own_maps],
        [(shape, jnp.bfloat16), (shape, jnp.bfloat16), (own_maps.shape, jnp.bfloat16)],
        after=mix_pieces[1:] + param_pieces[1:],
    )
    first_maps, first_query, second_maps, second_query = join(tail, pieces_of(own_maps))
    width = 2 * key_proj.shape[2]
    made = make_queries(0, planes, count, mine, in_all, first_query, width)
    held, held_log, mine = run(0, mine, sibling, first_maps, made, latents)
    made = make_queries(1, 1, count, mine, in_all, second_query, width)
    (packed,) = run(1, mine, None, second_maps, made, latents, (held, held_log))
    final_latent, token_loglik = on_chip(
        finish_kernel,
        "finish",
        [packed, swap(packed)],
        [((rows, channels), jnp.float32), ((1, rows), jnp.float32)],
        out_memory=None,
    )
    return (final_latent, token_loglik.reshape(rows))


def solution(mesh):
    placed = (
        P("seq", None),
        P(),
        P(None, None, "head"),
        P(None, None, "head"),
        P(None, None, "head"),
        P(None, "head", None),
        P(None, "head", None),
        P(),
        P(),
    )
    return jax.shard_map(
        body, mesh=mesh, in_specs=placed, out_specs=(P("seq", None), P("seq")), check_vma=False
    )
```

```python
import functools
import math

import jax
import jax.numpy as jnp
from jax import lax
from jax.experimental import pallas as pl
from jax.experimental.pallas import tpu as pltpu
from jax.sharding import PartitionSpec as P

HS = 64

score_scale = 8.0
epsilon = 1e-06

VMEM_LIMIT = 32 * 1024 * 1024


def dot(a, b):
    return jnp.dot(a, b, preferred_element_type=jnp.float32)


def dot_nt(a, b):
    return lax.dot_general(a, b, (((1,), (1,)), ((), ())), preferred_element_type=jnp.float32)


def cat(parts, axis):
    return parts[0] if len(parts) == 1 else jnp.concatenate(parts, axis=axis)


def side_of():
    return lax.rem(lax.axis_index("head"), 2)


def on_chip(kernel, name, operands, results, far=(), after=(), scratch=(), out_memory=pltpu.VMEM):
    near = [pltpu.with_memory_space_constraint(array, pltpu.VMEM) for array in operands]
    far = [pltpu.with_memory_space_constraint(array, pltpu.HBM) for array in far]
    if out_memory is pltpu.VMEM:
        out_shape = tuple(pltpu.VMEM(shape, dtype) for shape, dtype in results)
    else:
        out_shape = tuple(jax.ShapeDtypeStruct(shape, dtype) for shape, dtype in results)
    return pl.pallas_call(
        kernel,
        in_specs=[pl.BlockSpec(memory_space=pltpu.VMEM)] * len(near)
        + [pl.BlockSpec(memory_space=pl.ANY)] * (len(far) + len(after)),
        out_specs=tuple(pl.BlockSpec(memory_space=pltpu.VMEM) for _ in results),
        out_shape=out_shape,
        scratch_shapes=list(scratch),
        compiler_params=pltpu.CompilerParams(vmem_limit_bytes=VMEM_LIMIT),
        name=name,
    )(*near, *far, *after)


def fetch(sources, targets, sems):
    copies = []
    for at, (source, target) in enumerate(zip(sources, targets)):
        copies.append(pltpu.make_async_copy(source, target, sems.at[at]))
        copies[-1].start()
    return copies


def round_kernel(rows_ref, out_ref, buffer, sems):
    for copy in fetch([rows_ref], [buffer], sems):
        copy.wait()
    out_ref[...] = buffer[...].astype(jnp.bfloat16)


def arrange_kernel(planes, *refs):
    place = lax.axis_index("seq") // (lax.axis_size("seq") // planes)
    mine_ref, other_ref, maps_ref = refs[-3:]
    maps_ref[...] = refs[planes][...]
    count = mine_ref.shape[0] // planes
    for step in range(planes):
        first, second = refs[step][:count, :], refs[step][count:, :]
        at = pl.ds(pl.multiple_of((place ^ step) * count, 16), count)
        mine_ref[at, :] = jnp.where(side_of() == 0, first, second)
        other_ref[at, :] = jnp.where(side_of() == 0, second, first)


def gates_kernel(many, *refs):
    for source, target in zip(refs[:many], refs[-many:]):
        target[...] = source[...]


def stack_kernel(one_ref, two_ref, *refs):
    rows = one_ref.shape[0]
    for source, target, at in ((one_ref, refs[-3], 0), (two_ref, refs[-2], rows)):
        target[...] = source[...]
        refs[-1][at : at + rows, :] = source[...]


def stack(one, two, made):
    rows, channels = one.shape
    shapes = [(rows, channels), (rows, channels), (2 * rows, channels)]
    results = [(shape, one.dtype) for shape in shapes]
    return on_chip(stack_kernel, "stack", [one, two, *made], results)


def unstack_kernel(both_ref, one_ref, two_ref):
    rows = one_ref.shape[0]
    one_ref[...] = both_ref[:rows, :]
    two_ref[...] = both_ref[rows:, :]


def unstack(both):
    shape = (both.shape[0] // 2, both.shape[1])
    return on_chip(unstack_kernel, "unstack", [both], [(shape, both.dtype)] * 2)


def gate_all(rows, made):
    results = [(piece.shape, piece.dtype) for piece in rows]
    return on_chip(functools.partial(gates_kernel, len(rows)), "gate", [*rows, *made], results)


def turned(step, bits):
    return sum(((step >> b) & 1) << (bits - 1 - b) for b in range(bits))


def chip_of(step, per_plane, other):
    bits = per_plane.bit_length() - 1
    first = side_of() == (1 if other else 0)
    return (lax.axis_index("seq") % per_plane) ^ jnp.where(first, step, turned(step, bits))


def prepare_kernel(in_src, gain_src, key_src, value_src, query_src, *refs):
    in_ref, tail_ref, maps_ref, gain_ref, buffer, sems = refs[-6:]
    layers, channels, _ = in_ref.shape
    weights = (key_src, value_src, query_src)
    sources = [in_src, gain_src] + [src.at[b] for b in range(layers) for src in weights]
    targets = [in_ref, gain_ref] + [buffer.at[b, at] for b in range(layers) for at in range(3)]
    copies = fetch(sources, targets, sems)
    for copy in copies[:2]:
        copy.wait()
    eye = lax.broadcasted_iota(jnp.int32, (channels, channels), 0) == lax.broadcasted_iota(
        jnp.int32, (channels, channels), 1
    )

    def store(ref, row, value):
        high = value.astype(jnp.bfloat16)
        rows = slice(row, row + value.shape[0])
        ref[rows, :channels] = high
        ref[rows, channels:] = (value - high.astype(jnp.float32)).astype(jnp.bfloat16)

    for layer in range(layers):
        base = in_ref[layer]
        store(tail_ref.at[layer], 0, dot_nt(base, base))
        store(tail_ref.at[layer], channels, jnp.where(eye, 1.0, 0.0))
        scaled = base.astype(jnp.float32) * gain_ref[layer : layer + 1, :]
        high = scaled.astype(jnp.bfloat16)
        low = (scaled - high.astype(jnp.float32)).astype(jnp.bfloat16)
        both = jnp.concatenate([high, low], axis=0)
        for at in range(3):
            copies[2 + 3 * layer + at].wait()
        product = dot(both, cat([buffer[layer, at] for at in range(3)], 1))
        store(maps_ref.at[layer], 0, (product[:channels] + product[channels:]).T)


def prepare(in_proj, attn_gain, key_proj, value_proj, query_proj, after):
    layers, channels, features = in_proj.shape
    columns = key_proj.shape[2]
    return on_chip(
        prepare_kernel,
        "prepare",
        [],
        [
            (in_proj.shape, jnp.bfloat16),
            ((layers, 2 * channels, 2 * channels), jnp.bfloat16),
            ((layers, 3 * columns, 2 * channels), jnp.bfloat16),
        ],
        far=[in_proj, attn_gain, key_proj, value_proj, query_proj],
        after=after,
        scratch=[
            pltpu.VMEM(attn_gain.shape, jnp.float32),
            pltpu.VMEM((layers, 3, features, columns), jnp.bfloat16),
            pltpu.SemaphoreType.DMA((2 + 3 * layers,)),
        ],
    )


def join_kernel(pieces, tail_ref, *refs):
    sources, outs = refs[:pieces], refs[pieces:]
    layers = tail_ref.shape[0]
    columns = sources[0].shape[1] // 3
    for layer in range(layers):
        maps_ref, query_ref = outs[2 * layer : 2 * layer + 2]
        total = pieces * columns
        for j, source in enumerate(sources):
            for at in range(2):
                row = at * total + j * columns
                maps_ref[row : row + columns, :] = source[layer, at * columns : (at + 1) * columns]
            query_ref[j * columns : (j + 1) * columns, :] = source[layer, 2 * columns :]
        maps_ref[2 * total :, :] = tail_ref[layer]


def join(tail, pieces):
    layers, rows, width = pieces[0].shape
    total = len(pieces) * rows // 3
    results = [((2 * total + tail.shape[1], width), jnp.bfloat16), ((total, width), jnp.bfloat16)]
    return on_chip(
        functools.partial(join_kernel, len(pieces)), "join", [tail, *pieces], results * layers
    )


def queries_kernel(layer, planes, rows_ref, in_ref, maps_ref, hidden_ref, out_ref):
    total = hidden_ref.shape[0]
    count = total // planes
    if layer == 0:
        rows = rows_ref[...]
    else:
        place = lax.axis_index("seq") // (lax.axis_size("seq") // (rows_ref.shape[0] // count))
        rows = rows_ref[pl.ds(pl.multiple_of(place * count, 16), count), :]
    hidden = dot(rows, in_ref[layer])
    hidden_ref[...] = hidden
    spread = lax.rsqrt(jnp.mean(hidden * hidden, axis=1, keepdims=True) + epsilon)
    twice = jnp.concatenate([rows, rows], axis=1)
    groups, _, width = out_ref.shape
    heads = width // HS
    head = lax.broadcasted_iota(jnp.int32, (1, width), 1) // HS
    same = head == lax.broadcasted_iota(jnp.int32, (width, 1), 0) // HS
    same = jnp.where(same, 1.0, 0.0).astype(jnp.bfloat16)
    for g in range(groups):
        query = dot_nt(twice, maps_ref[g * width : (g + 1) * width, :]) * spread
        square = query * query
        high = square.astype(jnp.bfloat16)
        low = (square - high.astype(jnp.float32)).astype(jnp.bfloat16)
        mean = (dot(high, same) + dot(low, same)) * (1.0 / HS)
        query = query * lax.rsqrt(mean + epsilon)
        for h in range(heads):
            band = jnp.where(head == h, query, 0.0).astype(jnp.bfloat16)
            for p in range(planes):
                row = (p * heads + h) * count
                out_ref[g, row : row + count, :] = band[p * count : (p + 1) * count]


def make_queries(layer, planes, count, rows, in_all, maps, width):
    return on_chip(
        functools.partial(queries_kernel, layer, planes),
        "queries",
        [rows, in_all, maps],
        [
            ((planes * count, in_all.shape[2]), jnp.float32),
            ((maps.shape[0] // width, planes * width // HS * count, width), jnp.bfloat16),
        ],
    )


def attend_some(cfg, maps_ref, query_ref, some, start, sums):
    count, features, planes, per_plane = cfg["count"], cfg["features"], cfg["planes"], cfg["per_plane"]
    layer, side = cfg["layer"], side_of()
    groups, _, group_cols = query_ref.shape
    heads = group_cols // HS
    band = heads * count
    total_cols = groups * group_cols
    stride = 2 * per_plane * count
    token = lax.broadcasted_iota(jnp.int32, (count, 1), 0)
    member = lax.axis_index("seq")
    query_place = (member % per_plane * 2 + side) * count + jnp.concatenate([token] * heads, axis=0)
    offsets = [
        (chip_of(step, per_plane, other) * 2 + (1 - side if other else side)) * count
        for _, step, other in some
    ]
    if layer == 0:
        size = len(some) * count
        lane = lax.broadcasted_iota(jnp.int32, (1, size), 1)
        key_place = lane + offsets[0]
        for at in range(1, len(some)):
            key_place = jnp.where(lane >= at * count, lane - at * count + offsets[at], key_place)
        allowed = key_place <= query_place
        parts = [
            cat([rows[p * count : (p + 1) * count] for rows, _, _ in some], 0)
            for p in range(planes)
        ]
        low_rows = [p * band for p in range(planes)]
    else:
        size = len(some) * planes * count
        lane = lax.broadcasted_iota(jnp.int32, (1, planes * count), 1)
        plane = ((lane.astype(jnp.float32) + 0.5) * (1.0 / count)).astype(jnp.int32)
        base_place = lane + plane * (stride - count)
        key_place = jnp.concatenate([base_place + offset for offset in offsets], axis=1)
        allowed = key_place >= query_place + member // per_plane * stride
        parts, low_rows = [cat([rows[: planes * count] for rows, _, _ in some], 0)], [0]

    def keys_and_values(source, g):
        low = g * group_cols
        twice = jnp.concatenate([source, source], axis=1)
        channels = source.shape[1]
        tail = dot_nt(maps_ref[2 * total_cols :, :], twice)
        square = jnp.sum(tail[:channels] * tail[channels:], axis=0, keepdims=True)
        scale = lax.rsqrt(jnp.maximum(square, 0.0) * (1.0 / features) + epsilon)
        scale_sq = scale * scale
        key = dot_nt(maps_ref[low : low + group_cols, :], twice)
        value = dot_nt(maps_ref[total_cols + low : total_cols + low + group_cols, :], twice)
        keys = []
        for h in range(heads):
            one = key[h * HS : (h + 1) * HS]
            mean = jnp.sum(one * one, axis=0, keepdims=True) * (1.0 / HS)
            factor = scale * lax.rsqrt(mean * scale_sq + epsilon) * (score_scale / HS)
            keys.append((one * factor).astype(jnp.bfloat16))
        return jnp.concatenate(keys, axis=0), (value * scale).astype(jnp.bfloat16)

    for g in range(groups):
        if size % 128 == 0 and len(parts) > 1:
            key, value = keys_and_values(cat(parts, 0), g)
            made = [
                (key[:, p * size : (p + 1) * size], value[:, p * size : (p + 1) * size])
                for p in range(len(parts))
            ]
        else:
            made = [keys_and_values(part, g) for part in parts]
        for index, ((key, value), low_row) in enumerate(zip(made, low_rows)):
            scores = dot(query_ref[g, low_row:, :], key)
            weights = jnp.exp(scores)
            first = jnp.where(allowed, weights[:band], 0.0)
            weights = first if weights.shape[0] == band else cat([first, weights[band:]], 0)
            product = dot_nt(weights.astype(jnp.bfloat16), value)
            lanes = [weights[:, at : at + 128] for at in range(0, weights.shape[1], 128)]
            news = [product, sum(part for part in lanes if part.shape[1] == 128)]
            news += [part for part in lanes if part.shape[1] < 128]
            for at, (old_ref, new_ref) in enumerate(sums):
                if start and index == 0:
                    old = None if old_ref is None else old_ref[g]
                else:
                    old = new_ref[g, low_row:, :]
                if at < len(news):
                    new = news[at] if old is None else old + news[at]
                else:
                    new = jnp.zeros(new_ref.shape[1:], jnp.float32) if old is None else old
                if at < len(news) or (start and index == 0):
                    new_ref[g, low_row:, :] = new


def sum_shapes(cfg, queries):
    groups, rows, cols = queries.shape
    shapes = [(groups, rows, cols), (groups, rows, 128)]
    rest = 2 * cfg["count"] % 128
    return shapes + ([(groups, rows, rest)] if cfg["layer"] == 0 and rest else [])


def attend_kernel(cfg, kinds, resume, maps_ref, query_ref, *refs):
    refs = list(refs)
    pieces = [(refs.pop(0), step, other) for step, other in kinds]
    many = len(refs) // 2 if resume else len(refs)
    olds = refs[:many] if resume else [None] * many
    sums = list(zip(olds, refs[-many:]))
    some = [(ref[...], step, other) for ref, step, other in pieces]
    attend_some(cfg, maps_ref, query_ref, some, True, sums)


def attend(cfg, maps, queries, pieces, sums=()):
    kinds = tuple((step, other) for _, step, other in pieces)
    return on_chip(
        functools.partial(attend_kernel, cfg, kinds, len(sums) > 0),
        "attend",
        [maps, queries, *[piece for piece, _, _ in pieces], *sums],
        [(shape, jnp.float32) for shape in sum_shapes(cfg, queries)],
    )


def chosen_rows(others, per_plane, chip, start):
    result = None
    for step, ref in enumerate(others):
        value = ref[pl.ds(start, 16), :].astype(jnp.float32)
        here = chip_of(step, per_plane, True) == chip
        result = value if result is None else jnp.where(here, value, result)
    return result


def second_half_kernel(cfg, kinds, many, maps_ref, query_ref, hidden_ref, gain_ref, latent_ref, *refs):
    layer, pieces, last, count = cfg["layer"], cfg["pieces"], cfg["last"], cfg["count"]
    planes, per_plane = cfg["planes"], cfg["per_plane"]
    refs = list(refs)
    olds = [refs.pop(0) for _ in range(many)]
    rows_of = {False: [refs.pop(0) for _ in range(per_plane)]}
    rows_of[True] = others = [refs.pop(0) for _ in range(per_plane)]
    mix_refs = [refs.pop(0) for _ in range(pieces)]
    param_refs = [refs.pop(0) for _ in range(pieces)]
    param_all = refs.pop(3)
    sums = list(zip(olds, [refs.pop(3) for _ in range(many)]))
    side, way, member = side_of(), lax.axis_index("head"), lax.axis_index("seq")
    members = planes * per_plane
    features, channels = hidden_ref.shape[1], latent_ref.shape[-1]
    groups, _, group_cols = query_ref.shape
    heads = group_cols // HS
    if len(kinds) <= 8:
        some = [(rows_of[other][step][...], step, other) for step, other in kinds]
        attend_some(cfg, maps_ref, query_ref, some, True, sums)
    else:
        for old, new in sums:
            new[...] = old[...]
        for buffer, other in zip(refs[-2:], (False, True)):
            for step in range(1, per_plane):
                buffer[step] = rows_of[other][step][...]

        def one_step(step, nothing):
            pair = [(refs[-2][step], step, False), (refs[-1][step], step, True)]
            attend_some(cfg, maps_ref, query_ref, pair, False, sums)
            return nothing

        lax.fori_loop(1, per_plane, one_step, 0)

    share = features // pieces
    for j, ref in enumerate(param_refs):
        at = pl.multiple_of(lax.rem(way + j, pieces) * share, 16)
        param_all[pl.ds(at, share), :] = ref[layer]
    mixture = hidden_ref[...]
    bands = mixture.shape[0] // count
    head = lax.broadcasted_iota(jnp.int32, (1, group_cols), 1) // HS
    for g in range(groups):
        total = sum(jnp.sum(new[g], axis=1, keepdims=True) for _, new in sums[1:])
        share_of = 1.0 / (total + (0.0 if last else 1.0))
        number_ref = sums[0][1]
        attended = []
        for p in range(bands):
            one = jnp.zeros((count, group_cols), jnp.float32)
            for h in range(heads):
                band = slice((p * heads + h) * count, (p * heads + h + 1) * count)
                one = jnp.where(head == h, number_ref[g, band, :] * share_of[band], one)
            attended.append(one)
        rows = cat([ref[layer] for ref in mix_refs[2 * g : 2 * g + 2]], 0)
        mixture = mixture + dot(cat(attended, 0).astype(jnp.bfloat16), rows)
    spread = lax.rsqrt(jnp.mean(mixture * mixture, axis=1, keepdims=True) + epsilon)
    scaled = (mixture * gain_ref[layer : layer + 1, :]).astype(jnp.bfloat16)
    predicted = dot(scaled, param_all[...]) * spread
    shift_all = predicted[:, :channels]
    log_all = 2.0 * jnp.tanh(0.5 * predicted[:, channels:])
    token = lax.broadcasted_iota(jnp.int32, (count, 1), 0)
    if last:
        held_ref, held_log_ref, out_ref = refs[:3]
        before = member - 1 + side
        chip = (before + per_plane) % per_plane
        edge = chosen_rows(others, per_plane, chip, planes * count)
        edge = jnp.where(before >= 0, edge[0:2] + edge[2:4] + edge[4:6], 0.0)
        edge_log = edge[1:2]
        start = pl.multiple_of(side * count, 8)
        first = (latent_ref[pl.ds(start, 8), :][:1] - edge[0:1]) * jnp.exp(-edge_log)
        values = jnp.where(token == 0, first, pltpu.roll(held_ref[...], 1, 0))
        first_log = jnp.where(token == 0, edge_log, pltpu.roll(held_log_ref[...], 1, 0))
        result = (values - shift_all) * jnp.exp(-log_all)
        term = -(first_log + log_all) - 0.5 * (result * result)
        loglik = jnp.sum(term.T, axis=0, keepdims=True) * (1.0 / channels) - 0.5 * math.log(
            2.0 * math.pi
        )
        out_ref[:count, :] = result
        out_ref[count:, :count] = jnp.broadcast_to(loglik, (8, count))
        return
    held_ref, held_log_ref, narrow_ref = refs[:3]
    narrow_ref[planes * count :, :] = jnp.zeros((16, channels), jnp.bfloat16)
    own = latent_ref[pl.ds(pl.multiple_of(side * count, 8), count), :]
    for p in range(planes):
        shift_mu = shift_all[p * count : (p + 1) * count]
        log_scale = log_all[p * count : (p + 1) * count]
        following = p * per_plane + member % per_plane + side
        following_row = pl.multiple_of(jnp.minimum(following, members - 1) // per_plane * count, 16)
        after = chosen_rows(others, per_plane, following % per_plane, following_row)
        here = member // per_plane == p
        rows = rows_of[False][0][p * count : (p + 1) * count, :]
        values = jnp.where(here, own, rows.astype(jnp.float32))
        values = pltpu.roll(values, count - 1, 0)
        values = jnp.where(token == count - 1, after[:1], values)
        result = (values - shift_mu) * jnp.exp(-log_scale)
        if p == planes - 1:
            result = jnp.where((following == members) & (token == count - 1), 0.0, result)

        @pl.when(here)
        def keep(result=result, log_scale=log_scale):
            held_ref[...] = result
            held_log_ref[...] = log_scale

        narrow_ref[p * count : (p + 1) * count, :] = result.astype(jnp.bfloat16)

        @pl.when(member // per_plane - (member % per_plane + side) // per_plane == p)
        def send(shift_mu=shift_mu, log_scale=log_scale):
            edge = jnp.concatenate([shift_mu[count - 1 :], log_scale[count - 1 :]], axis=0)
            terms = []
            for _ in range(3):
                terms.append(edge.astype(jnp.bfloat16).astype(jnp.float32))
                edge = edge - terms[-1]
            rest = jnp.zeros((16 - 6, channels), jnp.float32)
            rows = jnp.concatenate(terms + [rest], axis=0)
            narrow_ref[planes * count :, :] = rows.astype(jnp.bfloat16)


def second_half(cfg, kinds, maps, queries, sums, hidden, param_gain, latents, mine, others, mix_pieces, param_pieces, held=()):
    count, planes, channels = cfg["count"], cfg["planes"], latents.shape[-1]
    operands = [maps, queries, hidden, param_gain, latents, *sums, *mine, *others]
    operands += [*mix_pieces, *param_pieces, *held]
    if cfg["last"]:
        results = [((count + 8, channels), jnp.float32)]
    else:
        results = [
            ((count, channels), jnp.float32),
            ((count, channels), jnp.float32),
            ((planes * count + 16, channels), jnp.bfloat16),
        ]
    scratch = [pltpu.VMEM((cfg["features"], param_pieces[0].shape[2]), jnp.bfloat16)]
    scratch += [pltpu.VMEM(one.shape, jnp.float32) for one in sums]
    if len(kinds) > 8:
        scratch += [pltpu.VMEM((len(mine), *mine[0].shape), jnp.bfloat16)] * 2
    return on_chip(
        functools.partial(second_half_kernel, cfg, kinds, len(sums)),
        "second_half",
        operands,
        results,
        scratch=scratch,
    )


def finish_kernel(own_ref, other_ref, final_ref, loglik_ref):
    count = final_ref.shape[0] // 2
    side = side_of()
    for ref, place in ((own_ref, side), (other_ref, 1 - side)):
        final_ref[pl.ds(pl.multiple_of(place * count, 8), count), :] = ref[:count, :]
    first = jnp.where(side == 0, own_ref[count : count + 1, :], other_ref[count : count + 1, :])
    second = jnp.where(side == 0, other_ref[count : count + 1, :], own_ref[count : count + 1, :])
    loglik_ref[...] = jnp.concatenate([first[:, :count], second[:, :count]], axis=1)


def body(
    latents, in_proj, query_proj, key_proj, value_proj, mix_proj, param_proj, attn_gain, param_gain
):
    members, ways = lax.axis_size("seq"), lax.axis_size("head")
    rows, channels = latents.shape
    features = in_proj.shape[2]
    count = rows // 2
    planes = 4 if members % 4 == 0 else 1
    per_plane = members // planes
    bits = per_plane.bit_length() - 1

    def swap(array):
        return lax.ppermute(array, "head", [(i, i ^ 1) for i in range(ways)])

    def pieces_of(array):
        shares = [array]
        for j in range(1, ways):
            shares.append(
                lax.ppermute(array, "head", [((i + j) % ways, i) for i in range(ways)])
            )
        return shares

    def in_plane(mine):
        arrived = []
        for step in range(1, per_plane):
            pairs = []
            for i in range(members):
                for w in range(ways):
                    to = i ^ (turned(step, bits) if w % 2 else step)
                    pairs.append((i * ways + w, to * ways + w))
            arrived.append(lax.ppermute(mine, ("seq", "head"), pairs))
        return arrived

    def run(layer, mine, sibling, maps, made, latents, *rest):
        cfg = {
            "layer": layer,
            "last": layer == 1,
            "count": count,
            "features": features,
            "pieces": ways,
            "planes": planes,
            "per_plane": per_plane,
        }
        hidden, queries = made
        arrived = in_plane(mine)
        if per_plane == 4:
            one, two, three = (1, 2, 3)
            if layer == 1:
                sibling = swap(mine)
            others = {0: sibling}
            early = [(mine, 0, False)] + [(sibling, 0, True)]
            sums = attend(cfg, maps, queries, early)
            mines = {0: mine}
            mines[one], mines[two], both = stack(arrived[one - 1], arrived[two - 1], sums)
            others[one], others[two] = unstack(swap(both))
            batch = [(mines[one], one, False), (mines[two], two, False)]
            sums = attend(cfg, maps, queries, batch, sums)
            (mines[three],) = gate_all([arrived[three - 1]], sums)
            others[three] = swap(mines[three])
            batch = [(mines[three], three, False), (others[one], one, True)]
            sums = attend(cfg, maps, queries, batch, sums)
            kinds = [(two, True), (three, True)]
            mines, others = [[each[step] for step in range(4)] for each in (mines, others)]
        else:
            others = [swap(mine) if layer == 1 else sibling]
            sums = attend(cfg, maps, queries, [(mine, 0, False), (others[0], 0, True)])
            mines = [mine]
            if per_plane > 1:
                arrived = gate_all(arrived, sums)
                mines += arrived
                others += [swap(piece) for piece in arrived]
            kinds = [(step, False) for step in range(1, per_plane)]
            kinds += [(step, True) for step in range(1, per_plane)]
        return second_half(
            cfg, tuple(kinds), maps, queries, sums, hidden, param_gain, latents, mines, others, mix_pieces, param_pieces, *rest
        )

    (rounded,) = on_chip(
        round_kernel,
        "round",
        [],
        [(latents.shape, jnp.bfloat16)],
        far=[latents],
        scratch=[pltpu.VMEM(latents.shape, jnp.float32), pltpu.SemaphoreType.DMA((1,))],
    )
    parts = [rounded] + [
        lax.ppermute(rounded, "seq", [(i, i ^ (b * per_plane)) for i in range(members)])
        for b in range(1, planes)
    ]
    mix_pieces, param_pieces = pieces_of(mix_proj), pieces_of(param_proj)
    in_all, tail, own_maps = prepare(
        in_proj, attn_gain, key_proj, value_proj, query_proj, []
    )
    shape = (planes * count, channels)
    mine, sibling, own_maps = on_chip(
        functools.partial(arrange_kernel, planes),
        "arrange",
        [*parts, own_maps],
        [(shape, jnp.bfloat16), (shape, jnp.bfloat16), (own_maps.shape, jnp.bfloat16)],
        after=mix_pieces[1:] + param_pieces[1:],
    )
    first_maps, first_query, second_maps, second_query = join(tail, pieces_of(own_maps))
    width = 2 * key_proj.shape[2]
    made = make_queries(0, planes, count, mine, in_all, first_query, width)
    held, held_log, mine = run(0, mine, sibling, first_maps, made, latents)
    made = make_queries(1, 1, count, mine, in_all, second_query, width)
    (packed,) = run(1, mine, None, second_maps, made, latents, (held, held_log))
    final_latent, token_loglik = on_chip(
        finish_kernel,
        "finish",
        [packed, swap(packed)],
        [((rows, channels), jnp.float32), ((1, rows), jnp.float32)],
        out_memory=None,
    )
    return (final_latent, token_loglik.reshape(rows))


def solution(mesh):
    placed = (
        P("seq", None),
        P(),
        P(None, None, "head"),
        P(None, None, "head"),
        P(None, None, "head"),
        P(None, "head", None),
        P(None, "head", None),
        P(),
        P(),
    )
    return jax.shard_map(
        body, mesh=mesh, in_specs=placed, out_specs=(P("seq", None), P("seq")), check_vma=False
    )
```

```python
import functools
import math

import jax
import jax.numpy as jnp
from jax import lax
from jax.experimental import pallas as pl
from jax.experimental.pallas import tpu as pltpu
from jax.sharding import PartitionSpec as P

HS = 64

score_scale = 8.0
epsilon = 1e-06

VMEM_LIMIT = 32 * 1024 * 1024


def dot(a, b):
    return jnp.dot(a, b, preferred_element_type=jnp.float32)


def dot_nt(a, b):
    return lax.dot_general(a, b, (((1,), (1,)), ((), ())), preferred_element_type=jnp.float32)


def cat(parts, axis):
    return parts[0] if len(parts) == 1 else jnp.concatenate(parts, axis=axis)


def side_of():
    return lax.rem(lax.axis_index("head"), 2)


def on_chip(kernel, name, operands, results, far=(), after=(), scratch=(), out_memory=pltpu.VMEM):
    near = [pltpu.with_memory_space_constraint(array, pltpu.VMEM) for array in operands]
    far = [pltpu.with_memory_space_constraint(array, pltpu.HBM) for array in far]
    if out_memory is pltpu.VMEM:
        out_shape = tuple(pltpu.VMEM(shape, dtype) for shape, dtype in results)
    else:
        out_shape = tuple(jax.ShapeDtypeStruct(shape, dtype) for shape, dtype in results)
    return pl.pallas_call(
        kernel,
        in_specs=[pl.BlockSpec(memory_space=pltpu.VMEM)] * len(near)
        + [pl.BlockSpec(memory_space=pl.ANY)] * (len(far) + len(after)),
        out_specs=tuple(pl.BlockSpec(memory_space=pltpu.VMEM) for _ in results),
        out_shape=out_shape,
        scratch_shapes=list(scratch),
        compiler_params=pltpu.CompilerParams(vmem_limit_bytes=VMEM_LIMIT),
        name=name,
    )(*near, *far, *after)


def fetch(sources, targets, sems):
    copies = []
    for at, (source, target) in enumerate(zip(sources, targets)):
        copies.append(pltpu.make_async_copy(source, target, sems.at[at]))
        copies[-1].start()
    return copies


def round_kernel(rows_ref, out_ref, buffer, sems):
    for copy in fetch([rows_ref], [buffer], sems):
        copy.wait()
    out_ref[...] = buffer[...].astype(jnp.bfloat16)


def arrange_kernel(planes, *refs):
    place = lax.axis_index("seq") // (lax.axis_size("seq") // planes)
    mine_ref, other_ref, maps_ref = refs[-3:]
    maps_ref[...] = refs[planes][...]
    count = mine_ref.shape[0] // planes
    for step in range(planes):
        first, second = refs[step][:count, :], refs[step][count:, :]
        at = pl.ds(pl.multiple_of((place ^ step) * count, 16), count)
        mine_ref[at, :] = jnp.where(side_of() == 0, first, second)
        other_ref[at, :] = jnp.where(side_of() == 0, second, first)


def gates_kernel(many, *refs):
    for source, target in zip(refs[:many], refs[-many:]):
        target[...] = source[...]


def stack_kernel(one_ref, two_ref, *refs):
    rows = one_ref.shape[0]
    for source, target, at in ((one_ref, refs[-3], 0), (two_ref, refs[-2], rows)):
        target[...] = source[...]
        refs[-1][at : at + rows, :] = source[...]


def stack(one, two, made):
    rows, channels = one.shape
    shapes = [(rows, channels), (rows, channels), (2 * rows, channels)]
    results = [(shape, one.dtype) for shape in shapes]
    return on_chip(stack_kernel, "stack", [one, two, *made], results)


def unstack_kernel(both_ref, one_ref, two_ref):
    rows = one_ref.shape[0]
    one_ref[...] = both_ref[:rows, :]
    two_ref[...] = both_ref[rows:, :]


def unstack(both):
    shape = (both.shape[0] // 2, both.shape[1])
    return on_chip(unstack_kernel, "unstack", [both], [(shape, both.dtype)] * 2)


def gate_all(rows, made):
    results = [(piece.shape, piece.dtype) for piece in rows]
    return on_chip(functools.partial(gates_kernel, len(rows)), "gate", [*rows, *made], results)


def turned(step, bits):
    return sum(((step >> b) & 1) << (bits - 1 - b) for b in range(bits))


def chip_of(step, per_plane, other):
    bits = per_plane.bit_length() - 1
    first = side_of() == (1 if other else 0)
    return (lax.axis_index("seq") % per_plane) ^ jnp.where(first, step, turned(step, bits))


def prepare_kernel(in_src, gain_src, key_src, value_src, query_src, *refs):
    in_ref, tail_ref, maps_ref, gain_ref, buffer, sems = refs[-6:]
    layers, channels, _ = in_ref.shape
    weights = (key_src, value_src, query_src)
    sources = [in_src, gain_src] + [src.at[b] for b in range(layers) for src in weights]
    targets = [in_ref, gain_ref] + [buffer.at[b, at] for b in range(layers) for at in range(3)]
    copies = fetch(sources, targets, sems)
    for copy in copies[:2]:
        copy.wait()
    eye = lax.broadcasted_iota(jnp.int32, (channels, channels), 0) == lax.broadcasted_iota(
        jnp.int32, (channels, channels), 1
    )

    def store(ref, row, value):
        high = value.astype(jnp.bfloat16)
        rows = slice(row, row + value.shape[0])
        ref[rows, :channels] = high
        ref[rows, channels:] = (value - high.astype(jnp.float32)).astype(jnp.bfloat16)

    for layer in range(layers):
        base = in_ref[layer]
        store(tail_ref.at[layer], 0, dot_nt(base, base))
        store(tail_ref.at[layer], channels, jnp.where(eye, 1.0, 0.0))
        scaled = base.astype(jnp.float32) * gain_ref[layer : layer + 1, :]
        high = scaled.astype(jnp.bfloat16)
        low = (scaled - high.astype(jnp.float32)).astype(jnp.bfloat16)
        both = jnp.concatenate([high, low], axis=0)
        for at in range(3):
            copies[2 + 3 * layer + at].wait()
        product = dot(both, cat([buffer[layer, at] for at in range(3)], 1))
        store(maps_ref.at[layer], 0, (product[:channels] + product[channels:]).T)


def prepare(in_proj, attn_gain, key_proj, value_proj, query_proj, after):
    layers, channels, features = in_proj.shape
    columns = key_proj.shape[2]
    return on_chip(
        prepare_kernel,
        "prepare",
        [],
        [
            (in_proj.shape, jnp.bfloat16),
            ((layers, 2 * channels, 2 * channels), jnp.bfloat16),
            ((layers, 3 * columns, 2 * channels), jnp.bfloat16),
        ],
        far=[in_proj, attn_gain, key_proj, value_proj, query_proj],
        after=after,
        scratch=[
            pltpu.VMEM(attn_gain.shape, jnp.float32),
            pltpu.VMEM((layers, 3, features, columns), jnp.bfloat16),
            pltpu.SemaphoreType.DMA((2 + 3 * layers,)),
        ],
    )


def join_kernel(pieces, tail_ref, *refs):
    sources, outs = refs[:pieces], refs[pieces:]
    layers = tail_ref.shape[0]
    columns = sources[0].shape[1] // 3
    for layer in range(layers):
        maps_ref, query_ref = outs[2 * layer : 2 * layer + 2]
        total = pieces * columns
        for j, source in enumerate(sources):
            for at in range(2):
                row = at * total + j * columns
                maps_ref[row : row + columns, :] = source[layer, at * columns : (at + 1) * columns]
            query_ref[j * columns : (j + 1) * columns, :] = source[layer, 2 * columns :]
        maps_ref[2 * total :, :] = tail_ref[layer]


def join(tail, pieces):
    layers, rows, width = pieces[0].shape
    total = len(pieces) * rows // 3
    results = [((2 * total + tail.shape[1], width), jnp.bfloat16), ((total, width), jnp.bfloat16)]
    return on_chip(
        functools.partial(join_kernel, len(pieces)), "join", [tail, *pieces], results * layers
    )


def queries_kernel(layer, planes, rows_ref, in_ref, maps_ref, hidden_ref, out_ref):
    total = hidden_ref.shape[0]
    count = total // planes
    if layer == 0:
        rows = rows_ref[...]
    else:
        place = lax.axis_index("seq") // (lax.axis_size("seq") // (rows_ref.shape[0] // count))
        rows = rows_ref[pl.ds(pl.multiple_of(place * count, 16), count), :]
    hidden = dot(rows, in_ref[layer])
    hidden_ref[...] = hidden
    spread = lax.rsqrt(jnp.mean(hidden * hidden, axis=1, keepdims=True) + epsilon)
    twice = jnp.concatenate([rows, rows], axis=1)
    groups, _, width = out_ref.shape
    heads = width // HS
    head = lax.broadcasted_iota(jnp.int32, (1, width), 1) // HS
    same = head == lax.broadcasted_iota(jnp.int32, (width, 1), 0) // HS
    same = jnp.where(same, 1.0, 0.0).astype(jnp.bfloat16)
    for g in range(groups):
        query = dot_nt(twice, maps_ref[g * width : (g + 1) * width, :]) * spread
        square = query * query
        high = square.astype(jnp.bfloat16)
        low = (square - high.astype(jnp.float32)).astype(jnp.bfloat16)
        mean = (dot(high, same) + dot(low, same)) * (1.0 / HS)
        query = query * lax.rsqrt(mean + epsilon)
        for h in range(heads):
            band = jnp.where(head == h, query, 0.0).astype(jnp.bfloat16)
            for p in range(planes):
                row = (p * heads + h) * count
                out_ref[g, row : row + count, :] = band[p * count : (p + 1) * count]


def make_queries(layer, planes, count, rows, in_all, maps, width):
    return on_chip(
        functools.partial(queries_kernel, layer, planes),
        "queries",
        [rows, in_all, maps],
        [
            ((planes * count, in_all.shape[2]), jnp.float32),
            ((maps.shape[0] // width, planes * width // HS * count, width), jnp.bfloat16),
        ],
    )


def attend_some(cfg, maps_ref, query_ref, some, start, sums):
    count, features, planes, per_plane = cfg["count"], cfg["features"], cfg["planes"], cfg["per_plane"]
    layer, side = cfg["layer"], side_of()
    groups, _, group_cols = query_ref.shape
    heads = group_cols // HS
    band = heads * count
    total_cols = groups * group_cols
    stride = 2 * per_plane * count
    token = lax.broadcasted_iota(jnp.int32, (count, 1), 0)
    member = lax.axis_index("seq")
    query_place = (member % per_plane * 2 + side) * count + jnp.concatenate([token] * heads, axis=0)
    offsets = [
        (chip_of(step, per_plane, other) * 2 + (1 - side if other else side)) * count
        for _, step, other in some
    ]
    if layer == 0:
        size = len(some) * count
        lane = lax.broadcasted_iota(jnp.int32, (1, size), 1)
        key_place = lane + offsets[0]
        for at in range(1, len(some)):
            key_place = jnp.where(lane >= at * count, lane - at * count + offsets[at], key_place)
        allowed = key_place <= query_place
        parts = [
            cat([rows[p * count : (p + 1) * count] for rows, _, _ in some], 0)
            for p in range(planes)
        ]
        low_rows = [p * band for p in range(planes)]
    else:
        size = len(some) * planes * count
        lane = lax.broadcasted_iota(jnp.int32, (1, planes * count), 1)
        plane = ((lane.astype(jnp.float32) + 0.5) * (1.0 / count)).astype(jnp.int32)
        base_place = lane + plane * (stride - count)
        key_place = jnp.concatenate([base_place + offset for offset in offsets], axis=1)
        allowed = key_place >= query_place + member // per_plane * stride
        parts, low_rows = [cat([rows[: planes * count] for rows, _, _ in some], 0)], [0]

    def keys_and_values(source, g):
        low = g * group_cols
        twice = jnp.concatenate([source, source], axis=1)
        channels = source.shape[1]
        tail = dot_nt(maps_ref[2 * total_cols :, :], twice)
        square = jnp.sum(tail[:channels] * tail[channels:], axis=0, keepdims=True)
        scale = lax.rsqrt(jnp.maximum(square, 0.0) * (1.0 / features) + epsilon)
        scale_sq = scale * scale
        key = dot_nt(maps_ref[low : low + group_cols, :], twice)
        value = dot_nt(maps_ref[total_cols + low : total_cols + low + group_cols, :], twice)
        keys = []
        for h in range(heads):
            one = key[h * HS : (h + 1) * HS]
            mean = jnp.sum(one * one, axis=0, keepdims=True) * (1.0 / HS)
            factor = scale * lax.rsqrt(mean * scale_sq + epsilon) * (score_scale / HS)
            keys.append((one * factor).astype(jnp.bfloat16))
        return jnp.concatenate(keys, axis=0), (value * scale).astype(jnp.bfloat16)

    for g in range(groups):
        if size % 128 == 0 and len(parts) > 1:
            key, value = keys_and_values(cat(parts, 0), g)
            made = [
                (key[:, p * size : (p + 1) * size], value[:, p * size : (p + 1) * size])
                for p in range(len(parts))
            ]
        else:
            made = [keys_and_values(part, g) for part in parts]
        for index, ((key, value), low_row) in enumerate(zip(made, low_rows)):
            scores = dot(query_ref[g, low_row:, :], key)
            weights = jnp.exp(scores)
            first = jnp.where(allowed, weights[:band], 0.0)
            weights = first if weights.shape[0] == band else cat([first, weights[band:]], 0)
            product = dot_nt(weights.astype(jnp.bfloat16), value)
            lanes = [weights[:, at : at + 128] for at in range(0, weights.shape[1], 128)]
            news = [product, sum(part for part in lanes if part.shape[1] == 128)]
            news += [part for part in lanes if part.shape[1] < 128]
            for at, (old_ref, new_ref) in enumerate(sums):
                if start and index == 0:
                    old = None if old_ref is None else old_ref[g]
                else:
                    old = new_ref[g, low_row:, :]
                if at < len(news):
                    new = news[at] if old is None else old + news[at]
                else:
                    new = jnp.zeros(new_ref.shape[1:], jnp.float32) if old is None else old
                if at < len(news) or (start and index == 0):
                    new_ref[g, low_row:, :] = new


def sum_shapes(cfg, queries):
    groups, rows, cols = queries.shape
    shapes = [(groups, rows, cols), (groups, rows, 128)]
    rest = 2 * cfg["count"] % 128
    return shapes + ([(groups, rows, rest)] if cfg["layer"] == 0 and rest else [])


def attend_kernel(cfg, kinds, resume, maps_ref, query_ref, *refs):
    refs = list(refs)
    pieces = [(refs.pop(0), step, other) for step, other in kinds]
    many = len(refs) // 2 if resume else len(refs)
    olds = refs[:many] if resume else [None] * many
    sums = list(zip(olds, refs[-many:]))
    some = [(ref[...], step, other) for ref, step, other in pieces]
    attend_some(cfg, maps_ref, query_ref, some, True, sums)


def attend(cfg, maps, queries, pieces, sums=()):
    kinds = tuple((step, other) for _, step, other in pieces)
    return on_chip(
        functools.partial(attend_kernel, cfg, kinds, len(sums) > 0),
        "attend",
        [maps, queries, *[piece for piece, _, _ in pieces], *sums],
        [(shape, jnp.float32) for shape in sum_shapes(cfg, queries)],
    )


def chosen_rows(others, per_plane, chip, start):
    result = None
    for step, ref in enumerate(others):
        value = ref[pl.ds(start, 16), :].astype(jnp.float32)
        here = chip_of(step, per_plane, True) == chip
        result = value if result is None else jnp.where(here, value, result)
    return result


def second_half_kernel(cfg, kinds, many, maps_ref, query_ref, hidden_ref, gain_ref, latent_ref, *refs):
    layer, pieces, last, count = cfg["layer"], cfg["pieces"], cfg["last"], cfg["count"]
    planes, per_plane = cfg["planes"], cfg["per_plane"]
    refs = list(refs)
    olds = [refs.pop(0) for _ in range(many)]
    rows_of = {False: [refs.pop(0) for _ in range(per_plane)]}
    rows_of[True] = others = [refs.pop(0) for _ in range(per_plane)]
    mix_refs = [refs.pop(0) for _ in range(pieces)]
    param_refs = [refs.pop(0) for _ in range(pieces)]
    param_all = refs.pop(3)
    sums = list(zip(olds, [refs.pop(3) for _ in range(many)]))
    side, way, member = side_of(), lax.axis_index("head"), lax.axis_index("seq")
    members = planes * per_plane
    features, channels = hidden_ref.shape[1], latent_ref.shape[-1]
    groups, _, group_cols = query_ref.shape
    heads = group_cols // HS
    if len(kinds) <= 8:
        some = [(rows_of[other][step][...], step, other) for step, other in kinds]
        attend_some(cfg, maps_ref, query_ref, some, True, sums)
    else:
        for old, new in sums:
            new[...] = old[...]
        for buffer, other in zip(refs[-2:], (False, True)):
            for step in range(1, per_plane):
                buffer[step] = rows_of[other][step][...]

        def one_step(step, nothing):
            pair = [(refs[-2][step], step, False), (refs[-1][step], step, True)]
            attend_some(cfg, maps_ref, query_ref, pair, False, sums)
            return nothing

        lax.fori_loop(1, per_plane, one_step, 0)

    share = features // pieces
    for j, ref in enumerate(param_refs):
        at = pl.multiple_of(lax.rem(way + j, pieces) * share, 16)
        param_all[pl.ds(at, share), :] = ref[layer]
    mixture = hidden_ref[...]
    bands = mixture.shape[0] // count
    head = lax.broadcasted_iota(jnp.int32, (1, group_cols), 1) // HS
    for g in range(groups):
        total = sum(jnp.sum(new[g], axis=1, keepdims=True) for _, new in sums[1:])
        share_of = 1.0 / (total + (0.0 if last else 1.0))
        number_ref = sums[0][1]
        attended = []
        for p in range(bands):
            one = jnp.zeros((count, group_cols), jnp.float32)
            for h in range(heads):
                band = slice((p * heads + h) * count, (p * heads + h + 1) * count)
                one = jnp.where(head == h, number_ref[g, band, :] * share_of[band], one)
            attended.append(one)
        rows = cat([ref[layer] for ref in mix_refs[2 * g : 2 * g + 2]], 0)
        mixture = mixture + dot(cat(attended, 0).astype(jnp.bfloat16), rows)
    spread = lax.rsqrt(jnp.mean(mixture * mixture, axis=1, keepdims=True) + epsilon)
    scaled = (mixture * spread * gain_ref[layer : layer + 1, :]).astype(jnp.bfloat16)
    predicted = dot(scaled, param_all[...])
    shift_all = predicted[:, :channels]
    log_all = 2.0 * jnp.tanh(0.5 * predicted[:, channels:])
    token = lax.broadcasted_iota(jnp.int32, (count, 1), 0)
    if last:
        held_ref, held_log_ref, out_ref = refs[:3]
        before = member - 1 + side
        chip = (before + per_plane) % per_plane
        edge = chosen_rows(others, per_plane, chip, planes * count)
        edge = jnp.where(before >= 0, edge[0:2] + edge[2:4] + edge[4:6], 0.0)
        edge_log = edge[1:2]
        start = pl.multiple_of(side * count, 8)
        first = (latent_ref[pl.ds(start, 8), :][:1] - edge[0:1]) * jnp.exp(-edge_log)
        values = jnp.where(token == 0, first, pltpu.roll(held_ref[...], 1, 0))
        first_log = jnp.where(token == 0, edge_log, pltpu.roll(held_log_ref[...], 1, 0))
        result = (values - shift_all) * jnp.exp(-log_all)
        term = -(first_log + log_all) - 0.5 * (result * result)
        loglik = jnp.sum(term.T, axis=0, keepdims=True) * (1.0 / channels) - 0.5 * math.log(
            2.0 * math.pi
        )
        out_ref[:count, :] = result
        out_ref[count:, :count] = jnp.broadcast_to(loglik, (8, count))
        return
    held_ref, held_log_ref, narrow_ref = refs[:3]
    narrow_ref[planes * count :, :] = jnp.zeros((16, channels), jnp.bfloat16)
    own = latent_ref[pl.ds(pl.multiple_of(side * count, 8), count), :]
    for p in range(planes):
        shift_mu = shift_all[p * count : (p + 1) * count]
        log_scale = log_all[p * count : (p + 1) * count]
        following = p * per_plane + member % per_plane + side
        following_row = pl.multiple_of(jnp.minimum(following, members - 1) // per_plane * count, 16)
        after = chosen_rows(others, per_plane, following % per_plane, following_row)
        here = member // per_plane == p
        rows = rows_of[False][0][p * count : (p + 1) * count, :]
        values = jnp.where(here, own, rows.astype(jnp.float32))
        values = pltpu.roll(values, count - 1, 0)
        values = jnp.where(token == count - 1, after[:1], values)
        result = (values - shift_mu) * jnp.exp(-log_scale)
        if p == planes - 1:
            result = jnp.where((following == members) & (token == count - 1), 0.0, result)

        @pl.when(here)
        def keep(result=result, log_scale=log_scale):
            held_ref[...] = result
            held_log_ref[...] = log_scale

        narrow_ref[p * count : (p + 1) * count, :] = result.astype(jnp.bfloat16)

        @pl.when(member // per_plane - (member % per_plane + side) // per_plane == p)
        def send(shift_mu=shift_mu, log_scale=log_scale):
            edge = jnp.concatenate([shift_mu[count - 1 :], log_scale[count - 1 :]], axis=0)
            terms = []
            for _ in range(3):
                terms.append(edge.astype(jnp.bfloat16).astype(jnp.float32))
                edge = edge - terms[-1]
            rest = jnp.zeros((16 - 6, channels), jnp.float32)
            rows = jnp.concatenate(terms + [rest], axis=0)
            narrow_ref[planes * count :, :] = rows.astype(jnp.bfloat16)


def second_half(cfg, kinds, maps, queries, sums, hidden, param_gain, latents, mine, others, mix_pieces, param_pieces, held=()):
    count, planes, channels = cfg["count"], cfg["planes"], latents.shape[-1]
    operands = [maps, queries, hidden, param_gain, latents, *sums, *mine, *others]
    operands += [*mix_pieces, *param_pieces, *held]
    if cfg["last"]:
        results = [((count + 8, channels), jnp.float32)]
    else:
        results = [
            ((count, channels), jnp.float32),
            ((count, channels), jnp.float32),
            ((planes * count + 16, channels), jnp.bfloat16),
        ]
    scratch = [pltpu.VMEM((cfg["features"], param_pieces[0].shape[2]), jnp.bfloat16)]
    scratch += [pltpu.VMEM(one.shape, jnp.float32) for one in sums]
    if len(kinds) > 8:
        scratch += [pltpu.VMEM((len(mine), *mine[0].shape), jnp.bfloat16)] * 2
    return on_chip(
        functools.partial(second_half_kernel, cfg, kinds, len(sums)),
        "second_half",
        operands,
        results,
        scratch=scratch,
    )


def finish_kernel(own_ref, other_ref, final_ref, loglik_ref):
    count = final_ref.shape[0] // 2
    side = side_of()
    for ref, place in ((own_ref, side), (other_ref, 1 - side)):
        final_ref[pl.ds(pl.multiple_of(place * count, 8), count), :] = ref[:count, :]
    first = jnp.where(side == 0, own_ref[count : count + 1, :], other_ref[count : count + 1, :])
    second = jnp.where(side == 0, other_ref[count : count + 1, :], own_ref[count : count + 1, :])
    loglik_ref[...] = jnp.concatenate([first[:, :count], second[:, :count]], axis=1)


def body(
    latents, in_proj, query_proj, key_proj, value_proj, mix_proj, param_proj, attn_gain, param_gain
):
    members, ways = lax.axis_size("seq"), lax.axis_size("head")
    rows, channels = latents.shape
    features = in_proj.shape[2]
    count = rows // 2
    planes = 4 if members % 4 == 0 else 1
    per_plane = members // planes
    bits = per_plane.bit_length() - 1

    def swap(array):
        return lax.ppermute(array, "head", [(i, i ^ 1) for i in range(ways)])

    def pieces_of(array):
        shares = [array]
        for j in range(1, ways):
            shares.append(
                lax.ppermute(array, "head", [((i + j) % ways, i) for i in range(ways)])
            )
        return shares

    def in_plane(mine):
        arrived = []
        for step in range(1, per_plane):
            pairs = []
            for i in range(members):
                for w in range(ways):
                    to = i ^ (turned(step, bits) if w % 2 else step)
                    pairs.append((i * ways + w, to * ways + w))
            arrived.append(lax.ppermute(mine, ("seq", "head"), pairs))
        return arrived

    def run(layer, mine, sibling, maps, made, latents, *rest):
        cfg = {
            "layer": layer,
            "last": layer == 1,
            "count": count,
            "features": features,
            "pieces": ways,
            "planes": planes,
            "per_plane": per_plane,
        }
        hidden, queries = made
        arrived = in_plane(mine)
        if per_plane == 4:
            one, two, three = (1, 2, 3)
            if layer == 1:
                sibling = swap(mine)
            others = {0: sibling}
            early = [(mine, 0, False)] + [(sibling, 0, True)]
            sums = attend(cfg, maps, queries, early)
            mines = {0: mine}
            mines[one], mines[two], both = stack(arrived[one - 1], arrived[two - 1], sums)
            others[one], others[two] = unstack(swap(both))
            batch = [(mines[one], one, False), (mines[two], two, False)]
            sums = attend(cfg, maps, queries, batch, sums)
            (mines[three],) = gate_all([arrived[three - 1]], sums)
            others[three] = swap(mines[three])
            batch = [(mines[three], three, False), (others[one], one, True)]
            sums = attend(cfg, maps, queries, batch, sums)
            kinds = [(two, True), (three, True)]
            mines, others = [[each[step] for step in range(4)] for each in (mines, others)]
        else:
            others = [swap(mine) if layer == 1 else sibling]
            sums = attend(cfg, maps, queries, [(mine, 0, False), (others[0], 0, True)])
            mines = [mine]
            if per_plane > 1:
                arrived = gate_all(arrived, sums)
                mines += arrived
                others += [swap(piece) for piece in arrived]
            kinds = [(step, False) for step in range(1, per_plane)]
            kinds += [(step, True) for step in range(1, per_plane)]
        return second_half(
            cfg, tuple(kinds), maps, queries, sums, hidden, param_gain, latents, mines, others, mix_pieces, param_pieces, *rest
        )

    (rounded,) = on_chip(
        round_kernel,
        "round",
        [],
        [(latents.shape, jnp.bfloat16)],
        far=[latents],
        scratch=[pltpu.VMEM(latents.shape, jnp.float32), pltpu.SemaphoreType.DMA((1,))],
    )
    parts = [rounded] + [
        lax.ppermute(rounded, "seq", [(i, i ^ (b * per_plane)) for i in range(members)])
        for b in range(1, planes)
    ]
    mix_pieces, param_pieces = pieces_of(mix_proj), pieces_of(param_proj)
    in_all, tail, own_maps = prepare(
        in_proj, attn_gain, key_proj, value_proj, query_proj, []
    )
    shape = (planes * count, channels)
    mine, sibling, own_maps = on_chip(
        functools.partial(arrange_kernel, planes),
        "arrange",
        [*parts, own_maps],
        [(shape, jnp.bfloat16), (shape, jnp.bfloat16), (own_maps.shape, jnp.bfloat16)],
        after=mix_pieces[1:] + param_pieces[1:],
    )
    first_maps, first_query, second_maps, second_query = join(tail, pieces_of(own_maps))
    width = 2 * key_proj.shape[2]
    made = make_queries(0, planes, count, mine, in_all, first_query, width)
    held, held_log, mine = run(0, mine, sibling, first_maps, made, latents)
    made = make_queries(1, 1, count, mine, in_all, second_query, width)
    (packed,) = run(1, mine, None, second_maps, made, latents, (held, held_log))
    final_latent, token_loglik = on_chip(
        finish_kernel,
        "finish",
        [packed, swap(packed)],
        [((rows, channels), jnp.float32), ((1, rows), jnp.float32)],
        out_memory=None,
    )
    return (final_latent, token_loglik.reshape(rows))


def solution(mesh):
    placed = (
        P("seq", None),
        P(),
        P(None, None, "head"),
        P(None, None, "head"),
        P(None, None, "head"),
        P(None, "head", None),
        P(None, "head", None),
        P(),
        P(),
    )
    return jax.shard_map(
        body, mesh=mesh, in_specs=placed, out_specs=(P("seq", None), P("seq")), check_vma=False
    )
```
